32 devices in a mesh: dp: 4 (over y, core), fsdp: 8 (over z, x).
Axes of the slice: x: 2, y: 2, z: 4, core: 2. Of those that a mesh axis runs over, the one named last changes fastest.
Arguments:
- tokens: bfloat16 [12608, 768], P(('dp', 'fsdp')), may hold values from -6 to 6
- masked_rows: int32 [64, 196], P(('dp', 'fsdp')), may hold values from -1 to 196, as said below
- cotangent: bfloat16 [12608, 768], P(('dp', 'fsdp')), may hold values from -6 to 6
- norm1_gain: bfloat16 [2, 768], P(None, ('dp', 'fsdp')), may hold values from 0.099609375 to 1.8984375
- norm1_bias: bfloat16 [2, 768], P(None, ('dp', 'fsdp')), may hold values from -3 to 3
- qkv_weight: bfloat16 [2, 768, 2304], P(None, ('dp', 'fsdp')), may hold values from -0.21875 to 0.21875
- q_bias: bfloat16 [2, 768], P(None, ('dp', 'fsdp')), may hold values from -3 to 3
- v_bias: bfloat16 [2, 768], P(None, ('dp', 'fsdp')), may hold values from -3 to 3
- proj_weight: bfloat16 [2, 768, 768], P(None, ('dp', 'fsdp')), may hold values from -0.625 to 0.625
- proj_bias: bfloat16 [2, 768], P(None, ('dp', 'fsdp')), may hold values from -2 to 2
- gamma_attn: bfloat16 [2, 768], P(None, ('dp', 'fsdp')), may hold values from 0.5 to 1.5
- norm2_gain: bfloat16 [2, 768], P(None, ('dp', 'fsdp')), may hold values from 0.099609375 to 1.8984375
- norm2_bias: bfloat16 [2, 768], P(None, ('dp', 'fsdp')), may hold values from -3 to 3
- fc1_weight: bfloat16 [2, 768, 3072], P(None, ('dp', 'fsdp')), may hold values from -0.21875 to 0.21875
- fc1_bias: bfloat16 [2, 3072], P(None, ('dp', 'fsdp')), may hold values from -3 to 3
- fc2_weight: bfloat16 [2, 3072, 768], P(None, ('dp', 'fsdp')), may hold values from -0.109375 to 0.109375
- fc2_bias: bfloat16 [2, 768], P(None, ('dp', 'fsdp')), may hold values from -2 to 2
- gamma_mlp: bfloat16 [2, 768], P(None, ('dp', 'fsdp')), may hold values from 0.5 to 1.5
- rel_table: bfloat16 [2, 12, 736], P(None, None, ('dp', 'fsdp')), may hold values from -5 to 5
Outputs:
- encoded: bfloat16 [12608, 768], P(('dp', 'fsdp'))
- tokens_grad: float32 [12608, 768], P(('dp', 'fsdp'))
- grad_norm1_gain: float32 [2, 768], P(None, ('dp', 'fsdp'))
- grad_norm1_bias: float32 [2, 768], P(None, ('dp', 'fsdp'))
- grad_qkv_weight: float32 [2, 768, 2304], P(None, ('dp', 'fsdp'))
- grad_q_bias: float32 [2, 768], P(None, ('dp', 'fsdp'))
- grad_v_bias: float32 [2, 768], P(None, ('dp', 'fsdp'))
- grad_proj_weight: float32 [2, 768, 768], P(None, ('dp', 'fsdp'))
- grad_proj_bias: float32 [2, 768], P(None, ('dp', 'fsdp'))
- grad_gamma_attn: float32 [2, 768], P(None, ('dp', 'fsdp'))
- grad_norm2_gain: float32 [2, 768], P(None, ('dp', 'fsdp'))
- grad_norm2_bias: float32 [2, 768], P(None, ('dp', 'fsdp'))
- grad_fc1_weight: float32 [2, 768, 3072], P(None, ('dp', 'fsdp'))
- grad_fc1_bias: float32 [2, 3072], P(None, ('dp', 'fsdp'))
- grad_fc2_weight: float32 [2, 3072, 768], P(None, ('dp', 'fsdp'))
- grad_fc2_bias: float32 [2, 768], P(None, ('dp', 'fsdp'))
- grad_gamma_mlp: float32 [2, 768], P(None, ('dp', 'fsdp'))
- grad_rel_table: float32 [2, 12, 736], P(None, None, ('dp', 'fsdp'))
The draws below stay inside these ranges and needn't reach their ends.
Inputs may be any that keep to these rules, and one draw needn't show every extreme that they name: `masked_rows`: each image lists its masked patches first, distinct, then -1 to the end; some image has all 196 patches masked, and row 0 is never listed.
All inputs are finite; a program needn't handle non-finite values.
Results may differ from the reference program's by a relative error of at most 0.015.
Values may be sent and summed in bfloat16 or wider, within the bound.
No kernel may reach another device: no remote copies, remote signals or barrier semaphores. Data moves between devices by JAX's collectives and lax.ppermute only.
A program may use at most 256 MiB of HBM per device.

```python
import jax
import jax.numpy as jnp
import numpy as np
from jax import lax

D = 768
HEADS = 12
FF = 3072
GRID = 14
LAYERS = 2
IMG_DEV = 2
PATCHES = 196
ROWS_IMG = 197
TAB_PAD = 736
IMAGES = 64
ROWS = 12608
DEVICES = 32


def draw_masked_rows(key, part):
    key = jax.random.fold_in(key, 7)
    key_level, key_full, key_perm = jax.random.split(key, 3)
    levels = jax.random.randint(key_level, (IMAGES,), 0, 6)
    counts = jnp.minimum(PATCHES, jnp.left_shift(jnp.ones_like(levels), levels))
    chosen = jax.random.randint(key_full, (), 0, IMAGES)
    counts = jnp.where(jnp.arange(IMAGES) == chosen, PATCHES, counts)
    keys = jax.random.split(key_perm, IMAGES)
    orders = jax.vmap(lambda single: jax.random.permutation(single, PATCHES))(keys) + 1
    slots = jnp.arange(PATCHES)
    return jnp.where(slots[None, :] < counts[:, None], orders, -1).astype(jnp.int32)


def level_of(own_key, extent, cuts, low, high):
    def one(axis_at, blocks):
        draws = jax.random.uniform(jax.random.fold_in(jax.random.fold_in(own_key, 6), axis_at), (blocks,), jnp.float32, low / len(cuts), high / len(cuts))
        return jnp.repeat(jnp.exp(draws), extent[axis_at] // blocks).reshape((-1,) + (1,) * (len(extent) - axis_at - 1))

    factor_of = one(*cuts[0])
    for cut in cuts[1:]:
        factor_of = factor_of * one(*cut)
    return factor_of


def bell_draw(stream_key, shape, scale, reach, shards=(), held_as=jnp.bfloat16):
    array = scale * jax.random.normal(stream_key, shape, jnp.float32)
    if shards:
        array = array * level_of(stream_key, shape, shards, -0.22, 0.18)
    return jnp.clip(array, -reach, reach).astype(held_as)


def setup_inputs(seed: int = 0) -> dict:
    key_list = jax.random.split(jax.random.key(seed), 20)
    tokens = bell_draw(key_list[0], (ROWS, D), 1.0, 6.0, ((0, 32),))
    masked_rows = draw_masked_rows(jax.random.fold_in(key_list[19], 71), 0)
    cotangent = bell_draw(key_list[2], (ROWS, D), 1.0, 6.0, ((0, 32),))
    norm1_gain = jnp.clip(1.0 + 0.18 * jax.random.normal(key_list[3], (LAYERS, D), jnp.float32), 0.099609375, 1.8984375).astype(jnp.bfloat16)
    norm1_bias = bell_draw(key_list[4], (LAYERS, D), 0.5, 3.0, ((1, 32),))
    qkv_weight = bell_draw(key_list[5], (LAYERS, D, 3 * D), D ** -0.5, 0.21875, ((1, 32),))
    q_bias = bell_draw(key_list[6], (LAYERS, D), 0.5, 3.0, ((1, 32),))
    v_bias = bell_draw(key_list[7], (LAYERS, D), 0.5, 3.0, ((1, 32),))
    proj_weight = bell_draw(key_list[8], (LAYERS, D, D), (D // 8) ** -0.5, 0.625, ((1, 32),))
    proj_bias = bell_draw(key_list[9], (LAYERS, D), 0.3, 2.0, ((1, 32),))
    gamma_attn = jnp.clip(0.5 + 1.0 * jax.random.uniform(key_list[10], (LAYERS, D), jnp.float32) ** level_of(key_list[10], (LAYERS, D), ((1, 32),), -0.2, 0.2), 0.5, 1.5).astype(jnp.bfloat16)
    norm2_gain = jnp.clip(1.0 + 0.18 * jax.random.normal(key_list[11], (LAYERS, D), jnp.float32), 0.099609375, 1.8984375).astype(jnp.bfloat16)
    norm2_bias = bell_draw(key_list[12], (LAYERS, D), 0.5, 3.0, ((1, 32),))
    fc1_weight = bell_draw(key_list[13], (LAYERS, D, FF), D ** -0.5, 0.21875, ((1, 32),))
    fc1_bias = bell_draw(key_list[14], (LAYERS, FF), 0.5, 3.0, ((1, 32),))
    fc2_weight = bell_draw(key_list[15], (LAYERS, FF, D), FF ** -0.5, 0.109375, ((1, 32),))
    fc2_bias = bell_draw(key_list[16], (LAYERS, D), 0.3, 2.0, ((1, 32),))
    gamma_mlp = jnp.clip(0.5 + 1.0 * jax.random.uniform(key_list[17], (LAYERS, D), jnp.float32) ** level_of(key_list[17], (LAYERS, D), ((1, 32),), -0.2, 0.2), 0.5, 1.5).astype(jnp.bfloat16)
    rel_table = bell_draw(key_list[18], (LAYERS, HEADS, TAB_PAD), 1.0, 5.0, ((2, 32),))
    return {"tokens": tokens, "masked_rows": masked_rows, "cotangent": cotangent, "norm1_gain": norm1_gain, "norm1_bias": norm1_bias, "qkv_weight": qkv_weight, "q_bias": q_bias, "v_bias": v_bias, "proj_weight": proj_weight, "proj_bias": proj_bias, "gamma_attn": gamma_attn, "norm2_gain": norm2_gain, "norm2_bias": norm2_bias, "fc1_weight": fc1_weight, "fc1_bias": fc1_bias, "fc2_weight": fc2_weight, "fc2_bias": fc2_bias, "gamma_mlp": gamma_mlp, "rel_table": rel_table}


@jax.custom_vjp
def low(v):
    return lax.optimization_barrier(v.astype(jnp.bfloat16)).astype(jnp.float32)

@jax.custom_vjp
def low_back(v):
    return v

def low_keep(v):
    return (low(v), None)

def low_pass(kept, grad):
    return (grad,)

def back_keep(v):
    return (v, None)

def back_low(kept, grad):
    return (low(grad),)
low.defvjp(low_keep, low_pass)
low_back.defvjp(back_keep, back_low)
HIGH = lax.Precision.HIGHEST

def rel_index(grid):
    rows = np.arange(grid)
    coords = np.stack(np.meshgrid(rows, rows, indexing='ij')).reshape(2, -1)
    offsets = coords[:, :, None] - coords[:, None, :] + grid - 1
    count = (2 * grid - 1) * (2 * grid - 1) + 3
    table_idx = np.zeros((grid * grid + 1, grid * grid + 1), np.int32)
    table_idx[1:, 1:] = offsets[0] * (2 * grid - 1) + offsets[1]
    table_idx[0, :] = count - 3
    table_idx[:, 0] = count - 2
    table_idx[0, 0] = count - 1
    return table_idx

def layer_norm(values, gain, shift):
    centered = values - lax.optimization_barrier(jnp.mean(values, -1, keepdims=True))
    variance = lax.optimization_barrier(jnp.mean(centered * centered, -1, keepdims=True))
    return centered * lax.rsqrt(variance + 1e-06) * gain + shift

def block(inputs, params, index):
    n1g, n1b, w_qkv, qb, vb, w_proj, b_proj, g_attn, n2g, n2b, w_one, b_one, w_two, b_two, g_mlp, table = params
    batch, length, width = inputs.shape
    heads = table.shape[0]
    size = width // heads
    hidden = low(layer_norm(inputs, n1g, n1b))
    qkv = jnp.einsum('bnd,de->bne', hidden, w_qkv, precision=HIGH) + jnp.concatenate([qb, jnp.zeros_like(qb), vb])
    qkv = low(low_back(qkv)).reshape(batch, length, 3, heads, size)
    query, keys, values = (qkv[:, :, 0], qkv[:, :, 1], qkv[:, :, 2])
    bias = table[:, index]
    scores = jnp.einsum('bqhe,bkhe->bhqk', query, keys, precision=HIGH) * size ** (-0.5) + bias[None]
    scores = low_back(scores)
    probs = low(jax.nn.softmax(scores, -1))
    attended = jnp.einsum('bhqk,bkhe->bqhe', probs, values, precision=HIGH).reshape(batch, length, width)
    attended = low(low_back(attended))
    branch = low_back(jnp.einsum('bnd,de->bne', attended, w_proj, precision=HIGH) + b_proj)
    middle = inputs + g_attn * branch
    hidden_two = low(layer_norm(middle, n2g, n2b))
    pre = low_back(jnp.einsum('bnd,df->bnf', hidden_two, w_one, precision=HIGH) + b_one)
    active = low(jax.nn.gelu(pre, approximate=False))
    mlp_out = low_back(jnp.einsum('bnf,fd->bnd', active, w_two, precision=HIGH) + b_two)
    return middle + g_mlp * mlp_out

def reference(tokens, masked_rows, cotangent, norm1_gain, norm1_bias, qkv_weight, q_bias, v_bias, proj_weight, proj_bias, gamma_attn, norm2_gain, norm2_bias, fc1_weight, fc1_bias, fc2_weight, fc2_bias, gamma_mlp, rel_table):
    weights = (norm1_gain, norm1_bias, qkv_weight, q_bias, v_bias, proj_weight, proj_bias, gamma_attn, norm2_gain, norm2_bias, fc1_weight, fc1_bias, fc2_weight, fc2_bias, gamma_mlp, rel_table)
    params = tuple((w.astype(jnp.float32) for w in weights))
    index = jnp.asarray(rel_index(GRID))
    groups = DEVICES // 8
    inputs = tokens.astype(jnp.float32).reshape(groups, IMG_DEV * 8, ROWS_IMG, D)
    positions = jnp.arange(ROWS_IMG, dtype=jnp.int32)
    mask = jnp.any(masked_rows[:, :, None] == positions[None, None, :], axis=1).astype(jnp.float32)
    seed_grad = (cotangent.astype(jnp.float32).reshape(IMAGES, ROWS_IMG, D) * mask[:, :, None]).reshape(groups, IMG_DEV * 8, ROWS_IMG, D)

    def forward(values, prm):

        def stack_layers(group):
            for layer_idx in range(LAYERS):
                group = block(group, tuple((p[layer_idx] for p in prm)), index)
            return group
        return lax.map(jax.checkpoint(stack_layers), values)
    result, pullback = jax.vjp(forward, inputs, params)
    grad_in, grads = pullback(seed_grad)
    return (result.reshape(ROWS, D).astype(jnp.bfloat16), grad_in.reshape(ROWS, D), grads[0], grads[1], grads[2], grads[3], grads[4], grads[5], grads[6], grads[7], grads[8], grads[9], grads[10], grads[11], grads[12], grads[13], grads[14], grads[15])
```

```python
import functools
import math

import jax
import jax.numpy as jnp
import numpy as np
from jax import lax
from jax.experimental import pallas as pl
from jax.experimental.pallas import tpu as pltpu
from jax.sharding import PartitionSpec as P

GRID = 14
SPAN = 2 * GRID - 1
LAYERS = 2
IMG_ROWS = GRID * GRID + 1
PAD_ROWS = 208
LANES = 256
E_LANES = 512
HEAD = 64
PAIR = 2 * HEAD
NEG = -1e30
SMALL = 128
F32 = jnp.float32
B16 = jnp.bfloat16
AXES = ("dp", "fsdp")
VMEM = pltpu.CompilerParams(vmem_limit_bytes=56 * 1024 * 1024)


def dot(a, b, dims):
    return lax.dot_general(a, b, (dims, ((), ())), preferred_element_type=F32)


NN = ((1,), (0,))
NT = ((1,), (1,))
TN = ((0,), (0,))


def shift_onehot():
    v, d, b = np.meshgrid(np.arange(SPAN), np.arange(GRID), np.arange(GRID), indexing="ij")
    return (v == b - d + GRID - 1).astype(np.float32)


def bias_kernel(cls_ref, e_ref, out_ref, tmp_ref):
    head = pl.program_id(0)
    tmp_ref[...] = jnp.zeros_like(tmp_ref)
    for c in range(GRID):
        start = (GRID - 1 - c) * GRID
        tmp_ref[1 + c * GRID : 1 + (c + 1) * GRID, 0:IMG_ROWS] = e_ref[
            0, 0:GRID, start : start + IMG_ROWS
        ]
    row = lax.broadcasted_iota(jnp.int32, (PAD_ROWS, LANES), 0)
    lane = lax.broadcasted_iota(jnp.int32, (PAD_ROWS, LANES), 1)
    to_patch = cls_ref[head, 0]
    from_patch = cls_ref[head, 1]
    to_self = cls_ref[head, 2]
    val = jnp.where(lane == 0, to_patch, tmp_ref[...])
    first = jnp.where(lane == 0, to_self, from_patch)
    val = jnp.where(row == 0, first, val)
    out_ref[0] = jnp.where(row >= IMG_ROWS, NEG, val)


def build_bias(table):
    heads = table.shape[0]
    grid_part = table[:, : SPAN * SPAN].reshape(heads, SPAN, SPAN).astype(B16)
    onehot = jnp.asarray(shift_onehot(), B16)
    e = jnp.einsum("huv,vdb->hdub", grid_part, onehot, preferred_element_type=F32)
    e = e.reshape(heads, GRID, SPAN * GRID)
    e = jnp.pad(e, ((0, 0), (0, 16 - GRID), (1, E_LANES - 1 - SPAN * GRID)))
    cls = table[:, SPAN * SPAN : SPAN * SPAN + 3]
    return pl.pallas_call(
        bias_kernel,
        grid=(heads,),
        out_shape=jax.ShapeDtypeStruct((heads, PAD_ROWS, LANES), F32),
        in_specs=[
            pl.BlockSpec(memory_space=pltpu.SMEM),
            pl.BlockSpec((1, 16, E_LANES), lambda h: (h, 0, 0)),
        ],
        out_specs=pl.BlockSpec((1, PAD_ROWS, LANES), lambda h: (h, 0, 0)),
        scratch_shapes=[pltpu.VMEM((PAD_ROWS, LANES), F32)],
        compiler_params=VMEM,
        name="bias_expand",
    )(cls, e)


def bias_grad_kernel(g_ref, e_ref, cls_ref):
    lane = lax.broadcasted_iota(jnp.int32, (PAD_ROWS, LANES), 1)
    row = lax.broadcasted_iota(jnp.int32, (PAD_ROWS, LANES), 0)
    g = g_ref[0]
    g = jnp.where((lane < IMG_ROWS) & (row < IMG_ROWS), g, 0.0)
    e_ref[...] = jnp.zeros_like(e_ref)
    for c in range(GRID):
        start = (GRID - 1 - c) * GRID
        rows = g_ref[0, 1 + c * GRID : 1 + (c + 1) * GRID, 1:IMG_ROWS]
        e_ref[0, 0:GRID, start + 1 : start + IMG_ROWS] += rows
    to_patch = jnp.sum(jnp.where((lane == 0) & (row > 0), g, 0.0))
    from_patch = jnp.sum(jnp.where((lane > 0) & (row == 0), g, 0.0))
    to_self = jnp.sum(jnp.where((lane == 0) & (row == 0), g, 0.0))
    spot = lax.broadcasted_iota(jnp.int32, (8, 128), 1)
    cls_ref[0] = jnp.where(
        spot == 0, to_patch, jnp.where(spot == 1, from_patch, jnp.where(spot == 2, to_self, 0.0))
    )


def reduce_bias(grad, entries):
    heads = grad.shape[0]
    e, cls = pl.pallas_call(
        bias_grad_kernel,
        grid=(heads,),
        out_shape=(
            jax.ShapeDtypeStruct((heads, 16, E_LANES), F32),
            jax.ShapeDtypeStruct((heads, 8, 128), F32),
        ),
        in_specs=[pl.BlockSpec((1, PAD_ROWS, LANES), lambda h: (h, 0, 0))],
        out_specs=(
            pl.BlockSpec((1, 16, E_LANES), lambda h: (h, 0, 0)),
            pl.BlockSpec((1, 8, 128), lambda h: (h, 0, 0)),
        ),
        compiler_params=VMEM,
        name="bias_reduce",
    )(grad)
    e = e[:, :GRID, 1 : 1 + SPAN * GRID].reshape(heads, GRID, SPAN, GRID)
    onehot = jnp.asarray(shift_onehot(), F32)
    grid_part = jnp.einsum("hdub,vdb->huv", e, onehot, precision=lax.Precision.HIGHEST)
    flat = jnp.concatenate([grid_part.reshape(heads, SPAN * SPAN), cls[:, 0, :3]], axis=1)
    return jnp.pad(flat, ((0, 0), (0, entries - flat.shape[1])))


def head_mask(which):
    lane = lax.broadcasted_iota(jnp.int32, (PAD_ROWS, PAIR), 1)
    return (lane < HEAD) if which == 0 else (lane >= HEAD)


def attention_kernel(width, qkv_ref, bias_ref, out_ref, lse_ref):
    heads = width // HEAD
    for pair in range(heads // 2):
        at = pair * PAIR
        q = qkv_ref[0, :, at : at + PAIR]
        k = qkv_ref[0, :, width + at : width + at + PAIR]
        v = qkv_ref[0, :, 2 * width + at : 2 * width + at + PAIR]
        q = q * jnp.asarray(HEAD ** (-0.5), B16)
        v_t = v.T
        parts = []
        for t in range(2):
            head = 2 * pair + t
            q_t = jnp.where(head_mask(t), q, jnp.zeros_like(q))
            scores = dot(k, q_t, NT) + bias_ref[head, :, 0:PAD_ROWS]
            top = jnp.max(scores, axis=0, keepdims=True)
            weights = jnp.exp(scores - top)
            total = jnp.sum(weights, axis=0, keepdims=True)
            probs = (weights * (1.0 / total)).astype(B16)
            lse_ref[0, head : head + 1, 0:PAD_ROWS] = top + jnp.log(total)
            parts.append(dot(v_t[t * HEAD : (t + 1) * HEAD], probs, NN))
        out_ref[0, :, at : at + PAIR] = jnp.concatenate(parts, axis=0).T.astype(B16)


def attention_forward(qkv, bias):
    images = qkv.shape[0]
    width = qkv.shape[2] // 3
    heads = width // HEAD
    return pl.pallas_call(
        functools.partial(attention_kernel, width),
        grid=(images,),
        out_shape=(
            jax.ShapeDtypeStruct((images, PAD_ROWS, width), B16),
            jax.ShapeDtypeStruct((images, 16, LANES), F32),
        ),
        in_specs=[
            pl.BlockSpec((1, PAD_ROWS, 3 * width), lambda i: (i, 0, 0)),
            pl.BlockSpec((heads, PAD_ROWS, LANES), lambda i: (0, 0, 0)),
        ],
        out_specs=(
            pl.BlockSpec((1, PAD_ROWS, width), lambda i: (i, 0, 0)),
            pl.BlockSpec((1, 16, LANES), lambda i: (i, 0, 0)),
        ),
        compiler_params=VMEM,
        name="attention",
    )(qkv, bias)


def attention_grad_kernel(width, qkv_ref, bias_ref, lse_ref, g_ref, out_ref, dbias_ref):
    heads = width // HEAD
    scale = HEAD ** (-0.5)

    @pl.when(pl.program_id(0) == 0)
    def _():
        dbias_ref[...] = jnp.zeros_like(dbias_ref)

    for pair in range(heads // 2):
        at = pair * PAIR
        q = qkv_ref[0, :, at : at + PAIR]
        k = qkv_ref[0, :, width + at : width + at + PAIR]
        v = qkv_ref[0, :, 2 * width + at : 2 * width + at + PAIR]
        g = g_ref[0, :, at : at + PAIR]
        q = q * jnp.asarray(scale, B16)
        k_t = k.T
        dq_parts = []
        dk = None
        dv = None
        for t in range(2):
            head = 2 * pair + t
            q_t = jnp.where(head_mask(t), q, jnp.zeros_like(q))
            g_t = jnp.where(head_mask(t), g, jnp.zeros_like(g))
            scores = dot(k, q_t, NT) + bias_ref[head, :, 0:PAD_ROWS]
            probs = jnp.exp(scores - lse_ref[0, head : head + 1, 0:PAD_ROWS])
            dprobs = dot(v, g_t, NT)
            dv_t = dot(probs.astype(B16), g_t, NN)
            mean = jnp.sum(probs * dprobs, axis=0, keepdims=True)
            dscores = (probs * (dprobs - mean)).astype(B16)
            dbias_ref[head, :, 0:PAD_ROWS] += dscores.astype(F32)
            dk_t = dot(dscores, q_t, NN)
            dq_parts.append(dot(k_t[t * HEAD : (t + 1) * HEAD], dscores, NN))
            dk = dk_t if dk is None else dk + dk_t
            dv = dv_t if dv is None else dv + dv_t
        dq = jnp.concatenate(dq_parts, axis=0).T * scale
        out_ref[0, :, at : at + PAIR] = dq.astype(B16)
        out_ref[0, :, width + at : width + at + PAIR] = dk.astype(B16)
        out_ref[0, :, 2 * width + at : 2 * width + at + PAIR] = dv.astype(B16)


def attention_backward(qkv, bias, lse, grad):
    images = qkv.shape[0]
    width = qkv.shape[2] // 3
    heads = width // HEAD
    return pl.pallas_call(
        functools.partial(attention_grad_kernel, width),
        grid=(images,),
        out_shape=(
            jax.ShapeDtypeStruct((images, PAD_ROWS, 3 * width), B16),
            jax.ShapeDtypeStruct((heads, PAD_ROWS, LANES), F32),
        ),
        in_specs=[
            pl.BlockSpec((1, PAD_ROWS, 3 * width), lambda i: (i, 0, 0)),
            pl.BlockSpec((heads, PAD_ROWS, LANES), lambda i: (0, 0, 0)),
            pl.BlockSpec((1, 16, LANES), lambda i: (i, 0, 0)),
            pl.BlockSpec((1, PAD_ROWS, width), lambda i: (i, 0, 0)),
        ],
        out_specs=(
            pl.BlockSpec((1, PAD_ROWS, 3 * width), lambda i: (i, 0, 0)),
            pl.BlockSpec((heads, PAD_ROWS, LANES), lambda i: (0, 0, 0)),
        ),
        compiler_params=VMEM,
        name="attention_grad",
    )(qkv, bias, lse, grad)


def normalize(x):
    centered = x - jnp.mean(x, -1, keepdims=True)
    scale = lax.rsqrt(jnp.mean(centered * centered, -1, keepdims=True) + 1e-06)
    return centered * scale, scale


def normalize_grad(x_hat, scale, dy):
    return scale * (
        dy - jnp.mean(dy, -1, keepdims=True) - x_hat * jnp.mean(dy * x_hat, -1, keepdims=True)
    )


def gelu_and_slope(x):
    t = 1.0 / (1.0 + (0.3275911 / math.sqrt(2.0)) * jnp.abs(x))
    bell = jnp.exp(-0.5 * x * x)
    poly = 0.5 * 1.061405429
    for coef in (-1.453152027, 1.421413741, -0.284496736, 0.254829592):
        poly = poly * t + 0.5 * coef
    tail = poly * t * bell
    phi = jnp.where(x >= 0, 1.0 - tail, tail)
    return x * phi, phi + x * bell * (1.0 / math.sqrt(2.0 * math.pi))


def mlp_kernel(mid_ref, vec_ref, b1_ref, w1_ref, w2_ref, out_ref, mlp_ref, h2_ref, act_ref, slope_ref):
    step = pl.program_id(0)

    @pl.when(step == 0)
    def _():
        x_hat, _ = normalize(mid_ref[...])
        h2_ref[...] = (x_hat * vec_ref[0:1] + vec_ref[1:2]).astype(B16)

    pre = dot(h2_ref[...], w1_ref[...], NN) + b1_ref[...]
    act, slope = gelu_and_slope(pre)
    act = act.astype(B16)
    act_ref[...] = act
    slope_ref[...] = slope.astype(slope_ref.dtype)
    part = dot(act, w2_ref[...], NN)

    @pl.when(step == 0)
    def _():
        mlp_ref[...] = part + vec_ref[2:3]

    @pl.when(step > 0)
    def _():
        mlp_ref[...] += part

    @pl.when(step == pl.num_programs(0) - 1)
    def _():
        out_ref[...] = mid_ref[...] + vec_ref[3:4] * mlp_ref[...]


def mlp_forward(mid, vecs, b1, w1, w2, tile=768):
    rows, width = mid.shape
    hidden = w1.shape[1]
    whole = pl.BlockSpec((rows, width), lambda i: (0, 0))
    cols = pl.BlockSpec((rows, tile), lambda i: (0, i))
    return pl.pallas_call(
        mlp_kernel,
        grid=(hidden // tile,),
        out_shape=(
            jax.ShapeDtypeStruct((rows, width), F32),
            jax.ShapeDtypeStruct((rows, width), F32),
            jax.ShapeDtypeStruct((rows, width), B16),
            jax.ShapeDtypeStruct((rows, hidden), B16),
            jax.ShapeDtypeStruct((rows, hidden), F32),
        ),
        in_specs=[
            whole,
            pl.BlockSpec((8, width), lambda i: (0, 0)),
            pl.BlockSpec((1, tile), lambda i: (0, i)),
            pl.BlockSpec((width, tile), lambda i: (0, i)),
            pl.BlockSpec((tile, width), lambda i: (i, 0)),
        ],
        out_specs=(whole, whole, whole, cols, cols),
        compiler_params=VMEM,
        name="mlp",
    )(mid, vecs, b1, w1, w2)


def mlp_grad_kernel(
    g_ref, mid_ref, mlp_ref, branch_ref, vec_ref, h2_ref, act_ref, slope_ref, w1_ref, w2_ref,
    dw1_ref, dw2_ref, db1_ref, dmid_ref, dbranch_ref, sums_ref, dmlp_ref, h2t_ref, dh2_ref,
):
    step = pl.program_id(0)

    @pl.when(step == 0)
    def _():
        g = g_ref[...]
        dmlp = (g * vec_ref[3:4]).astype(B16)
        dmlp_ref[...] = dmlp
        h2t_ref[...] = h2_ref[...].T
        sums_ref[...] = jnp.zeros_like(sums_ref)
        sums_ref[0:1] = jnp.sum(g * mlp_ref[...], axis=0, keepdims=True)
        sums_ref[1:2] = jnp.sum(dmlp.astype(F32), axis=0, keepdims=True)

    dmlp = dmlp_ref[...]
    dact = dot(dmlp, w2_ref[...], NT)
    dpre = (dact * slope_ref[...].astype(F32)).astype(B16)
    dw2_ref[...] = dot(act_ref[...].T, dmlp, NN).astype(dw2_ref.dtype)
    dw1_ref[...] = dot(h2t_ref[...], dpre, NN).astype(dw1_ref.dtype)
    db1_ref[...] = jnp.sum(dpre.astype(F32), axis=0, keepdims=True)
    part = dot(dpre, w1_ref[...], NT)

    @pl.when(step == 0)
    def _():
        dh2_ref[...] = part

    @pl.when(step > 0)
    def _():
        dh2_ref[...] += part

    @pl.when(step == pl.num_programs(0) - 1)
    def _():
        x_hat, scale = normalize(mid_ref[...])
        dh2 = dh2_ref[...]
        sums_ref[2:3] = jnp.sum(dh2 * x_hat, axis=0, keepdims=True)
        sums_ref[3:4] = jnp.sum(dh2, axis=0, keepdims=True)
        dmid = g_ref[...] + normalize_grad(x_hat, scale, dh2 * vec_ref[0:1])
        dmid_ref[...] = dmid
        dbranch = (dmid * vec_ref[4:5]).astype(B16)
        dbranch_ref[...] = dbranch
        sums_ref[4:5] = jnp.sum(dmid * branch_ref[...], axis=0, keepdims=True)
        sums_ref[5:6] = jnp.sum(dbranch.astype(F32), axis=0, keepdims=True)


def mlp_backward(grad, mid, mlp_out, branch, vecs, h2, act, slope, w1, w2, tile=768):
    rows, width = mid.shape
    hidden = w1.shape[1]
    whole = pl.BlockSpec((rows, width), lambda i: (0, 0))
    cols = pl.BlockSpec((rows, tile), lambda i: (0, i))
    eight = pl.BlockSpec((8, width), lambda i: (0, 0))
    w1_spec = pl.BlockSpec((width, tile), lambda i: (0, i))
    w2_spec = pl.BlockSpec((tile, width), lambda i: (i, 0))
    return pl.pallas_call(
        mlp_grad_kernel,
        grid=(hidden // tile,),
        out_shape=(
            jax.ShapeDtypeStruct((width, hidden), B16),
            jax.ShapeDtypeStruct((hidden, width), B16),
            jax.ShapeDtypeStruct((1, hidden), F32),
            jax.ShapeDtypeStruct((rows, width), F32),
            jax.ShapeDtypeStruct((rows, width), B16),
            jax.ShapeDtypeStruct((8, width), F32),
        ),
        in_specs=[whole, whole, whole, whole, eight, whole, cols, cols, w1_spec, w2_spec],
        out_specs=(
            w1_spec,
            w2_spec,
            pl.BlockSpec((1, tile), lambda i: (0, i)),
            whole,
            whole,
            eight,
        ),
        scratch_shapes=[
            pltpu.VMEM((rows, width), B16),
            pltpu.VMEM((width, rows), B16),
            pltpu.VMEM((rows, width), F32),
        ],
        compiler_params=VMEM,
        name="mlp_grad",
    )(grad, mid, mlp_out, branch, vecs, h2, act, slope, w1, w2)


def layer_forward(x, weights, images):
    small, w_qkv, w_proj, w_one, w_two = weights
    width = x.shape[1]
    vec = small["vec"]
    x_hat, _ = normalize(x)
    h = (x_hat * vec[0] + vec[1]).astype(B16)
    qkv_bias = jnp.concatenate([vec[2], jnp.zeros((width,), F32), vec[3]])
    qkv = (dot(h, w_qkv, NN) + qkv_bias).astype(B16)
    qkv = qkv.reshape(images, PAD_ROWS, 3 * width)
    att, lse = attention_forward(qkv, small["bias"])
    att = att.reshape(images * PAD_ROWS, width)
    branch = dot(att, w_proj, NN) + vec[4]
    mid = x + vec[5] * branch
    mlp_vecs = jnp.concatenate([vec[6:10], vec[5:6], jnp.zeros((3, width), F32)])
    out, mlp_out, h2, act, slope = mlp_forward(mid, mlp_vecs, small["b1"], w_one, w_two)
    return out, (x, h, qkv, lse, att, branch, mid, mlp_vecs, mlp_out, h2, act, slope)


def layer_backward(saved, weights, grad, images):
    x, h, qkv, lse, att, branch, mid, mlp_vecs, mlp_out, h2, act, slope = saved
    small, w_qkv, w_proj, w_one, w_two = weights
    vec = small["vec"]
    width = x.shape[1]
    d_one, d_two, d_b1, d_mid, d_branch, sums = mlp_backward(
        grad, mid, mlp_out, branch, mlp_vecs, h2, act, slope, w_one, w_two
    )
    d_att = dot(d_branch, w_proj, NT).astype(B16)
    d_proj = dot(att, d_branch, TN).astype(B16)
    d_qkv, d_bias = attention_backward(
        qkv, small["bias"], lse, d_att.reshape(images, PAD_ROWS, width)
    )
    d_qkv = d_qkv.reshape(images * PAD_ROWS, 3 * width)
    d_wqkv = dot(h, d_qkv, TN).astype(B16)
    d_h = dot(d_qkv, w_qkv, NT)
    x_hat, scale = normalize(x)
    d_gain = jnp.sum(d_h * x_hat, 0)
    d_shift = jnp.sum(d_h, 0)
    d_x = d_mid + normalize_grad(x_hat, scale, d_h * vec[0])
    sums_qkv = jnp.sum(d_qkv.astype(F32), 0)
    d_table = reduce_bias(d_bias, small["entries"])
    d_vec = jnp.stack(
        [
            d_gain, d_shift, sums_qkv[:width], sums_qkv[2 * width :], sums[5], sums[4],
            sums[2], sums[3], sums[1], sums[0],
        ]
    )
    return d_x, (d_wqkv, d_proj, d_one, d_two), (d_vec, d_b1.reshape(-1), d_table)


def pack_small(vectors, b1, table, dtype):
    rows = vectors[0].shape[0]
    tab = jnp.pad(jnp.transpose(table), ((0, rows - table.shape[1]), (0, 0)))
    cols = jnp.concatenate(
        [jnp.stack(vectors, axis=1), b1.reshape(rows, -1), tab], axis=1
    ).astype(dtype)
    return jnp.pad(cols, ((0, 0), (0, SMALL - cols.shape[1])))


def unpack_small(packed, heads, per_dev, shards):
    count = 10
    ratio = 4
    rows = packed.shape[0]
    turned = jnp.transpose(packed.astype(F32))
    vec = turned[:count]
    b1 = packed[:, count : count + ratio].astype(F32).reshape(1, rows * ratio)
    tab = packed[:, count + ratio : count + ratio + heads].astype(F32)
    tab = tab.reshape(shards, rows // shards, heads)[:, :per_dev].reshape(shards * per_dev, heads)
    table = jnp.transpose(tab)
    return {"vec": vec, "b1": b1, "bias": build_bias(table), "entries": table.shape[1]}


def pack_small_grad(d_vec, d_b1, d_table, shards):
    rows = d_vec.shape[1]
    heads, entries = d_table.shape
    per_dev = entries // shards
    tab = jnp.transpose(d_table).reshape(shards, per_dev, heads)
    tab = jnp.pad(tab, ((0, 0), (0, rows // shards - per_dev), (0, 0))).reshape(rows, heads)
    cols = jnp.concatenate([jnp.transpose(d_vec), d_b1.reshape(rows, -1), tab], axis=1)
    return jnp.pad(cols, ((0, 0), (0, SMALL - cols.shape[1])))


def unpack_small_grad(packed, heads, per_dev):
    vec = [packed[:, i] for i in range(10)]
    b1 = packed[:, 10:14].reshape(-1)
    table = jnp.transpose(packed[:per_dev, 14 : 14 + heads])
    return vec, b1, table


def per_device(
    shards,
    tokens, masked_rows, cotangent, norm1_gain, norm1_bias, qkv_weight, q_bias, v_bias,
    proj_weight, proj_bias, gamma_attn, norm2_gain, norm2_bias, fc1_weight, fc1_bias,
    fc2_weight, fc2_bias, gamma_mlp, rel_table,
):
    vectors = (norm1_gain, norm1_bias, q_bias, v_bias, proj_bias, gamma_attn, norm2_gain,
               norm2_bias, fc2_bias, gamma_mlp)
    width = tokens.shape[1]
    images = masked_rows.shape[0]
    heads, per_dev = rel_table.shape[1:]
    own_rows = qkv_weight.shape[1]
    ratio = fc2_weight.shape[1] // own_rows
    hidden = fc1_weight.shape[2]
    ends = np.cumsum([3 * width, width, hidden, ratio * width, SMALL])

    def pad_rows(v):
        v = v.astype(F32).reshape(images, IMG_ROWS, width)
        v = jnp.pad(v, ((0, 0), (0, PAD_ROWS - IMG_ROWS), (0, 0)))
        return v.reshape(images * PAD_ROWS, width)

    def cut_rows(v):
        return v.reshape(images, PAD_ROWS, width)[:, :IMG_ROWS].reshape(images * IMG_ROWS, width)

    def fetch(layer):
        two = fc2_weight[layer].reshape(ratio, own_rows, width)
        small = pack_small([v[layer] for v in vectors], fc1_bias[layer], rel_table[layer], B16)
        block = jnp.concatenate(
            [qkv_weight[layer], proj_weight[layer], fc1_weight[layer]]
            + [two[i] for i in range(ratio)]
            + [small],
            axis=1,
        )
        full = lax.all_gather(block, AXES, axis=0, tiled=True)
        w_qkv, w_proj, w_one, w_two, small = jnp.split(full, ends[:-1], axis=1)
        w_two = w_two.reshape(shards, own_rows, ratio, width).transpose(0, 2, 1, 3)
        w_two = w_two.reshape(hidden, width)
        return unpack_small(small, heads, per_dev, shards), w_qkv, w_proj, w_one, w_two

    def reduce(big, small):
        d_wqkv, d_proj, d_one, d_two = big
        packed = pack_small_grad(*small, shards).astype(B16)
        d_two = d_two.reshape(shards, ratio, own_rows, width).transpose(0, 2, 1, 3)
        d_two = d_two.reshape(width, ratio * width)
        block = jnp.concatenate([d_wqkv, d_proj, d_one, d_two, packed], axis=1)
        own = lax.psum_scatter(block, AXES, scatter_dimension=0, tiled=True).astype(F32)
        o_qkv, o_proj, o_one, o_two, o_small = jnp.split(own, ends[:-1], axis=1)
        o_two = o_two.reshape(own_rows, ratio, width).transpose(1, 0, 2)
        o_two = o_two.reshape(ratio * own_rows, width)
        return o_qkv, o_proj, o_one, o_two, unpack_small_grad(o_small, heads, per_dev)

    x = pad_rows(tokens)
    weights = []
    saved = []
    for layer in range(LAYERS):
        weights.append(fetch(layer))
        x, keep = layer_forward(x, weights[layer], images)
        saved.append(keep)
    encoded = cut_rows(x.astype(B16))

    positions = jnp.arange(IMG_ROWS, dtype=jnp.int32)
    mask = jnp.any(masked_rows[:, :, None] == positions[None, None, :], axis=1)
    mask = jnp.pad(mask, ((0, 0), (0, PAD_ROWS - IMG_ROWS))).reshape(-1, 1)
    grad = jnp.where(mask, pad_rows(cotangent), 0.0)
    owned = [None] * LAYERS
    for layer in reversed(range(LAYERS)):
        grad, big, small = layer_backward(saved[layer], weights[layer], grad, images)
        owned[layer] = reduce(big, small)

    def both(pick):
        return jnp.stack([pick(o) for o in owned])

    g = [both(lambda o, i=i: o[4][0][i]) for i in range(10)]
    g_qkv, g_proj, g_one, g_two = (both(lambda o, i=i: o[i]) for i in range(4))
    g_b1 = both(lambda o: o[4][1])
    g_table = both(lambda o: o[4][2])
    return (encoded, cut_rows(grad), g[0], g[1], g_qkv, g[2], g[3], g_proj, g[4], g[5], g[6],
            g[7], g_one, g_b1, g_two, g[8], g[9], g_table)


def solution(mesh):
    shards = math.prod(mesh.shape[a] for a in AXES)
    row = P(AXES, None)
    vec = P(None, AXES)
    mat = P(None, AXES, None)
    tab = P(None, None, AXES)
    return jax.shard_map(
        functools.partial(per_device, shards),
        mesh=mesh,
        in_specs=(row, row, row, vec, vec, mat, vec, vec, mat, vec, vec, vec, vec, mat, vec, mat,
                  vec, vec, tab),
        out_specs=(row, row, vec, vec, mat, vec, vec, mat, vec, vec, vec, vec, mat, vec, mat,
                   vec, vec, tab),
        check_vma=False,
    )
```

```python
import functools
import math

import jax
import jax.numpy as jnp
import numpy as np
from jax import lax
from jax.experimental import pallas as pl
from jax.experimental.pallas import tpu as pltpu
from jax.sharding import PartitionSpec as P

GRID = 14
SPAN = 2 * GRID - 1
LAYERS = 2
IMG_ROWS = GRID * GRID + 1
PAD_ROWS = 208
LANES = 256
HEAD = 64
PAIR = 2 * HEAD
NEG = -1e30
TILE = 768
WIDE = 384
BLOCK = 16
SMALL_ROWS = 32
F32 = jnp.float32
B16 = jnp.bfloat16
AXES = ("dp", "fsdp")


def cost(us):
    return pl.CostEstimate(flops=us * 1_100_000_000, bytes_accessed=us * 3_500_000, transcendentals=0)


ANY = pl.BlockSpec(memory_space=pl.ANY)
SMEM = pl.BlockSpec(memory_space=pltpu.SMEM)

N1_GAIN, N1_SHIFT, Q_BIAS, V_BIAS, B_PROJ, G_ATTN, N2_GAIN, N2_SHIFT, B_TWO, G_MLP = range(10)
B_ONE = 10
TABLE = 14


def params(limit=56):
    return pltpu.CompilerParams(vmem_limit_bytes=limit * 1024 * 1024)


def dot(a, b, dims):
    return lax.dot_general(a, b, (dims, ((), ())), preferred_element_type=F32)


NN = ((1,), (0,))
NT = ((1,), (1,))
TN = ((0,), (0,))


def lane_onehot():
    out = np.zeros((WIDE, LANES), np.float32)
    for a in range(GRID):
        for b in range(GRID):
            out[SPAN * a + b, 1 + GRID * a + b] = 1.0
    return out


def row_onehot(turned):
    out = np.zeros((PAD_ROWS, BLOCK * GRID), np.float32)
    for c in range(GRID):
        for d in range(GRID):
            out[1 + GRID * c + d, BLOCK * c + (GRID - 1 - d if turned else d)] = 1.0
    return out


def bias_kernel(heads, small_ref, rows_ref, lanes_ref, out_ref, wide_ref):
    head = lax.rem(pl.program_id(0), heads)
    table = small_ref[0, pl.ds(TABLE + head, 1), :]
    shifted = pltpu.roll(jnp.broadcast_to(table, (BLOCK, TILE)), TILE - (GRID - 1), 1)
    shifted = pltpu.roll(shifted, 0, 1, stride=1, stride_axis=0)
    for c in range(GRID):
        start = SPAN * (GRID - 1 - c)
        wide_ref[BLOCK * c : BLOCK * (c + 1), :] = shifted[:, start : start + WIDE].astype(B16)
    narrow = dot(wide_ref[...], lanes_ref[...], NN).astype(B16)
    val = dot(rows_ref[...], narrow, NN)
    row = lax.broadcasted_iota(jnp.int32, (PAD_ROWS, LANES), 0)
    lane = lax.broadcasted_iota(jnp.int32, (PAD_ROWS, LANES), 1)
    cls = SPAN * SPAN
    val = jnp.where(lane == 0, table[:, cls : cls + 1], val)
    first = jnp.where(lane == 0, table[:, cls + 2 : cls + 3], table[:, cls + 1 : cls + 2])
    val = jnp.where(row == 0, first, val)
    out_ref[0] = jnp.where(row >= IMG_ROWS, NEG, val)


def build_bias(small, heads):
    layers = small.shape[0]
    return pl.pallas_call(
        functools.partial(bias_kernel, heads),
        grid=(layers * heads,),
        out_shape=jax.ShapeDtypeStruct((layers * heads, PAD_ROWS, LANES), F32),
        in_specs=[
            pl.BlockSpec((1, SMALL_ROWS, TILE), lambda h: (h // heads, 0, 0)),
            pl.BlockSpec((PAD_ROWS, BLOCK * GRID), lambda h: (0, 0)),
            pl.BlockSpec((WIDE, LANES), lambda h: (0, 0)),
        ],
        out_specs=pl.BlockSpec((1, PAD_ROWS, LANES), lambda h: (h, 0, 0)),
        scratch_shapes=[pltpu.VMEM((BLOCK * GRID, WIDE), B16)],
        compiler_params=params(),
        cost_estimate=cost(18),
        name="bias_expand",
    )(small, jnp.asarray(row_onehot(False), B16), jnp.asarray(lane_onehot(), B16))


def bias_grad_kernel(g_ref, rows_ref, lanes_ref, *refs):
    out_ref, acc_ref = refs[-2:]
    row = lax.broadcasted_iota(jnp.int32, (PAD_ROWS, LANES), 0)
    lane = lax.broadcasted_iota(jnp.int32, (PAD_ROWS, LANES), 1)
    g = jnp.where((lane < IMG_ROWS) & (row < IMG_ROWS), g_ref[0], 0.0)
    high = g.astype(B16)
    wide = None
    for part in (high, (g - high.astype(F32)).astype(B16)):
        moved = dot(rows_ref[...], part, NN).astype(B16)
        moved = dot(moved, lanes_ref[...], NN)
        wide = moved if wide is None else wide + moved
    acc_ref[...] = jnp.zeros_like(acc_ref)
    for c in range(GRID):
        start = SPAN * (GRID - 1 - c)
        acc_ref[:, start : start + WIDE] += wide[BLOCK * c : BLOCK * (c + 1), :]
    turned = pltpu.roll(acc_ref[...], 0, 1, stride=1, stride_axis=0)
    total = jnp.sum(turned, axis=0, keepdims=True)
    column = jnp.sum(jnp.where(lane[:, :1] == 0, g[:, :1], 0.0), axis=0, keepdims=True)
    to_self = g[0:1, 0:1]
    to_patch = column - to_self
    from_patch = jnp.sum(g[0:1, :], axis=1, keepdims=True) - to_self
    spot = lax.broadcasted_iota(jnp.int32, (1, TILE), 1)
    cls = SPAN * SPAN
    total = jnp.where(spot == cls, to_patch, total)
    total = jnp.where(spot == cls + 1, from_patch, total)
    out_ref[0] = jnp.where(spot == cls + 2, to_self, total)


def reduce_bias(grad, after=()):
    heads = grad.shape[0]
    out = pl.pallas_call(
        bias_grad_kernel,
        grid=(heads,),
        out_shape=jax.ShapeDtypeStruct((heads, 1, TILE), F32),
        in_specs=[
            pl.BlockSpec((1, PAD_ROWS, LANES), lambda h: (h, 0, 0)),
            pl.BlockSpec((BLOCK * GRID, PAD_ROWS), lambda h: (0, 0)),
            pl.BlockSpec((LANES, WIDE), lambda h: (0, 0)),
        ]
        + [ANY] * len(after),
        out_specs=pl.BlockSpec((1, 1, TILE), lambda h: (h, 0, 0)),
        scratch_shapes=[pltpu.VMEM((BLOCK, TILE), F32)],
        compiler_params=params(),
        cost_estimate=cost(11),
        name="bias_reduce",
    )(grad, jnp.asarray(row_onehot(True).T, B16), jnp.asarray(lane_onehot().T, B16), *after)
    return out.reshape(heads, TILE)


def head_mask(which):
    lane = lax.broadcasted_iota(jnp.int32, (PAD_ROWS, PAIR), 1)
    return (lane < HEAD) if which == 0 else (lane >= HEAD)


def attention_kernel(width, qkv_ref, bias_ref, out_ref, lse_ref):
    heads = width // HEAD
    for pair in range(heads // 2):
        at = pair * PAIR
        q = qkv_ref[0, :, at : at + PAIR]
        k = qkv_ref[0, :, width + at : width + at + PAIR]
        v = qkv_ref[0, :, 2 * width + at : 2 * width + at + PAIR]
        q = q * jnp.asarray(HEAD ** (-0.5), B16)
        v_t = v.T
        parts = []
        for t in range(2):
            head = 2 * pair + t
            q_t = jnp.where(head_mask(t), q, jnp.zeros_like(q))
            scores = dot(k, q_t, NT) + bias_ref[head, :, 0:PAD_ROWS]
            top = jnp.max(scores, axis=0, keepdims=True)
            weights = jnp.exp(scores - top)
            total = jnp.sum(weights, axis=0, keepdims=True)
            probs = (weights * (1.0 / total)).astype(B16)
            lse_ref[0, head : head + 1, 0:PAD_ROWS] = top + jnp.log(total)
            parts.append(dot(v_t[t * HEAD : (t + 1) * HEAD], probs, NN))
        out_ref[0, :, at : at + PAIR] = jnp.concatenate(parts, axis=0).T.astype(B16)


def attention_forward(qkv, bias, layer):
    images = qkv.shape[0]
    width = qkv.shape[2] // 3
    heads = width // HEAD
    return pl.pallas_call(
        functools.partial(attention_kernel, width),
        grid=(images,),
        out_shape=(
            jax.ShapeDtypeStruct((images, PAD_ROWS, width), B16),
            jax.ShapeDtypeStruct((images, 16, LANES), F32),
        ),
        in_specs=[
            pl.BlockSpec((1, PAD_ROWS, 3 * width), lambda i: (i, 0, 0)),
            pl.BlockSpec((heads, PAD_ROWS, LANES), lambda i: (layer, 0, 0)),
        ],
        out_specs=(
            pl.BlockSpec((1, PAD_ROWS, width), lambda i: (i, 0, 0)),
            pl.BlockSpec((1, 16, LANES), lambda i: (i, 0, 0)),
        ),
        compiler_params=params(),
        cost_estimate=cost(8),
        name="attention",
    )(qkv, bias)


def attention_grad_kernel(width, qkv_ref, bias_ref, lse_ref, g_ref, *refs):
    out_ref, dbias_ref = refs[-2:]
    heads = width // HEAD
    scale = HEAD ** (-0.5)

    @pl.when(pl.program_id(0) == 0)
    def _():
        dbias_ref[...] = jnp.zeros_like(dbias_ref)

    for pair in range(heads // 2):
        at = pair * PAIR
        q = qkv_ref[0, :, at : at + PAIR]
        k = qkv_ref[0, :, width + at : width + at + PAIR]
        v = qkv_ref[0, :, 2 * width + at : 2 * width + at + PAIR]
        g = g_ref[0, :, at : at + PAIR]
        q = q * jnp.asarray(scale, B16)
        k_t = k.T
        dq_parts = []
        dk = None
        dv = None
        for t in range(2):
            head = 2 * pair + t
            q_t = jnp.where(head_mask(t), q, jnp.zeros_like(q))
            g_t = jnp.where(head_mask(t), g, jnp.zeros_like(g))
            scores = dot(k, q_t, NT) + bias_ref[head, :, 0:PAD_ROWS]
            probs = jnp.exp(scores - lse_ref[0, head : head + 1, 0:PAD_ROWS])
            dprobs = dot(v, g_t, NT)
            dv_t = dot(probs.astype(B16), g_t, NN)
            mean = jnp.sum(probs * dprobs, axis=0, keepdims=True)
            dscores = (probs * (dprobs - mean)).astype(B16)
            dbias_ref[head, :, 0:PAD_ROWS] += dscores.astype(F32)
            dk_t = dot(dscores, q_t, NN)
            dq_parts.append(dot(k_t[t * HEAD : (t + 1) * HEAD], dscores, NN))
            dk = dk_t if dk is None else dk + dk_t
            dv = dv_t if dv is None else dv + dv_t
        dq = jnp.concatenate(dq_parts, axis=0).T * scale
        out_ref[0, :, at : at + PAIR] = dq.astype(B16)
        out_ref[0, :, width + at : width + at + PAIR] = dk.astype(B16)
        out_ref[0, :, 2 * width + at : 2 * width + at + PAIR] = dv.astype(B16)


def attention_backward(qkv, bias, lse, grad, layer, after=()):
    images = qkv.shape[0]
    width = qkv.shape[2] // 3
    heads = width // HEAD
    return pl.pallas_call(
        functools.partial(attention_grad_kernel, width),
        grid=(images,),
        out_shape=(
            jax.ShapeDtypeStruct((images, PAD_ROWS, 3 * width), B16),
            jax.ShapeDtypeStruct((heads, PAD_ROWS, LANES), F32),
        ),
        in_specs=[
            pl.BlockSpec((1, PAD_ROWS, 3 * width), lambda i: (i, 0, 0)),
            pl.BlockSpec((heads, PAD_ROWS, LANES), lambda i: (layer, 0, 0)),
            pl.BlockSpec((1, 16, LANES), lambda i: (i, 0, 0)),
            pl.BlockSpec((1, PAD_ROWS, width), lambda i: (i, 0, 0)),
        ]
        + [ANY] * len(after),
        out_specs=(
            pl.BlockSpec((1, PAD_ROWS, 3 * width), lambda i: (i, 0, 0)),
            pl.BlockSpec((heads, PAD_ROWS, LANES), lambda i: (0, 0, 0)),
        ),
        compiler_params=params(),
        cost_estimate=cost(12),
        name="attention_grad",
    )(qkv, bias, lse, grad, *after)


def normalize(x):
    centered = x - jnp.mean(x, -1, keepdims=True)
    scale = lax.rsqrt(jnp.mean(centered * centered, -1, keepdims=True) + 1e-06)
    return centered * scale, scale


def normalize_grad(x_hat, scale, dy):
    return scale * (
        dy - jnp.mean(dy, -1, keepdims=True) - x_hat * jnp.mean(dy * x_hat, -1, keepdims=True)
    )


def gelu_and_slope(x):
    t = 1.0 / (1.0 + (0.3275911 / math.sqrt(2.0)) * jnp.abs(x))
    bell = jnp.exp(-0.5 * x * x)
    poly = 0.5 * 1.061405429
    for coef in (-1.453152027, 1.421413741, -0.284496736, 0.254829592):
        poly = poly * t + 0.5 * coef
    tail = poly * t * bell
    phi = jnp.where(x >= 0, 1.0 - tail, tail)
    return x * phi, phi + x * bell * (1.0 / math.sqrt(2.0 * math.pi))


def total_rows(v):
    return jnp.sum(v, axis=0, keepdims=True)


def small_spec(layer):
    return pl.BlockSpec((1, SMALL_ROWS, TILE), lambda i: (layer, 0, 0))


def whole_spec(shape):
    return pl.BlockSpec(shape, lambda i: (0,) * len(shape))


def col_spec(weight):
    array, first = weight
    return pl.BlockSpec((array.shape[0], TILE), lambda i: (0, first + i))


def qkv_kernel(x_ref, small_ref, w_ref, qkv_ref, h_ref):
    step = pl.program_id(0)

    @pl.when(step == 0)
    def _():
        x_hat, _ = normalize(x_ref[...])
        gain = small_ref[0, N1_GAIN : N1_GAIN + 1]
        h_ref[...] = (x_hat * gain + small_ref[0, N1_SHIFT : N1_SHIFT + 1]).astype(B16)

    zero = jnp.zeros((1, TILE), F32)
    bias = jnp.where(step == 0, small_ref[0, Q_BIAS : Q_BIAS + 1], zero)
    bias = jnp.where(step == 2, small_ref[0, V_BIAS : V_BIAS + 1], bias)
    qkv_ref[...] = (dot(h_ref[...], w_ref[...], NN) + bias).astype(B16)


def qkv_forward(x, small, layer, w_qkv):
    rows, width = x.shape
    return pl.pallas_call(
        qkv_kernel,
        grid=(3,),
        out_shape=(
            jax.ShapeDtypeStruct((rows, 3 * width), B16),
            jax.ShapeDtypeStruct((rows, width), B16),
        ),
        in_specs=[whole_spec((rows, width)), small_spec(layer), col_spec(w_qkv)],
        out_specs=(
            pl.BlockSpec((rows, TILE), lambda i: (0, i)),
            whole_spec((rows, width)),
        ),
        compiler_params=params(),
        cost_estimate=cost(6),
        name="qkv",
    )(x, small, w_qkv[0])


def qkv_grad_kernel(core_ref, g_ref, h_ref, x_ref, dmid_ref, small_ref, w_ref, *refs):
    theirs_ref, mine_ref, dx_ref, sums_ref, ht_ref, dh_ref = refs[-6:]
    step = pl.program_id(0)

    @pl.when(step == 0)
    def _():
        ht_ref[...] = h_ref[...].T
        sums_ref[...] = jnp.zeros_like(sums_ref)

    g = g_ref[...]
    dw = dot(ht_ref[...], g, NN).astype(B16)
    low, high = dw[:, : TILE // 2], dw[:, TILE // 2 :]

    @pl.when(core_ref[0] == 0)
    def _():
        mine_ref[...] = low
        theirs_ref[...] = high

    @pl.when(core_ref[0] != 0)
    def _():
        mine_ref[...] = high
        theirs_ref[...] = low

    part = dot(g, w_ref[...], NT)
    total = total_rows(g.astype(F32))

    @pl.when(step == 0)
    def _():
        dh_ref[...] = part
        sums_ref[Q_BIAS : Q_BIAS + 1] = total

    @pl.when(step > 0)
    def _():
        dh_ref[...] += part

    @pl.when(step == 2)
    def _():
        sums_ref[V_BIAS : V_BIAS + 1] = total
        dh = dh_ref[...]
        x_hat, scale = normalize(x_ref[...])
        sums_ref[N1_GAIN : N1_GAIN + 1] = total_rows(dh * x_hat)
        sums_ref[N1_SHIFT : N1_SHIFT + 1] = total_rows(dh)
        gain = small_ref[0, N1_GAIN : N1_GAIN + 1]
        dx_ref[...] = dmid_ref[...] + normalize_grad(x_hat, scale, dh * gain)


def qkv_backward(core, grad, h, x, d_mid, small, layer, w_qkv, after=()):
    rows, width = x.shape
    whole = whole_spec((rows, width))
    tiles = pl.BlockSpec((rows, TILE), lambda i: (0, i))
    return pl.pallas_call(
        qkv_grad_kernel,
        grid=(3,),
        out_shape=(
            jax.ShapeDtypeStruct((width, 3 * width // 2), B16),
            jax.ShapeDtypeStruct((width, 3 * width // 2), B16),
            jax.ShapeDtypeStruct((rows, width), F32),
            jax.ShapeDtypeStruct((8, width), F32),
        ),
        in_specs=[SMEM, tiles, whole, whole, whole, small_spec(layer), col_spec(w_qkv)]
        + [ANY] * len(after),
        out_specs=(
            pl.BlockSpec((width, TILE // 2), lambda i: (0, i)),
            pl.BlockSpec((width, TILE // 2), lambda i: (0, i)),
            whole,
            whole_spec((8, width)),
        ),
        scratch_shapes=[pltpu.VMEM((width, rows), B16), pltpu.VMEM((rows, width), F32)],
        compiler_params=params(),
        cost_estimate=cost(11),
        name="qkv_grad",
    )(core, grad, h, x, d_mid, small, w_qkv[0], *after)


def mlp_kernel(
    x_ref, att_ref, small_ref, wp_ref, w1_ref, w2_ref,
    out_ref, branch_ref, mid_ref, mlp_ref, h2_ref, act_ref, slope_ref,
):
    step = pl.program_id(0)

    def vec(i):
        return small_ref[0, i : i + 1]

    @pl.when(step == 0)
    def _():
        branch = dot(att_ref[...], wp_ref[...], NN) + vec(B_PROJ)
        branch_ref[...] = branch
        mid = x_ref[...] + vec(G_ATTN) * branch
        mid_ref[...] = mid
        x_hat, _ = normalize(mid)
        h2_ref[...] = (x_hat * vec(N2_GAIN) + vec(N2_SHIFT)).astype(B16)

    pre = dot(h2_ref[...], w1_ref[...], NN) + small_ref[0, pl.ds(B_ONE + step, 1)]
    act, slope = gelu_and_slope(pre)
    act = act.astype(B16)
    act_ref[...] = act
    slope_ref[...] = slope.astype(B16)
    part = dot(act, w2_ref[...], NN)

    @pl.when(step == 0)
    def _():
        mlp_ref[...] = part + vec(B_TWO)

    @pl.when(step > 0)
    def _():
        mlp_ref[...] += part

    @pl.when(step == pl.num_programs(0) - 1)
    def _():
        out_ref[...] = mid_ref[...] + vec(G_MLP) * mlp_ref[...]


def mlp_forward(x, att, small, layer, w_proj, w_one, w_two):
    rows, width = x.shape
    hidden = w_two.shape[0]
    whole = whole_spec((rows, width))
    cols = pl.BlockSpec((rows, TILE), lambda i: (0, i))
    full = jax.ShapeDtypeStruct((rows, width), F32)
    proj_at = w_proj[1]
    return pl.pallas_call(
        mlp_kernel,
        grid=(hidden // TILE,),
        out_shape=(
            full, full, full, full,
            jax.ShapeDtypeStruct((rows, width), B16),
            jax.ShapeDtypeStruct((rows, hidden), B16),
            jax.ShapeDtypeStruct((rows, hidden), B16),
        ),
        in_specs=[
            whole,
            whole,
            small_spec(layer),
            pl.BlockSpec((width, TILE), lambda i: (0, proj_at)),
            col_spec(w_one),
            pl.BlockSpec((TILE, width), lambda i: (i, 0)),
        ],
        out_specs=(whole, whole, whole, whole, whole, cols, cols),
        compiler_params=params(),
        cost_estimate=cost(15),
        name="mlp",
    )(x, att, small, w_proj[0], w_one[0], w_two)


SUM_ROWS = 16
STRIP = 128


def mlp_grad_kernel(
    core_ref, g_ref, mid_ref, mlp_ref, branch_ref, att_ref, small_ref, h2_ref, act_ref, slope_ref, wp_ref,
    w1_ref, w2_ref, *refs,
):
    (theirs_ref, mine_ref, dmid_ref, datt_ref, sums_ref,
     dmlp_ref, h2t_ref, dh2_ref, one_ref, wide_ref, two_ref, proj_ref, sems) = refs[-13:]
    step = pl.program_id(0)
    steps = pl.num_programs(0)
    slot = lax.rem(step, 2)
    width = mid_ref.shape[1]
    hidden = 4 * width
    part_rows = TILE // 4

    def vec(i):
        return small_ref[0, i : i + 1]

    def put(row, value):
        at = row - B_PROJ
        sums_ref[at : at + 1] = value

    def copy_one(out_ref, j, s):
        return pltpu.make_async_copy(
            one_ref.at[s],
            out_ref.at[:, pl.ds(pl.multiple_of(lax.rem(j, 2) * TILE, TILE), TILE)],
            sems.at[0, s],
        )

    def copy_two(out_ref, j, s, which):
        return pltpu.make_async_copy(
            two_ref.at[s, which],
            out_ref.at[pl.ds(pl.multiple_of(j * part_rows, part_rows), part_rows),
                       pl.ds(2 * width, 2 * width)],
            sems.at[1 + which, s],
        )

    def proj_copy(out_ref, which):
        return pltpu.make_async_copy(
            proj_ref.at[which], out_ref.at[:, pl.ds(4 * width, width // 2)], sems.at[3, which]
        )

    def on_halves(run):
        for core in range(2):

            @pl.when(core_ref[0] == core)
            def _(core=core):
                run(mine_ref, core)
                run(theirs_ref, 1 - core)

    def send_one(j, s):
        def run(out_ref, which):
            @pl.when(j // 2 == which)
            def _():
                copy_one(out_ref, j, s).start()

        on_halves(run)

    def send_two(j, s):
        on_halves(lambda out_ref, which: copy_two(out_ref, j, s, which).start())

    def wait_step(j, s):
        copy_one(mine_ref, j, s).wait()
        for which in range(2):
            copy_two(mine_ref, j, s, which).wait()

    @pl.when(step == 0)
    def _():
        g = g_ref[...]
        dmlp = (g * vec(G_MLP)).astype(B16)
        dmlp_ref[...] = dmlp
        h2t_ref[...] = h2_ref[...].T
        sums_ref[...] = jnp.zeros_like(sums_ref)
        put(G_MLP, total_rows(g * mlp_ref[...]))
        put(B_TWO, total_rows(dmlp.astype(F32)))

    @pl.when(step >= 2)
    def _():
        wait_step(step - 2, slot)

    dmlp = dmlp_ref[...]
    dact = dot(dmlp, w2_ref[...], NT)
    dpre = (dact * slope_ref[...].astype(F32)).astype(B16)
    wide = dot(act_ref[...].T, dmlp, NN)
    for t in range(wide_ref.shape[0]):
        wide_ref[t] = wide[:, t * STRIP : (t + 1) * STRIP]
        for k in range(4):
            at = (k % 2) * width + t * STRIP
            two_ref[slot, k // 2, :, at : at + STRIP] = wide_ref[
                t, pl.ds(k, part_rows, stride=4), :
            ].astype(B16)
    send_two(step, slot)
    one_ref[slot] = dot(h2t_ref[...], dpre, NN).astype(B16)
    send_one(step, slot)
    sums_ref[pl.ds(B_ONE - B_PROJ + step, 1)] = total_rows(dpre.astype(F32))
    part = dot(dpre, w1_ref[...], NT)

    @pl.when(step == 0)
    def _():
        dh2_ref[...] = part

    @pl.when(step > 0)
    def _():
        dh2_ref[...] += part

    @pl.when(step == steps - 1)
    def _():
        x_hat, scale = normalize(mid_ref[...])
        dh2 = dh2_ref[...]
        put(N2_GAIN, total_rows(dh2 * x_hat))
        put(N2_SHIFT, total_rows(dh2))
        dmid = g_ref[...] + normalize_grad(x_hat, scale, dh2 * vec(N2_GAIN))
        dmid_ref[...] = dmid
        dbranch = (dmid * vec(G_ATTN)).astype(B16)
        put(G_ATTN, total_rows(dmid * branch_ref[...]))
        put(B_PROJ, total_rows(dbranch.astype(F32)))
        dproj = dot(att_ref[...].T, dbranch, NN).astype(B16)
        proj_ref[0] = dproj[:, : width // 2]
        proj_ref[1] = dproj[:, width // 2 :]
        on_halves(lambda out_ref, which: proj_copy(out_ref, which).start())
        datt_ref[...] = dot(dbranch, wp_ref[...], NT).astype(B16)
        wait_step(step - 1, 1 - slot)
        wait_step(step, slot)
        for which in range(2):
            proj_copy(mine_ref, which).wait()


def mlp_backward(core, grad, mid, mlp_out, branch, att, small, layer, h2, act, slope, w_proj, w_one,
                 w_two, after=()):
    rows, width = mid.shape
    hidden = w_two.shape[0]
    whole = whole_spec((rows, width))
    cols = pl.BlockSpec((rows, TILE), lambda i: (0, i))
    proj_at = w_proj[1]
    return pl.pallas_call(
        mlp_grad_kernel,
        grid=(hidden // TILE,),
        out_shape=(
            jax.ShapeDtypeStruct((width, hidden + width // 2), B16),
            jax.ShapeDtypeStruct((width, hidden + width // 2), B16),
            jax.ShapeDtypeStruct((rows, width), F32),
            jax.ShapeDtypeStruct((rows, width), B16),
            jax.ShapeDtypeStruct((SUM_ROWS, width), F32),
        ),
        in_specs=[
            SMEM, whole, whole, whole, whole, whole, small_spec(layer), whole, cols, cols,
            pl.BlockSpec((width, TILE), lambda i: (0, proj_at)),
            col_spec(w_one),
            pl.BlockSpec((TILE, width), lambda i: (i, 0)),
        ]
        + [ANY] * len(after),
        out_specs=(ANY, ANY, whole, whole, whole_spec((SUM_ROWS, width))),
        scratch_shapes=[
            pltpu.VMEM((rows, width), B16),
            pltpu.VMEM((width, rows), B16),
            pltpu.VMEM((rows, width), F32),
            pltpu.VMEM((2, width, TILE), B16),
            pltpu.VMEM((width // STRIP, TILE, STRIP), F32),
            pltpu.VMEM((2, 2, TILE // 4, 2 * width), B16),
            pltpu.VMEM((2, width, width // 2), B16),
            pltpu.SemaphoreType.DMA((4, 2)),
        ],
        compiler_params=params(),
        cost_estimate=cost(20),
        name="mlp_grad",
    )(core, grad, mid, mlp_out, branch, att, small, h2, act, slope, w_proj[0], w_one[0], w_two, *after)


CHIP_Y, CORES, CHIP_Z, CHIP_X = 2, 2, 4, 2
FAST_SHARDS = CHIP_Y * CORES * CHIP_Z * CHIP_X

def place(y, c, z, x):
    return (y * CORES + c) * (CHIP_Z * CHIP_X) + z * CHIP_X + x

def moves(fn):
    pairs = []
    for y in range(CHIP_Y):
        for c in range(CORES):
            for z in range(CHIP_Z):
                for x in range(CHIP_X):
                    pairs.append((place(y, c, z, x), place(*fn(y, c, z, x))))
    return pairs

CORE_SWAP = moves(lambda y, c, z, x: (y, 1 - c, z, x))
PLANE = (
    moves(lambda y, c, z, x: (y, c, z, 1 - x) if c == 0 else (1 - y, c, z, x)),
    moves(lambda y, c, z, x: (1 - y, c, z, x) if c == 0 else (y, c, z, 1 - x)),
)
X_SWAP = moves(lambda y, c, z, x: (y, c, z, 1 - x))
Y_SWAP = moves(lambda y, c, z, x: (1 - y, c, z, x))
Z_SHIFT = [moves(lambda y, c, z, x, k=k: (y, c, (z + k) % CHIP_Z, x)) for k in range(CHIP_Z)]

def send(v, pairs):
    return lax.ppermute(v, AXES, pairs)

def my_place():
    dp = lax.axis_index("dp"); fs = lax.axis_index("fsdp")
    return dp // CORES, dp % CORES, fs // CHIP_X, fs % CHIP_X

def half_of(v, which):
    h = v.shape[-1] // 2
    return lax.dynamic_slice_in_dim(v, which * h, h, axis=v.ndim - 1)

def no_sooner(arrays):
    zero = jnp.zeros((), B16)
    for v in arrays:
        zero = zero + jnp.minimum(jnp.abs(v.reshape(-1)[0]), 0)
    return zero


class Gathering:
    def __init__(self, mats):
        self.mats = mats
        _, c, _, _ = my_place()

        def pick(which):
            return jnp.concatenate(
                [half_of(m, which)[i] for m in mats for i in range(m.shape[0])], axis=-1
            )

        self.piece = jnp.stack([pick(c), send(pick(1 - c), CORE_SWAP)])

    def along(self, behind=()):
        piece = self.piece + no_sooner(behind) if behind else self.piece
        self.moved = [send(piece, Z_SHIFT[k]) for k in range(1, CHIP_Z)]
        return self.moved

    def plane(self):
        base = jnp.stack([self.piece] + self.moved)
        first = send(base, PLANE[0])
        self.own = [base, first, send(base, PLANE[1]), send(first, PLANE[1])]
        self.other = [send(v, CORE_SWAP) for v in self.own]

    def finish(self, after=()):
        return assemble(self.own, self.other, self.mats, after)


def assemble_kernel(counts, widths, pos_ref, *refs):
    src = refs[:8]; outs = refs[-1 - len(counts):-1]; sem = refs[-1]
    y, c, z, x = (pos_ref[i] for i in range(4))
    copies = []
    for side in range(2):
        core = c if side == 0 else 1 - c
        for a in range(4):
            for e in range(4):
                f1, f2 = a & 1, a >> 1
                fx = jnp.where(core == 0, f1, f2)
                fy = jnp.where(core == 0, f2, f1)
                yy = (y + fy) % 2
                xx = (x + fx) % 2
                zz = (z + CHIP_Z - e) % CHIP_Z
                for dc in range(2):
                    cc = core if dc == 0 else 1 - core
                    d = place(yy, cc, zz, xx)
                    col = 0
                    for out, count, w in zip(outs, counts, widths):
                        for k in range(count):
                            cp = pltpu.make_async_copy(
                                src[side * 4 + a].at[e, dc, :, pl.ds(col, w)],
                                out.at[d, k, :, pl.ds(pl.multiple_of(core * w, 128), w)],
                                sem,
                            )
                            cp.start(); copies.append(cp)
                            col += w
    for cp in copies:
        cp.wait()

def assemble(own, other, mats, after=()):
    rows = mats[0].shape[1]
    counts = [m.shape[0] for m in mats]; widths = [m.shape[2] // 2 for m in mats]
    pos = jnp.stack([p.astype(jnp.int32) for p in my_place()])
    return pl.pallas_call(
        functools.partial(assemble_kernel, counts, widths),
        out_shape=[jax.ShapeDtypeStruct((FAST_SHARDS, n, rows, 2 * w), B16) for n, w in zip(counts, widths)],
        in_specs=[pl.BlockSpec(memory_space=pltpu.SMEM)] + [ANY] * (8 + len(after)),
        out_specs=[pl.BlockSpec(memory_space=pltpu.VMEM)] * len(counts),
        scratch_shapes=[pltpu.SemaphoreType.DMA],
        compiler_params=params(),
        cost_estimate=cost(7),
        name="assemble",
    )(pos, *own, *other, *after)


def sum_plane(v):
    for pairs in (CORE_SWAP, X_SWAP, Y_SWAP):
        v = v + send(v, pairs)
    return v


def sum_everywhere(v):
    v = sum_plane(v)
    parts = [send(v, Z_SHIFT[k]) for k in range(1, CHIP_Z)]
    return v + parts[0] + parts[1] + parts[2]


class Reduction:
    def __init__(self, theirs, mine):
        self.theirs = theirs
        self.own = mine
        self.y, self.c, self.z, self.x = my_place()
        self.split = (CHIP_Y, CORES, CHIP_Z, CHIP_X, mine.shape[0] // FAST_SHARDS)

    def swap(self):
        self.got = send(self.theirs, CORE_SWAP)
        return [self.got]

    def part(self, f1, f2):
        c = self.c
        fx = jnp.where(c == 0, f1, f2)
        fy = jnp.where(c == 0, f2, f1)

        def cut(v):
            v = v.reshape(self.split + (v.shape[-1],))
            at = ((self.y + fy) % CHIP_Y, 0, 0, (self.x + fx) % CHIP_X, 0, 0)
            size = (1, CORES, CHIP_Z, 1) + v.shape[4:]
            return lax.dynamic_slice(v, at, size)[0, :, :, 0].astype(F32)

        return cut(self.own) + cut(self.got)

    def far(self):
        self.r3 = send(self.part(1, 1).astype(B16), PLANE[1])
        self.r2 = send(self.part(0, 1).astype(B16), PLANE[1])
        return [self.r3, self.r2]

    def near(self):
        self.r1 = send((self.part(1, 0) + self.r3.astype(F32)).astype(B16), PLANE[0])
        return [self.r1]

    def along(self):
        base = self.part(0, 0) + self.r2.astype(F32) + self.r1.astype(F32)

        def at_z(k):
            return lax.dynamic_slice_in_dim(base, (self.z + k) % CHIP_Z, 1, axis=1)[:, 0]

        self.mine = at_z(0)
        self.rz = [send(at_z(k).astype(B16), Z_SHIFT[k]) for k in range(1, CHIP_Z)]
        return self.rz

    def finish(self):
        total = self.mine
        for r in self.rz:
            total = total + r.astype(F32)
        c = self.c
        keep = lax.dynamic_slice_in_dim(total, c, 1, axis=0)[0]
        give = lax.dynamic_slice_in_dim(total, 1 - c, 1, axis=0)[0]
        other = send(give, CORE_SWAP)
        first = jnp.where(c == 0, keep, other)
        second = jnp.where(c == 0, other, keep)
        return first, second


def unpack_kernel(first, src_ref, *refs):
    out_ref, sem = refs[-2:]
    shards, ratio, _, width = out_ref.shape
    copies = []
    for d in range(shards):
        for k in range(ratio):
            copy = pltpu.make_async_copy(
                src_ref.at[d, :, pl.ds(first + k * width, width)], out_ref.at[d, k], sem
            )
            copy.start()
            copies.append(copy)
    for copy in copies:
        copy.wait()


def unpack_two(packed, first, ratio, width, after=()):
    shards, rows, _ = packed.shape
    return pl.pallas_call(
        functools.partial(unpack_kernel, first),
        out_shape=jax.ShapeDtypeStruct((shards, ratio, rows, width), B16),
        in_specs=[ANY] * (1 + len(after)),
        out_specs=pl.BlockSpec(memory_space=pltpu.VMEM),
        scratch_shapes=[pltpu.SemaphoreType.DMA],
        compiler_params=params(),
        cost_estimate=cost(5),
        name="unpack",
    )(packed, *after)


def per_device(
    shards, fast,
    tokens, masked_rows, cotangent, norm1_gain, norm1_bias, qkv_weight, q_bias, v_bias,
    proj_weight, proj_bias, gamma_attn, norm2_gain, norm2_bias, fc1_weight, fc1_bias,
    fc2_weight, fc2_bias, gamma_mlp, rel_table,
):
    vectors = (norm1_gain, norm1_bias, q_bias, v_bias, proj_bias, gamma_attn, norm2_gain,
               norm2_bias, fc2_bias, gamma_mlp)
    width = tokens.shape[1]
    images = masked_rows.shape[0]
    heads, entries = rel_table.shape[1:]
    own = qkv_weight.shape[1]
    ratio = fc2_weight.shape[1] // own
    hidden = fc1_weight.shape[2]
    me = lax.axis_index("dp") * lax.axis_size("fsdp") + lax.axis_index("fsdp")

    def pad_rows(v):
        v = v.astype(F32).reshape(images, IMG_ROWS, width)
        v = jnp.pad(v, ((0, 0), (0, PAD_ROWS - IMG_ROWS), (0, 0)))
        return v.reshape(images * PAD_ROWS, width)

    def cut_rows(v):
        return v.reshape(images, PAD_ROWS, width)[:, :IMG_ROWS].reshape(images * IMG_ROWS, width)

    def everywhere(v):
        return sum_everywhere(v) if fast else lax.psum(v, AXES)

    def placed(shard, total):
        empty = jnp.zeros(shard.shape[:-1] + (total,), shard.dtype)
        at = (0,) * (shard.ndim - 1) + (me * shard.shape[-1],)
        return lax.dynamic_update_slice(empty, shard, at)

    small = jnp.concatenate(
        [
            placed(jnp.stack(vectors, axis=1), width),
            placed(fc1_bias, hidden).reshape(LAYERS, ratio, width),
            placed(rel_table, TILE),
        ],
        axis=1,
    )
    used = small.shape[1]
    small = everywhere(small.reshape(LAYERS * used, width)).reshape(LAYERS, used, width)
    small = jnp.pad(small.astype(F32), ((0, 0), (0, SMALL_ROWS - used), (0, 0)))
    bias = build_bias(small, heads)

    def two_blocks(layer):
        return fc2_weight[layer].reshape(ratio, own, width)

    def fetch_packed(layer):
        two = two_blocks(layer)
        block = jnp.concatenate(
            [qkv_weight[layer], proj_weight[layer], fc1_weight[layer]]
            + [two[i] for i in range(ratio)],
            axis=1,
        )
        return lax.all_gather(block, AXES, axis=0, tiled=True)

    packed_weights = [None if fast and layer == 0 else fetch_packed(layer) for layer in range(LAYERS)]
    if fast:
        first = Gathering([qkv_weight[0][None], proj_weight[0][None]])
        second = Gathering([fc1_weight[0][None], two_blocks(0)])
        second.along(first.along())
        first.plane()
        second.plane()
    weights = []
    x = pad_rows(tokens)
    saved = []
    for layer in range(LAYERS):
        full = packed_weights[layer]
        if full is None:
            w_qkv, w_proj = first.finish([bias])
            w_qkv = (w_qkv.reshape(width, 3 * width), 0)
            w_proj = (w_proj.reshape(width, width), 0)
        else:
            w_qkv, w_proj, w_one = (full, 0), (full, 3), (full, 4)
        qkv, h = qkv_forward(x, small, layer, w_qkv)
        qkv = qkv.reshape(images, PAD_ROWS, 3 * width)
        att, lse = attention_forward(qkv, bias, layer)
        att = att.reshape(images * PAD_ROWS, width)
        if full is None:
            w_one, w_two = second.finish([att])
            w_one = (w_one.reshape(width, hidden), 0)
        elif fast:
            w_two = unpack_two(full.reshape(shards, own, -1), 4 * width + hidden, ratio, width)
        else:
            w_two = full[:, 4 * width + hidden :].reshape(shards, own, ratio, width)
            w_two = w_two.transpose(0, 2, 1, 3)
        w_two = w_two.reshape(hidden, width)
        weights.append((w_qkv, w_proj, w_one, w_two))
        out, branch, mid, mlp_out, h2, act, slope = mlp_forward(
            x, att, small, layer, w_proj, w_one, w_two
        )
        saved.append((x, h, qkv, lse, att, branch, mid, mlp_out, h2, act, slope))
        x = out
    encoded = cut_rows(x.astype(B16))

    positions = jnp.arange(IMG_ROWS, dtype=jnp.int32)
    mask = jnp.any(masked_rows[:, :, None] == positions[None, None, :], axis=1)
    mask = jnp.pad(mask, ((0, 0), (0, PAD_ROWS - IMG_ROWS))).reshape(-1, 1)
    grad = jnp.where(mask, pad_rows(cotangent), 0.0)

    def scatter(theirs, mine):
        both = jnp.stack([mine, theirs])
        own_part = lax.psum_scatter(both, AXES, scatter_dimension=1, tiled=True).astype(F32)
        return own_part[0], own_part[1]

    core = (lax.axis_index("dp") % CORES if fast else jnp.int32(0)).astype(jnp.int32).reshape(1)
    reduced = [None] * LAYERS
    small_grads = [None] * LAYERS
    tables = [None] * LAYERS

    def backward(layer, grad, hooks):
        x, h, qkv, lse, att, branch, mid, mlp_out, h2, act, slope = saved[layer]
        w_qkv, w_proj, w_one, w_two = weights[layer]
        theirs, mine, d_mid, d_att, mlp_sums = mlp_backward(
            core, grad, mid, mlp_out, branch, att, small, layer, h2, act, slope, w_proj, w_one,
            w_two, hooks[0](),
        )
        main = (theirs, mine)
        d_qkv, d_bias = attention_backward(
            qkv, bias, lse, d_att.reshape(images, PAD_ROWS, width), layer, hooks[1](main)
        )
        theirs, mine, grad, qkv_sums = qkv_backward(
            core, d_qkv.reshape(images * PAD_ROWS, 3 * width), h, x, d_mid, small, layer, w_qkv,
            hooks[2](),
        )
        small_grads[layer] = (qkv_sums, mlp_sums)
        tables[layer] = d_bias
        return grad, main, (theirs, mine)

    if not fast:
        for layer in reversed(range(LAYERS)):
            none = (lambda: (), lambda main: (), lambda: ())
            grad, main, rest = backward(layer, grad, none)
            reduced[layer] = (scatter(*main), scatter(*rest))
        tables = [reduce_bias(t) for t in tables]
    else:
        a1, b1, a0, b0 = (None,) * 4

        def one_attention(main):
            nonlocal a1
            a1 = Reduction(*main)
            return ()

        def one_qkv():
            return a1.swap()

        grad, _, rest = backward(1, grad, (lambda: (), one_attention, one_qkv))
        b1 = Reduction(*rest)
        a1.far()

        def zero_mlp():
            return ()

        def zero_attention(main):
            nonlocal a0
            a0 = Reduction(*main)
            b1.swap()
            return [a1.r3, a1.r2, b1.got]

        def zero_qkv():
            return a1.near() + b1.far() + a0.swap()

        grad, _, rest = backward(0, grad, (zero_mlp, zero_attention, zero_qkv))
        b0 = Reduction(*rest)
        a0.far()
        a1.along()
        b1.near()
        b0.swap()
        tables[1] = reduce_bias(tables[1])
        b0.far()
        a0.near()
        b1.along()
        tables[0] = reduce_bias(tables[0])
        a0.along()
        b0.near()
        b0.along()
        reduced[1] = (a1.finish(), b1.finish())
        reduced[0] = (a0.finish(), b0.finish())

    rows = []
    for (qkv_sums, mlp_sums), table in zip(small_grads, tables):
        rows += [qkv_sums[:4], mlp_sums[: TABLE - B_PROJ], table]
    totals = jnp.concatenate(rows, axis=0)
    totals = sum_plane(totals) if fast else lax.psum(totals, AXES)
    totals = totals.reshape(LAYERS, used, width)

    def owned_by(device):
        def cut(v, size):
            return lax.dynamic_slice_in_dim(v, device * size, size, axis=v.ndim - 1)

        g_vec = cut(totals[:, :B_ONE], own).reshape(LAYERS, -1)
        g_b1 = cut(totals[:, B_ONE:TABLE].reshape(LAYERS, hidden), ratio * own)
        g_tab = cut(totals[:, TABLE:], entries).reshape(LAYERS, -1)
        return jnp.concatenate([g_vec, g_b1, g_tab], axis=1)

    g_small = owned_by(me)
    if fast:
        per_z = CHIP_X
        ring = CHIP_Z * CHIP_X
        for k in range(1, CHIP_Z):
            device = (me // ring) * ring + (me + k * per_z) % ring
            g_small = g_small + send(owned_by(device), Z_SHIFT[k])
    g = g_small[:, : B_ONE * own].reshape(LAYERS, B_ONE, own)
    g = [g[:, i] for i in range(B_ONE)]
    g_b1 = g_small[:, B_ONE * own : (B_ONE + ratio) * own]
    g_table = g_small[:, (B_ONE + ratio) * own :].reshape(LAYERS, heads, entries)

    def both(pick):
        return jnp.stack([pick(*r) for r in reduced])

    def thirds(low, high):
        half = width // 2
        cols = [v[:, i * half : (i + 1) * half] for i in range(3) for v in (low, high)]
        return jnp.concatenate(cols, axis=1)

    def join(low, high, first, last):
        return jnp.concatenate([low[:, first:last], high[:, first:last]], axis=1)

    half = hidden // 2
    g_qkv = both(lambda a, b: thirds(*b))
    g_one = both(lambda a, b: join(*a, 0, half))
    g_two = both(lambda a, b: join(*a, half, hidden).reshape(ratio * own, width))
    g_proj = both(lambda a, b: join(*a, hidden, hidden + width // 2))
    return (encoded, cut_rows(grad), g[N1_GAIN], g[N1_SHIFT], g_qkv, g[Q_BIAS], g[V_BIAS], g_proj,
            g[B_PROJ], g[G_ATTN], g[N2_GAIN], g[N2_SHIFT], g_one, g_b1, g_two, g[B_TWO], g[G_MLP],
            g_table)


def solution(mesh):
    shards = math.prod(mesh.shape[a] for a in AXES)
    fast = mesh.shape["dp"] == CHIP_Y * CORES and mesh.shape["fsdp"] == CHIP_Z * CHIP_X
    row = P(AXES, None)
    vec = P(None, AXES)
    mat = P(None, AXES, None)
    tab = P(None, None, AXES)
    return jax.shard_map(
        functools.partial(per_device, shards, fast),
        mesh=mesh,
        in_specs=(row, row, row, vec, vec, mat, vec, vec, mat, vec, vec, vec, vec, mat, vec, mat,
                  vec, vec, tab),
        out_specs=(row, row, vec, vec, mat, vec, vec, mat, vec, vec, vec, vec, mat, vec, mat,
                   vec, vec, tab),
        check_vma=False,
    )
```

```python
import functools
import math

import jax
import jax.numpy as jnp
import numpy as np
from jax import lax
from jax.experimental import pallas as pl
from jax.experimental.pallas import tpu as pltpu
from jax.sharding import PartitionSpec as P

GRID = 14
SPAN = 2 * GRID - 1
LAYERS = 2
IMG_ROWS = GRID * GRID + 1
PAD_ROWS = 208
LANES = 256
HEAD = 64
PAIR = 2 * HEAD
NEG = -1e30
TILE = 768
WIDE = 384
GROUP = 4
BLOCK = 16
SMALL_ROWS = 32
F32 = jnp.float32
B16 = jnp.bfloat16
AXES = ("dp", "fsdp")


def cost(us):
    return pl.CostEstimate(flops=us * 4_400_000_000, bytes_accessed=us * 14_000_000, transcendentals=0)


ANY = pl.BlockSpec(memory_space=pl.ANY)
SMEM = pl.BlockSpec(memory_space=pltpu.SMEM)

N1_GAIN, N1_SHIFT, Q_BIAS, V_BIAS, B_PROJ, G_ATTN, N2_GAIN, N2_SHIFT, B_TWO, G_MLP = range(10)
B_ONE = 10
TABLE = 14


def params(limit=56):
    return pltpu.CompilerParams(vmem_limit_bytes=limit * 1024 * 1024)


def dot(a, b, dims):
    return lax.dot_general(a, b, (dims, ((), ())), preferred_element_type=F32)


NN = ((1,), (0,))
NT = ((1,), (1,))
TN = ((0,), (0,))


def lane_onehot():
    out = np.zeros((WIDE, LANES), np.float32)
    for a in range(GRID):
        for b in range(GRID):
            out[SPAN * a + b, 1 + GRID * a + b] = 1.0
    return out


def row_onehot(turned):
    out = np.zeros((PAD_ROWS, BLOCK * GRID), np.float32)
    for c in range(GRID):
        for d in range(GRID):
            out[1 + GRID * c + d, BLOCK * c + (GRID - 1 - d if turned else d)] = 1.0
    return out


def bias_kernel(heads, small_ref, rows_ref, lanes_ref, *refs):
    out_ref, wide_ref = refs[-2:]
    first = lax.rem(pl.program_id(0) * GROUP, heads)
    for i in range(GROUP):
        table = small_ref[0, pl.ds(TABLE + first + i, 1), :]
        one_bias(table, rows_ref, lanes_ref, out_ref.at[i], wide_ref.at[i])


def one_bias(table, rows_ref, lanes_ref, out_ref, wide_ref):
    shifted = pltpu.roll(jnp.broadcast_to(table, (BLOCK, TILE)), TILE - (GRID - 1), 1)
    shifted = pltpu.roll(shifted, 0, 1, stride=1, stride_axis=0)
    for c in range(GRID):
        start = SPAN * (GRID - 1 - c)
        wide_ref[BLOCK * c : BLOCK * (c + 1), :] = shifted[:, start : start + WIDE].astype(B16)
    narrow = dot(wide_ref[...], lanes_ref[...], NN).astype(B16)
    val = dot(rows_ref[...], narrow, NN)
    row = lax.broadcasted_iota(jnp.int32, (PAD_ROWS, LANES), 0)
    lane = lax.broadcasted_iota(jnp.int32, (PAD_ROWS, LANES), 1)
    cls = SPAN * SPAN
    val = jnp.where(lane == 0, table[:, cls : cls + 1], val)
    first = jnp.where(lane == 0, table[:, cls + 2 : cls + 3], table[:, cls + 1 : cls + 2])
    val = jnp.where(row == 0, first, val)
    out_ref[...] = jnp.where(row >= IMG_ROWS, NEG, val)


def build_bias(small, heads, after=()):
    layers = small.shape[0]
    return pl.pallas_call(
        functools.partial(bias_kernel, heads),
        grid=(layers * heads // GROUP,),
        out_shape=jax.ShapeDtypeStruct((layers * heads, PAD_ROWS, LANES), F32),
        in_specs=[
            pl.BlockSpec((1, SMALL_ROWS, TILE), lambda h: (h * GROUP // heads, 0, 0)),
            pl.BlockSpec((PAD_ROWS, BLOCK * GRID), lambda h: (0, 0)),
            pl.BlockSpec((WIDE, LANES), lambda h: (0, 0)),
        ]
        + [ANY] * len(after),
        out_specs=pl.BlockSpec((GROUP, PAD_ROWS, LANES), lambda h: (h, 0, 0)),
        scratch_shapes=[pltpu.VMEM((GROUP, BLOCK * GRID, WIDE), B16)],
        compiler_params=params(),
        cost_estimate=cost(10),
        name="bias_expand",
    )(small, jnp.asarray(row_onehot(False), B16), jnp.asarray(lane_onehot(), B16), *after)


def bias_grad_kernel(g_ref, rows_ref, lanes_ref, *refs):
    out_ref, acc_ref = refs[-2:]
    for i in range(GROUP):
        one_bias_grad(g_ref.at[i], rows_ref, lanes_ref, out_ref.at[i], acc_ref.at[i])


def one_bias_grad(g_ref, rows_ref, lanes_ref, out_ref, acc_ref):
    row = lax.broadcasted_iota(jnp.int32, (PAD_ROWS, LANES), 0)
    lane = lax.broadcasted_iota(jnp.int32, (PAD_ROWS, LANES), 1)
    g = jnp.where((lane < IMG_ROWS) & (row < IMG_ROWS), g_ref[...], 0.0)
    high = g.astype(B16)
    wide = None
    for part in (high, (g - high.astype(F32)).astype(B16)):
        moved = dot(rows_ref[...], part, NN).astype(B16)
        moved = dot(moved, lanes_ref[...], NN)
        wide = moved if wide is None else wide + moved
    acc_ref[...] = jnp.zeros_like(acc_ref)
    for c in range(GRID):
        start = SPAN * (GRID - 1 - c)
        acc_ref[:, start : start + WIDE] += wide[BLOCK * c : BLOCK * (c + 1), :]
    turned = pltpu.roll(acc_ref[...], 0, 1, stride=1, stride_axis=0)
    total = jnp.sum(turned, axis=0, keepdims=True)
    column = jnp.sum(jnp.where(lane[:, :1] == 0, g[:, :1], 0.0), axis=0, keepdims=True)
    to_self = g[0:1, 0:1]
    to_patch = column - to_self
    from_patch = jnp.sum(g[0:1, :], axis=1, keepdims=True) - to_self
    spot = lax.broadcasted_iota(jnp.int32, (1, TILE), 1)
    cls = SPAN * SPAN
    total = jnp.where(spot == cls, to_patch, total)
    total = jnp.where(spot == cls + 1, from_patch, total)
    out_ref[...] = jnp.where(spot == cls + 2, to_self, total)


def reduce_bias(grad, after=()):
    heads = grad.shape[0]
    out = pl.pallas_call(
        bias_grad_kernel,
        grid=(heads // GROUP,),
        out_shape=jax.ShapeDtypeStruct((heads, 1, TILE), F32),
        in_specs=[
            pl.BlockSpec((GROUP, PAD_ROWS, LANES), lambda h: (h, 0, 0)),
            pl.BlockSpec((BLOCK * GRID, PAD_ROWS), lambda h: (0, 0)),
            pl.BlockSpec((LANES, WIDE), lambda h: (0, 0)),
        ]
        + [ANY] * len(after),
        out_specs=pl.BlockSpec((GROUP, 1, TILE), lambda h: (h, 0, 0)),
        scratch_shapes=[pltpu.VMEM((GROUP, BLOCK, TILE), F32)],
        compiler_params=params(),
        cost_estimate=cost(6),
        name="bias_reduce",
    )(grad, jnp.asarray(row_onehot(True).T, B16), jnp.asarray(lane_onehot().T, B16), *after)
    return out


def head_mask(which):
    lane = lax.broadcasted_iota(jnp.int32, (PAD_ROWS, PAIR), 1)
    return (lane < HEAD) if which == 0 else (lane >= HEAD)


def attention_kernel(width, qkv_ref, bias_ref, out_ref, lse_ref):
    heads = width // HEAD
    for pair in range(heads // 2):
        at = pair * PAIR
        q = qkv_ref[0, :, at : at + PAIR]
        k = qkv_ref[0, :, width + at : width + at + PAIR]
        v = qkv_ref[0, :, 2 * width + at : 2 * width + at + PAIR]
        q = q * jnp.asarray(HEAD ** (-0.5), B16)
        v_t = v.T
        parts = []
        for t in range(2):
            head = 2 * pair + t
            q_t = jnp.where(head_mask(t), q, jnp.zeros_like(q))
            scores = dot(k, q_t, NT) + bias_ref[head, :, 0:PAD_ROWS]
            top = jnp.max(scores, axis=0, keepdims=True)
            weights = jnp.exp(scores - top)
            total = jnp.sum(weights, axis=0, keepdims=True)
            probs = (weights * (1.0 / total)).astype(B16)
            lse_ref[0, head : head + 1, 0:PAD_ROWS] = top + jnp.log(total)
            parts.append(dot(v_t[t * HEAD : (t + 1) * HEAD], probs, NN))
        out_ref[0, :, at : at + PAIR] = jnp.concatenate(parts, axis=0).T.astype(B16)


def attention_forward(qkv, bias, layer):
    images = qkv.shape[0]
    width = qkv.shape[2] // 3
    heads = width // HEAD
    return pl.pallas_call(
        functools.partial(attention_kernel, width),
        grid=(images,),
        out_shape=(
            jax.ShapeDtypeStruct((images, PAD_ROWS, width), B16),
            jax.ShapeDtypeStruct((images, 16, LANES), F32),
        ),
        in_specs=[
            pl.BlockSpec((1, PAD_ROWS, 3 * width), lambda i: (i, 0, 0)),
            pl.BlockSpec((heads, PAD_ROWS, LANES), lambda i: (layer, 0, 0)),
        ],
        out_specs=(
            pl.BlockSpec((1, PAD_ROWS, width), lambda i: (i, 0, 0)),
            pl.BlockSpec((1, 16, LANES), lambda i: (i, 0, 0)),
        ),
        compiler_params=params(),
        cost_estimate=cost(8),
        name="attention",
    )(qkv, bias)


def attention_grad_kernel(width, qkv_ref, bias_ref, lse_ref, g_ref, *refs):
    out_ref, dbias_ref = refs[-2:]
    heads = width // HEAD
    scale = HEAD ** (-0.5)

    @pl.when(pl.program_id(0) == 0)
    def _():
        dbias_ref[...] = jnp.zeros_like(dbias_ref)

    for pair in range(heads // 2):
        at = pair * PAIR
        q = qkv_ref[0, :, at : at + PAIR]
        k = qkv_ref[0, :, width + at : width + at + PAIR]
        v = qkv_ref[0, :, 2 * width + at : 2 * width + at + PAIR]
        g = g_ref[0, :, at : at + PAIR]
        q = q * jnp.asarray(scale, B16)
        k_t = k.T
        dq_parts = []
        dk = None
        dv = None
        for t in range(2):
            head = 2 * pair + t
            q_t = jnp.where(head_mask(t), q, jnp.zeros_like(q))
            g_t = jnp.where(head_mask(t), g, jnp.zeros_like(g))
            scores = dot(k, q_t, NT) + bias_ref[head, :, 0:PAD_ROWS]
            probs = jnp.exp(scores - lse_ref[0, head : head + 1, 0:PAD_ROWS])
            dprobs = dot(v, g_t, NT)
            dv_t = dot(probs.astype(B16), g_t, NN)
            mean = jnp.sum(probs * dprobs, axis=0, keepdims=True)
            dscores = (probs * (dprobs - mean)).astype(B16)
            dbias_ref[head, :, 0:PAD_ROWS] += dscores.astype(F32)
            dk_t = dot(dscores, q_t, NN)
            dq_parts.append(dot(k_t[t * HEAD : (t + 1) * HEAD], dscores, NN))
            dk = dk_t if dk is None else dk + dk_t
            dv = dv_t if dv is None else dv + dv_t
        dq = jnp.concatenate(dq_parts, axis=0).T * scale
        out_ref[0, :, at : at + PAIR] = dq.astype(B16)
        out_ref[0, :, width + at : width + at + PAIR] = dk.astype(B16)
        out_ref[0, :, 2 * width + at : 2 * width + at + PAIR] = dv.astype(B16)


def attention_backward(qkv, bias, lse, grad, layer, after=()):
    images = qkv.shape[0]
    width = qkv.shape[2] // 3
    heads = width // HEAD
    return pl.pallas_call(
        functools.partial(attention_grad_kernel, width),
        grid=(images,),
        out_shape=(
            jax.ShapeDtypeStruct((images, PAD_ROWS, 3 * width), B16),
            jax.ShapeDtypeStruct((heads, PAD_ROWS, LANES), F32),
        ),
        in_specs=[
            pl.BlockSpec((1, PAD_ROWS, 3 * width), lambda i: (i, 0, 0)),
            pl.BlockSpec((heads, PAD_ROWS, LANES), lambda i: (layer, 0, 0)),
            pl.BlockSpec((1, 16, LANES), lambda i: (i, 0, 0)),
            pl.BlockSpec((1, PAD_ROWS, width), lambda i: (i, 0, 0)),
        ]
        + [ANY] * len(after),
        out_specs=(
            pl.BlockSpec((1, PAD_ROWS, 3 * width), lambda i: (i, 0, 0)),
            pl.BlockSpec((heads, PAD_ROWS, LANES), lambda i: (0, 0, 0)),
        ),
        compiler_params=params(),
        cost_estimate=cost(12),
        name="attention_grad",
    )(qkv, bias, lse, grad, *after)


def normalize(x):
    centered = x - jnp.mean(x, -1, keepdims=True)
    scale = lax.rsqrt(jnp.mean(centered * centered, -1, keepdims=True) + 1e-06)
    return centered * scale, scale


def normalize_grad(x_hat, scale, dy):
    return scale * (
        dy - jnp.mean(dy, -1, keepdims=True) - x_hat * jnp.mean(dy * x_hat, -1, keepdims=True)
    )


def gelu_and_slope(x):
    t = 1.0 / (1.0 + (0.3275911 / math.sqrt(2.0)) * jnp.abs(x))
    bell = jnp.exp(-0.5 * x * x)
    poly = 0.5 * 1.061405429
    for coef in (-1.453152027, 1.421413741, -0.284496736, 0.254829592):
        poly = poly * t + 0.5 * coef
    tail = poly * t * bell
    phi = jnp.where(x >= 0, 1.0 - tail, tail)
    return x * phi, phi + x * bell * (1.0 / math.sqrt(2.0 * math.pi))


def total_rows(v):
    return jnp.sum(v, axis=0, keepdims=True)


def small_spec(layer):
    return pl.BlockSpec((1, SMALL_ROWS, TILE), lambda i: (layer, 0, 0))


def whole_spec(shape):
    return pl.BlockSpec(shape, lambda i: (0,) * len(shape))


def col_spec(weight):
    array, first = weight
    return pl.BlockSpec((array.shape[0], TILE), lambda i: (0, first + i))


def qkv_kernel(x_ref, small_ref, w_ref, qkv_ref, h_ref):
    step = pl.program_id(0)

    @pl.when(step == 0)
    def _():
        x_hat, _ = normalize(x_ref[...])
        gain = small_ref[0, N1_GAIN : N1_GAIN + 1]
        h_ref[...] = (x_hat * gain + small_ref[0, N1_SHIFT : N1_SHIFT + 1]).astype(B16)

    zero = jnp.zeros((1, TILE), F32)
    bias = jnp.where(step == 0, small_ref[0, Q_BIAS : Q_BIAS + 1], zero)
    bias = jnp.where(step == 2, small_ref[0, V_BIAS : V_BIAS + 1], bias)
    qkv_ref[...] = (dot(h_ref[...], w_ref[...], NN) + bias).astype(B16)


def qkv_forward(x, small, layer, w_qkv):
    rows, width = x.shape
    return pl.pallas_call(
        qkv_kernel,
        grid=(3,),
        out_shape=(
            jax.ShapeDtypeStruct((rows, 3 * width), B16),
            jax.ShapeDtypeStruct((rows, width), B16),
        ),
        in_specs=[whole_spec((rows, width)), small_spec(layer), col_spec(w_qkv)],
        out_specs=(
            pl.BlockSpec((rows, TILE), lambda i: (0, i)),
            whole_spec((rows, width)),
        ),
        compiler_params=params(),
        cost_estimate=cost(6),
        name="qkv",
    )(x, small, w_qkv[0])


def qkv_grad_kernel(core_ref, g_ref, h_ref, x_ref, dmid_ref, small_ref, w_ref, *refs):
    theirs_ref, mine_ref, dx_ref, sums_ref, ht_ref, dh_ref = refs[-6:]
    step = pl.program_id(0)

    @pl.when(step == 0)
    def _():
        ht_ref[...] = h_ref[...].T
        sums_ref[...] = jnp.zeros_like(sums_ref)

    g = g_ref[...]
    dw = dot(ht_ref[...], g, NN).astype(B16)
    low, high = dw[:, : TILE // 2], dw[:, TILE // 2 :]

    @pl.when(core_ref[0] == 0)
    def _():
        mine_ref[...] = low
        theirs_ref[...] = high

    @pl.when(core_ref[0] != 0)
    def _():
        mine_ref[...] = high
        theirs_ref[...] = low

    part = dot(g, w_ref[...], NT)
    total = total_rows(g.astype(F32))

    @pl.when(step == 0)
    def _():
        dh_ref[...] = part
        sums_ref[Q_BIAS : Q_BIAS + 1] = total

    @pl.when(step > 0)
    def _():
        dh_ref[...] += part

    @pl.when(step == 2)
    def _():
        sums_ref[V_BIAS : V_BIAS + 1] = total
        dh = dh_ref[...]
        x_hat, scale = normalize(x_ref[...])
        sums_ref[N1_GAIN : N1_GAIN + 1] = total_rows(dh * x_hat)
        sums_ref[N1_SHIFT : N1_SHIFT + 1] = total_rows(dh)
        gain = small_ref[0, N1_GAIN : N1_GAIN + 1]
        dx_ref[...] = dmid_ref[...] + normalize_grad(x_hat, scale, dh * gain)


def qkv_backward(core, grad, h, x, d_mid, small, layer, w_qkv, after=()):
    rows, width = x.shape
    whole = whole_spec((rows, width))
    tiles = pl.BlockSpec((rows, TILE), lambda i: (0, i))
    return pl.pallas_call(
        qkv_grad_kernel,
        grid=(3,),
        out_shape=(
            jax.ShapeDtypeStruct((width, 3 * width // 2), B16),
            jax.ShapeDtypeStruct((width, 3 * width // 2), B16),
            jax.ShapeDtypeStruct((rows, width), F32),
            jax.ShapeDtypeStruct((8, width), F32),
        ),
        in_specs=[SMEM, tiles, whole, whole, whole, small_spec(layer), col_spec(w_qkv)]
        + [ANY] * len(after),
        out_specs=(
            pl.BlockSpec((width, TILE // 2), lambda i: (0, i)),
            pl.BlockSpec((width, TILE // 2), lambda i: (0, i)),
            whole,
            whole_spec((8, width)),
        ),
        scratch_shapes=[pltpu.VMEM((width, rows), B16), pltpu.VMEM((rows, width), F32)],
        compiler_params=params(),
        cost_estimate=cost(11),
        name="qkv_grad",
    )(core, grad, h, x, d_mid, small, w_qkv[0], *after)


def mlp_kernel(
    x_ref, att_ref, small_ref, wp_ref, w1_ref, w2_ref,
    out_ref, branch_ref, mid_ref, mlp_ref, h2_ref, act_ref, slope_ref,
):
    step = pl.program_id(0)

    def vec(i):
        return small_ref[0, i : i + 1]

    @pl.when(step == 0)
    def _():
        branch = dot(att_ref[...], wp_ref[...], NN) + vec(B_PROJ)
        branch_ref[...] = branch
        mid = x_ref[...] + vec(G_ATTN) * branch
        mid_ref[...] = mid
        x_hat, _ = normalize(mid)
        h2_ref[...] = (x_hat * vec(N2_GAIN) + vec(N2_SHIFT)).astype(B16)

    pre = dot(h2_ref[...], w1_ref[...], NN) + small_ref[0, pl.ds(B_ONE + step, 1)]
    act, slope = gelu_and_slope(pre)
    act = act.astype(B16)
    act_ref[...] = act
    slope_ref[...] = slope.astype(B16)
    part = dot(act, w2_ref[...], NN)

    @pl.when(step == 0)
    def _():
        mlp_ref[...] = part + vec(B_TWO)

    @pl.when(step > 0)
    def _():
        mlp_ref[...] += part

    @pl.when(step == pl.num_programs(0) - 1)
    def _():
        out_ref[...] = mid_ref[...] + vec(G_MLP) * mlp_ref[...]


def mlp_forward(x, att, small, layer, w_proj, w_one, w_two):
    rows, width = x.shape
    hidden = w_two.shape[0]
    whole = whole_spec((rows, width))
    cols = pl.BlockSpec((rows, TILE), lambda i: (0, i))
    full = jax.ShapeDtypeStruct((rows, width), F32)
    proj_at = w_proj[1]
    return pl.pallas_call(
        mlp_kernel,
        grid=(hidden // TILE,),
        out_shape=(
            full, full, full, full,
            jax.ShapeDtypeStruct((rows, width), B16),
            jax.ShapeDtypeStruct((rows, hidden), B16),
            jax.ShapeDtypeStruct((rows, hidden), B16),
        ),
        in_specs=[
            whole,
            whole,
            small_spec(layer),
            pl.BlockSpec((width, TILE), lambda i: (0, proj_at)),
            col_spec(w_one),
            pl.BlockSpec((TILE, width), lambda i: (i, 0)),
        ],
        out_specs=(whole, whole, whole, whole, whole, cols, cols),
        compiler_params=params(),
        cost_estimate=cost(15),
        name="mlp",
    )(x, att, small, w_proj[0], w_one[0], w_two)


SUM_ROWS = 16
STRIP = 128


def mlp_grad_kernel(
    core_ref, g_ref, mid_ref, mlp_ref, branch_ref, att_ref, small_ref, h2_ref, act_ref, slope_ref, wp_ref,
    w1_ref, w2_ref, *refs,
):
    (theirs_ref, mine_ref, dmid_ref, datt_ref, sums_ref,
     dmlp_ref, h2t_ref, dh2_ref, one_ref, wide_ref, two_ref, proj_ref, sems) = refs[-13:]
    step = pl.program_id(0)
    steps = pl.num_programs(0)
    slot = lax.rem(step, 2)
    width = mid_ref.shape[1]
    hidden = 4 * width
    part_rows = TILE // 4

    def vec(i):
        return small_ref[0, i : i + 1]

    def put(row, value):
        at = row - B_PROJ
        sums_ref[at : at + 1] = value

    def copy_one(out_ref, j, s):
        return pltpu.make_async_copy(
            one_ref.at[s],
            out_ref.at[:, pl.ds(pl.multiple_of(lax.rem(j, 2) * TILE, TILE), TILE)],
            sems.at[0, s],
        )

    def copy_two(out_ref, j, s, which):
        return pltpu.make_async_copy(
            two_ref.at[s, which],
            out_ref.at[pl.ds(pl.multiple_of(j * part_rows, part_rows), part_rows),
                       pl.ds(2 * width, 2 * width)],
            sems.at[1 + which, s],
        )

    def proj_copy(out_ref, which):
        return pltpu.make_async_copy(
            proj_ref.at[which], out_ref.at[:, pl.ds(4 * width, width // 2)], sems.at[3, which]
        )

    def on_halves(run):
        for core in range(2):

            @pl.when(core_ref[0] == core)
            def _(core=core):
                run(mine_ref, core)
                run(theirs_ref, 1 - core)

    def send_one(j, s):
        def run(out_ref, which):
            @pl.when(j // 2 == which)
            def _():
                copy_one(out_ref, j, s).start()

        on_halves(run)

    def send_two(j, s):
        on_halves(lambda out_ref, which: copy_two(out_ref, j, s, which).start())

    def wait_step(j, s):
        copy_one(mine_ref, j, s).wait()
        for which in range(2):
            copy_two(mine_ref, j, s, which).wait()

    @pl.when(step == 0)
    def _():
        g = g_ref[...]
        dmlp = (g * vec(G_MLP)).astype(B16)
        dmlp_ref[...] = dmlp
        h2t_ref[...] = h2_ref[...].T
        sums_ref[...] = jnp.zeros_like(sums_ref)
        put(G_MLP, total_rows(g * mlp_ref[...]))
        put(B_TWO, total_rows(dmlp.astype(F32)))

    @pl.when(step >= 2)
    def _():
        wait_step(step - 2, slot)

    dmlp = dmlp_ref[...]
    dact = dot(dmlp, w2_ref[...], NT)
    dpre = (dact * slope_ref[...].astype(F32)).astype(B16)
    wide = dot(act_ref[...].T, dmlp, NN)
    for t in range(wide_ref.shape[0]):
        wide_ref[t] = wide[:, t * STRIP : (t + 1) * STRIP]
        for k in range(4):
            at = (k % 2) * width + t * STRIP
            two_ref[slot, k // 2, :, at : at + STRIP] = wide_ref[
                t, pl.ds(k, part_rows, stride=4), :
            ].astype(B16)
    send_two(step, slot)
    one_ref[slot] = dot(h2t_ref[...], dpre, NN).astype(B16)
    send_one(step, slot)
    sums_ref[pl.ds(B_ONE - B_PROJ + step, 1)] = total_rows(dpre.astype(F32))
    part = dot(dpre, w1_ref[...], NT)

    @pl.when(step == 0)
    def _():
        dh2_ref[...] = part

    @pl.when(step > 0)
    def _():
        dh2_ref[...] += part

    @pl.when(step == steps - 1)
    def _():
        x_hat, scale = normalize(mid_ref[...])
        dh2 = dh2_ref[...]
        put(N2_GAIN, total_rows(dh2 * x_hat))
        put(N2_SHIFT, total_rows(dh2))
        dmid = g_ref[...] + normalize_grad(x_hat, scale, dh2 * vec(N2_GAIN))
        dmid_ref[...] = dmid
        dbranch = (dmid * vec(G_ATTN)).astype(B16)
        put(G_ATTN, total_rows(dmid * branch_ref[...]))
        put(B_PROJ, total_rows(dbranch.astype(F32)))
        dproj = dot(att_ref[...].T, dbranch, NN).astype(B16)
        proj_ref[0] = dproj[:, : width // 2]
        proj_ref[1] = dproj[:, width // 2 :]
        on_halves(lambda out_ref, which: proj_copy(out_ref, which).start())
        datt_ref[...] = dot(dbranch, wp_ref[...], NT).astype(B16)
        wait_step(step - 1, 1 - slot)
        wait_step(step, slot)
        for which in range(2):
            proj_copy(mine_ref, which).wait()


def mlp_backward(core, grad, mid, mlp_out, branch, att, small, layer, h2, act, slope, w_proj, w_one,
                 w_two, after=()):
    rows, width = mid.shape
    hidden = w_two.shape[0]
    whole = whole_spec((rows, width))
    cols = pl.BlockSpec((rows, TILE), lambda i: (0, i))
    proj_at = w_proj[1]
    return pl.pallas_call(
        mlp_grad_kernel,
        grid=(hidden // TILE,),
        out_shape=(
            jax.ShapeDtypeStruct((width, hidden + width // 2), B16),
            jax.ShapeDtypeStruct((width, hidden + width // 2), B16),
            jax.ShapeDtypeStruct((rows, width), F32),
            jax.ShapeDtypeStruct((rows, width), B16),
            jax.ShapeDtypeStruct((SUM_ROWS, width), F32),
        ),
        in_specs=[
            SMEM, whole, whole, whole, whole, whole, small_spec(layer), whole, cols, cols,
            pl.BlockSpec((width, TILE), lambda i: (0, proj_at)),
            col_spec(w_one),
            pl.BlockSpec((TILE, width), lambda i: (i, 0)),
        ]
        + [ANY] * len(after),
        out_specs=(ANY, ANY, whole, whole, whole_spec((SUM_ROWS, width))),
        scratch_shapes=[
            pltpu.VMEM((rows, width), B16),
            pltpu.VMEM((width, rows), B16),
            pltpu.VMEM((rows, width), F32),
            pltpu.VMEM((2, width, TILE), B16),
            pltpu.VMEM((width // STRIP, TILE, STRIP), F32),
            pltpu.VMEM((2, 2, TILE // 4, 2 * width), B16),
            pltpu.VMEM((2, width, width // 2), B16),
            pltpu.SemaphoreType.DMA((4, 2)),
        ],
        compiler_params=params(),
        cost_estimate=cost(20),
        name="mlp_grad",
    )(core, grad, mid, mlp_out, branch, att, small, h2, act, slope, w_proj[0], w_one[0], w_two, *after)


CHIP_Y, CORES, CHIP_Z, CHIP_X = 2, 2, 4, 2
FAST_SHARDS = CHIP_Y * CORES * CHIP_Z * CHIP_X

def place(y, c, z, x):
    return (y * CORES + c) * (CHIP_Z * CHIP_X) + z * CHIP_X + x

def moves(fn):
    pairs = []
    for y in range(CHIP_Y):
        for c in range(CORES):
            for z in range(CHIP_Z):
                for x in range(CHIP_X):
                    pairs.append((place(y, c, z, x), place(*fn(y, c, z, x))))
    return pairs

CORE_SWAP = moves(lambda y, c, z, x: (y, 1 - c, z, x))
PLANE = (
    moves(lambda y, c, z, x: (y, c, z, 1 - x) if c == 0 else (1 - y, c, z, x)),
    moves(lambda y, c, z, x: (1 - y, c, z, x) if c == 0 else (y, c, z, 1 - x)),
)
X_SWAP = moves(lambda y, c, z, x: (y, c, z, 1 - x))
Y_SWAP = moves(lambda y, c, z, x: (1 - y, c, z, x))
Z_SHIFT = [moves(lambda y, c, z, x, k=k: (y, c, (z + k) % CHIP_Z, x)) for k in range(CHIP_Z)]

def send(v, pairs):
    return lax.ppermute(v, AXES, pairs)

def my_place():
    dp = lax.axis_index("dp"); fs = lax.axis_index("fsdp")
    return dp // CORES, dp % CORES, fs // CHIP_X, fs % CHIP_X

def half_of(v, which):
    h = v.shape[-1] // 2
    return lax.dynamic_slice_in_dim(v, which * h, h, axis=v.ndim - 1)

def no_sooner(arrays):
    zero = jnp.zeros((), B16)
    for v in arrays:
        zero = zero + jnp.minimum(jnp.abs(v[(0,) * v.ndim]), 0).astype(B16)
    return zero


class Gathering:
    def __init__(self, mats):
        self.mats = mats
        _, c, _, _ = my_place()

        def pick(which):
            return jnp.concatenate(
                [half_of(m, which)[i] for m in mats for i in range(m.shape[0])], axis=-1
            )

        self.piece = jnp.stack([pick(c), send(pick(1 - c), CORE_SWAP)])

    def along(self, behind=()):
        piece = self.piece + no_sooner(behind) if behind else self.piece
        self.moved = [send(piece, Z_SHIFT[k]) for k in range(1, CHIP_Z)]
        return self.moved

    def plane(self, behind=()):
        base = jnp.stack([self.piece] + self.moved)
        if behind:
            base = base + no_sooner(behind)
        self.own = [base, send(base, PLANE[0]), send(base, PLANE[1])]
        return self.own

    def far(self, behind=()):
        first = self.own[1] + no_sooner(behind) if behind else self.own[1]
        self.own.append(send(first, PLANE[1]))
        self.other = [send(v, CORE_SWAP) for v in self.own]

    def finish(self, after=()):
        return assemble(self.own, self.other, self.mats, after)


def assemble_kernel(counts, widths, pos_ref, *refs):
    src = refs[:8]; outs = refs[-1 - len(counts):-1]; sem = refs[-1]
    y, c, z, x = (pos_ref[i] for i in range(4))
    copies = []
    for side in range(2):
        core = c if side == 0 else 1 - c
        for a in range(4):
            for e in range(4):
                f1, f2 = a & 1, a >> 1
                fx = jnp.where(core == 0, f1, f2)
                fy = jnp.where(core == 0, f2, f1)
                yy = (y + fy) % 2
                xx = (x + fx) % 2
                zz = (z + CHIP_Z - e) % CHIP_Z
                for dc in range(2):
                    cc = core if dc == 0 else 1 - core
                    d = place(yy, cc, zz, xx)
                    col = 0
                    for out, count, w in zip(outs, counts, widths):
                        for k in range(count):
                            cp = pltpu.make_async_copy(
                                src[side * 4 + a].at[e, dc, :, pl.ds(col, w)],
                                out.at[d, k, :, pl.ds(pl.multiple_of(core * w, 128), w)],
                                sem,
                            )
                            cp.start(); copies.append(cp)
                            col += w
    for cp in copies:
        cp.wait()

def assemble(own, other, mats, after=()):
    rows = mats[0].shape[1]
    counts = [m.shape[0] for m in mats]; widths = [m.shape[2] // 2 for m in mats]
    pos = jnp.stack([p.astype(jnp.int32) for p in my_place()])
    return pl.pallas_call(
        functools.partial(assemble_kernel, counts, widths),
        out_shape=[jax.ShapeDtypeStruct((FAST_SHARDS, n, rows, 2 * w), B16) for n, w in zip(counts, widths)],
        in_specs=[pl.BlockSpec(memory_space=pltpu.SMEM)] + [ANY] * (8 + len(after)),
        out_specs=[pl.BlockSpec(memory_space=pltpu.VMEM)] * len(counts),
        scratch_shapes=[pltpu.SemaphoreType.DMA],
        compiler_params=params(),
        cost_estimate=cost(7),
        name="assemble",
    )(pos, *own, *other, *after)


def sum_plane(v):
    for pairs in (CORE_SWAP, X_SWAP, Y_SWAP):
        v = v + send(v, pairs)
    return v


class Reduction:
    def __init__(self, theirs, mine):
        self.theirs = theirs
        self.own = mine
        self.y, self.c, self.z, self.x = my_place()
        self.split = (CHIP_Y, CORES, CHIP_Z, CHIP_X, mine.shape[0] // FAST_SHARDS)

    def swap(self):
        self.got = send(self.theirs, CORE_SWAP)
        return [self.got]

    def part(self, f1, f2):
        c = self.c
        fx = jnp.where(c == 0, f1, f2)
        fy = jnp.where(c == 0, f2, f1)

        def cut(v):
            v = v.reshape(self.split + (v.shape[-1],))
            at = ((self.y + fy) % CHIP_Y, 0, 0, (self.x + fx) % CHIP_X, 0, 0)
            size = (1, CORES, CHIP_Z, 1) + v.shape[4:]
            return lax.dynamic_slice(v, at, size)[0, :, :, 0].astype(F32)

        return cut(self.own) + cut(self.got)

    def far(self):
        self.r3 = send(self.part(1, 1).astype(B16), PLANE[1])
        return [self.r3]

    def side(self):
        self.r2 = send(self.part(0, 1).astype(B16), PLANE[1])
        return [self.r2]

    def near(self):
        self.r1 = send((self.part(1, 0) + self.r3.astype(F32)).astype(B16), PLANE[0])
        return [self.r1]

    def along(self):
        base = self.part(0, 0) + self.r2.astype(F32) + self.r1.astype(F32)

        def at_z(k):
            return lax.dynamic_slice_in_dim(base, (self.z + k) % CHIP_Z, 1, axis=1)[:, 0]

        self.mine = at_z(0)
        self.rz = [send(at_z(k).astype(B16), Z_SHIFT[k]) for k in range(1, CHIP_Z)]
        return self.rz

    def finish(self, behind=()):
        total = self.mine + no_sooner(behind).astype(F32) if behind else self.mine
        for r in self.rz:
            total = total + r.astype(F32)
        c = self.c
        keep = lax.dynamic_slice_in_dim(total, c, 1, axis=0)[0]
        give = lax.dynamic_slice_in_dim(total, 1 - c, 1, axis=0)[0]
        other = send(give, CORE_SWAP)
        first = jnp.where(c == 0, keep, other)
        second = jnp.where(c == 0, other, keep)
        return first, second


def unpack_kernel(first, src_ref, *refs):
    out_ref, sem = refs[-2:]
    shards, ratio, _, width = out_ref.shape
    copies = []
    for d in range(shards):
        for k in range(ratio):
            copy = pltpu.make_async_copy(
                src_ref.at[d, :, pl.ds(first + k * width, width)], out_ref.at[d, k], sem
            )
            copy.start()
            copies.append(copy)
    for copy in copies:
        copy.wait()


def unpack_two(packed, first, ratio, width, after=()):
    shards, rows, _ = packed.shape
    return pl.pallas_call(
        functools.partial(unpack_kernel, first),
        out_shape=jax.ShapeDtypeStruct((shards, ratio, rows, width), B16),
        in_specs=[ANY] * (1 + len(after)),
        out_specs=pl.BlockSpec(memory_space=pltpu.VMEM),
        scratch_shapes=[pltpu.SemaphoreType.DMA],
        compiler_params=params(),
        cost_estimate=cost(5),
        name="unpack",
    )(packed, *after)


def fence_kernel(last_ref, *refs):
    refs[-1][...] = last_ref[...]


def fence(last, after):
    whole = pl.BlockSpec(memory_space=pltpu.VMEM)
    return pl.pallas_call(
        fence_kernel,
        out_shape=jax.ShapeDtypeStruct(last.shape, F32),
        in_specs=[whole] + [ANY] * len(after),
        out_specs=whole,
        compiler_params=params(),
        cost_estimate=cost(25),
        name="fence",
    )(last, *after)


def small_offsets(own, entries, device):
    per_row = TILE // (4 * own)
    return own * device, 4 * own * lax.rem(device, per_row), entries * device, device // per_row


def by_row(vectors, hidden, tables):
    row = lax.broadcasted_iota(jnp.int32, vectors.shape, 0)
    return jnp.where(row < B_ONE, vectors, jnp.where(row < TABLE, hidden, tables))


def own_kernel(*refs):
    out_ref, tmp_ref = refs[-2:]
    hidden_ref, table_ref = refs[-4:-2]
    tmp_ref[...] = jnp.zeros_like(tmp_ref)
    for layer in range(LAYERS):
        for i, ref in enumerate(refs[:B_ONE]):
            tmp_ref[layer, i : i + 1, : ref.shape[1]] = ref[layer : layer + 1, :].astype(F32)
        for i in range(B_ONE, TABLE):
            tmp_ref[layer, i : i + 1, : hidden_ref.shape[1]] = hidden_ref[
                layer : layer + 1, :
            ].astype(F32)
        heads, entries = table_ref.shape[1:]
        tmp_ref[layer, TABLE : TABLE + heads, :entries] = table_ref[layer].astype(F32)
    out_ref[...] = tmp_ref[...].astype(B16)


def own_small(vectors, hidden, table):
    whole = pl.BlockSpec(memory_space=pltpu.VMEM)
    return pl.pallas_call(
        own_kernel,
        out_shape=jax.ShapeDtypeStruct((LAYERS, SMALL_ROWS, STRIP), B16),
        in_specs=[whole] * (len(vectors) + 2),
        out_specs=whole,
        scratch_shapes=[pltpu.VMEM((LAYERS, SMALL_ROWS, STRIP), F32)],
        compiler_params=params(),
        cost_estimate=cost(1),
        name="small_own",
    )(*vectors, hidden, table)


def place_kernel(own, entries, device_ref, *refs):
    out_ref = refs[-1]
    row = lax.broadcasted_iota(jnp.int32, (SMALL_ROWS, TILE), 0)
    for layer in range(out_ref.shape[0]):
        total = jnp.zeros((SMALL_ROWS, TILE), F32)
        for k, piece_ref in enumerate(refs[:-1]):
            vec_at, b1_at, tab_at, line = small_offsets(own, entries, device_ref[k])
            piece = piece_ref[layer].astype(F32)
            rest = jnp.zeros((SMALL_ROWS, TILE - piece.shape[1]), F32)
            wide = jnp.concatenate([piece, rest], axis=1)
            hidden = jnp.where(row - B_ONE == line, pltpu.roll(wide, b1_at, 1), 0.0)
            total += by_row(pltpu.roll(wide, vec_at, 1), hidden, pltpu.roll(wide, tab_at, 1))
        out_ref[layer] = total.astype(B16)


def put_small(pieces, devices, own, entries):
    whole = pl.BlockSpec(memory_space=pltpu.VMEM)
    return pl.pallas_call(
        functools.partial(place_kernel, own, entries),
        out_shape=jax.ShapeDtypeStruct(pieces[0].shape[:2] + (TILE,), B16),
        in_specs=[SMEM] + [whole] * len(pieces),
        out_specs=whole,
        compiler_params=params(),
        cost_estimate=cost(1),
        name="small_place",
    )(devices, *pieces)


def collect_kernel(own, entries, device_ref, total_ref, *refs):
    outs = refs[-device_ref.shape[0] :]
    for k, out_ref in enumerate(outs):
        vec_at, b1_at, tab_at, line = small_offsets(own, entries, device_ref[k])

        def turn(v, at):
            return pltpu.roll(v, lax.rem(TILE - at, TILE), 1)

        for layer in range(total_ref.shape[0]):
            total = total_ref[layer]
            hidden = jnp.broadcast_to(total_ref[layer, pl.ds(B_ONE + line, 1), :], total.shape)
            wide = by_row(turn(total, vec_at), turn(hidden, b1_at), turn(total, tab_at))
            out_ref[layer] = wide[:, : out_ref.shape[2]]


def collect(total, devices, own, entries, after=()):
    whole = pl.BlockSpec(memory_space=pltpu.VMEM)
    count = devices.shape[0]
    piece = jax.ShapeDtypeStruct(total.shape[:2] + (STRIP,), F32)
    return pl.pallas_call(
        functools.partial(collect_kernel, own, entries),
        out_shape=[piece] * count,
        in_specs=[SMEM, whole] + [ANY] * len(after),
        out_specs=[whole] * count,
        compiler_params=params(),
        cost_estimate=cost(2),
        name="small_collect",
    )(devices, total, *after)


def pack_kernel(*refs):
    out_ref = refs[-1]
    out_ref[...] = jnp.zeros_like(out_ref)
    for layer in range(LAYERS):
        first, second, table = refs[3 * layer : 3 * layer + 3]
        out_ref[layer, 0:B_PROJ] = first[0:B_PROJ]
        out_ref[layer, B_PROJ:TABLE] = second[0 : TABLE - B_PROJ]
        for head in range(table.shape[0]):
            out_ref[layer, TABLE + head : TABLE + head + 1] = table[head]


def pack_small(parts, after=()):
    whole = pl.BlockSpec(memory_space=pltpu.VMEM)
    return pl.pallas_call(
        pack_kernel,
        out_shape=jax.ShapeDtypeStruct((LAYERS, SMALL_ROWS, TILE), F32),
        in_specs=[whole] * len(parts) + [ANY] * len(after),
        out_specs=whole,
        compiler_params=params(),
        cost_estimate=cost(2),
        name="small_pack",
    )(*parts, *after)


def per_device(
    shards, fast,
    tokens, masked_rows, cotangent, norm1_gain, norm1_bias, qkv_weight, q_bias, v_bias,
    proj_weight, proj_bias, gamma_attn, norm2_gain, norm2_bias, fc1_weight, fc1_bias,
    fc2_weight, fc2_bias, gamma_mlp, rel_table,
):
    vectors = (norm1_gain, norm1_bias, q_bias, v_bias, proj_bias, gamma_attn, norm2_gain,
               norm2_bias, fc2_bias, gamma_mlp)
    width = tokens.shape[1]
    images = masked_rows.shape[0]
    heads, entries = rel_table.shape[1:]
    own = qkv_weight.shape[1]
    ratio = fc2_weight.shape[1] // own
    hidden = fc1_weight.shape[2]
    me = lax.axis_index("dp") * lax.axis_size("fsdp") + lax.axis_index("fsdp")

    def pad_rows(v):
        v = v.astype(F32).reshape(images, IMG_ROWS, width)
        v = jnp.pad(v, ((0, 0), (0, PAD_ROWS - IMG_ROWS), (0, 0)))
        return v.reshape(images * PAD_ROWS, width)

    def cut_rows(v):
        return v.reshape(images, PAD_ROWS, width)[:, :IMG_ROWS].reshape(images * IMG_ROWS, width)

    used = TABLE + heads
    piece = own_small(vectors, fc1_bias, rel_table)
    hops = range(CHIP_Z) if fast else range(1)
    ring = CHIP_Z * CHIP_X

    def along_z(k):
        return (me // ring) * ring + (me + k * CHIP_X) % ring if fast else me

    backs = jnp.stack([along_z(-k) for k in hops]).astype(jnp.int32)
    ahead = jnp.stack([along_z(k) for k in hops]).astype(jnp.int32)
    pieces = [piece] + [send(piece, Z_SHIFT[k]) for k in hops[1:]]
    small = put_small(pieces, backs, own, entries)
    small = (sum_plane(small) if fast else lax.psum(small, AXES)).astype(F32)

    def two_blocks(layer):
        return fc2_weight[layer].reshape(ratio, own, width)

    def fetch_packed(layer, behind=()):
        two = two_blocks(layer)
        block = jnp.concatenate(
            [qkv_weight[layer], proj_weight[layer], fc1_weight[layer]]
            + [two[i] for i in range(ratio)],
            axis=1,
        )
        if behind:
            block = block + no_sooner(behind)
        return lax.all_gather(block, AXES, axis=0, tiled=True)

    if not fast:
        packed_weights = [fetch_packed(layer) for layer in range(LAYERS)]
        bias = build_bias(small, heads)
    else:
        first = Gathering([qkv_weight[0][None], proj_weight[0][None]])
        second = Gathering([fc1_weight[0][None], two_blocks(0)])
        moved = first.along()
        first.plane()
        first.far()
        moved = second.along(moved)
        bias = build_bias(small, heads, [moved[0], moved[2]])
        packed_weights = [None, fetch_packed(1)]
    weights = []
    x = pad_rows(tokens)
    saved = []
    for layer in range(LAYERS):
        full = packed_weights[layer]
        if full is None:
            w_qkv, w_proj = first.finish([bias])
            w_qkv = (w_qkv.reshape(width, 3 * width), 0)
            w_proj = (w_proj.reshape(width, width), 0)
        else:
            w_qkv, w_proj, w_one = (full, 0), (full, 3), (full, 4)
        qkv, h = qkv_forward(x, small, layer, w_qkv)
        qkv = qkv.reshape(images, PAD_ROWS, 3 * width)
        att, lse = attention_forward(qkv, bias, layer)
        att = att.reshape(images * PAD_ROWS, width)
        if full is None:
            second.plane([w_qkv[0]])
            second.far([att])
            w_one, w_two = second.finish()
            w_one = (w_one.reshape(width, hidden), 0)
        elif fast:
            w_two = unpack_two(full.reshape(shards, own, -1), 4 * width + hidden, ratio, width)
        else:
            w_two = full[:, 4 * width + hidden :].reshape(shards, own, ratio, width)
            w_two = w_two.transpose(0, 2, 1, 3)
        w_two = w_two.reshape(hidden, width)
        weights.append((w_qkv, w_proj, w_one, w_two))
        out, branch, mid, mlp_out, h2, act, slope = mlp_forward(
            x, att, small, layer, w_proj, w_one, w_two
        )
        saved.append((x, h, qkv, lse, att, branch, mid, mlp_out, h2, act, slope))
        x = out
    encoded = cut_rows(x.astype(B16))

    positions = jnp.arange(IMG_ROWS, dtype=jnp.int32)
    mask = jnp.any(masked_rows[:, :, None] == positions[None, None, :], axis=1)
    mask = jnp.pad(mask, ((0, 0), (0, PAD_ROWS - IMG_ROWS))).reshape(-1, 1)
    grad = jnp.where(mask, pad_rows(cotangent), 0.0)

    def scatter(theirs, mine):
        both = jnp.stack([mine, theirs])
        own_part = lax.psum_scatter(both, AXES, scatter_dimension=1, tiled=True).astype(F32)
        return own_part[0], own_part[1]

    core = (lax.axis_index("dp") % CORES if fast else jnp.int32(0)).astype(jnp.int32).reshape(1)
    reduced = [None] * LAYERS
    small_grads = [None] * LAYERS
    tables = [None] * LAYERS

    def backward(layer, grad, hooks):
        x, h, qkv, lse, att, branch, mid, mlp_out, h2, act, slope = saved[layer]
        w_qkv, w_proj, w_one, w_two = weights[layer]
        theirs, mine, d_mid, d_att, mlp_sums = mlp_backward(
            core, grad, mid, mlp_out, branch, att, small, layer, h2, act, slope, w_proj, w_one,
            w_two, hooks[0](),
        )
        main = (theirs, mine)
        d_qkv, d_bias = attention_backward(
            qkv, bias, lse, d_att.reshape(images, PAD_ROWS, width), layer, hooks[1](main)
        )
        tables[layer] = d_bias
        theirs, mine, grad, qkv_sums = qkv_backward(
            core, d_qkv.reshape(images * PAD_ROWS, 3 * width), h, x, d_mid, small, layer, w_qkv,
            hooks[2](),
        )
        small_grads[layer] = (qkv_sums, mlp_sums)
        return grad, main, (theirs, mine)

    if not fast:
        for layer in reversed(range(LAYERS)):
            none = (lambda: (), lambda main: (), lambda: ())
            grad, main, rest = backward(layer, grad, none)
            reduced[layer] = (scatter(*main), scatter(*rest))
        tables = [reduce_bias(t) for t in tables]
    else:
        a1, b1, a0, b0 = (None,) * 4

        def one_attention(main):
            nonlocal a1
            a1 = Reduction(*main)
            return ()

        def one_qkv():
            return a1.swap()

        grad, _, rest = backward(1, grad, (lambda: (), one_attention, one_qkv))
        b1 = Reduction(*rest)

        def zero_mlp():
            return a1.far()

        def zero_attention(main):
            nonlocal a0
            a0 = Reduction(*main)
            a0.swap()
            return a1.side() + b1.swap()

        def zero_qkv():
            for layer in range(LAYERS):
                tables[layer] = reduce_bias(tables[layer])
            moved = a1.near() + b1.far() + a0.far()
            a1.along()
            return moved + a1.rz + [tables[0], tables[1]]

        grad, _, rest = backward(0, grad, (zero_mlp, zero_attention, zero_qkv))
        b0 = Reduction(*rest)
        a0.side()
        a0.near()
        b1.side()
        b0.swap()

    parts = []
    for (qkv_sums, mlp_sums), table in zip(small_grads, tables):
        parts += [qkv_sums, mlp_sums, table]
    totals = pack_small(parts, [b0.got] if fast else ())
    totals = sum_plane(totals) if fast else lax.psum(totals, AXES)
    late = ()
    if fast:
        b1.near()
        a0.along()
        gate = fence(small_grads[0][0], b0.far() + b0.side() + [b1.r1, a0.rz[0], a0.rz[2], totals])
        late = [gate, a0.rz[1]] + b1.along() + b0.near()
    pieces = collect(totals, ahead, own, entries, late)
    if fast:
        b0.along()
        reduced[1] = (a1.finish([pieces[0]]), b1.finish([pieces[0]]))
        reduced[0] = (a0.finish([pieces[0]]), b0.finish())
    g_small = pieces[0]
    for k in hops[1:]:
        g_small = g_small + send(pieces[k], Z_SHIFT[k])
    g = [g_small[:, i, :own] for i in range(B_ONE)]
    g_b1 = g_small[:, B_ONE, : ratio * own]
    g_table = g_small[:, TABLE:used, :entries]

    def both(pick):
        return jnp.stack([pick(*r) for r in reduced])

    def thirds(low, high):
        half = width // 2
        cols = [v[:, i * half : (i + 1) * half] for i in range(3) for v in (low, high)]
        return jnp.concatenate(cols, axis=1)

    def join(low, high, first, last):
        return jnp.concatenate([low[:, first:last], high[:, first:last]], axis=1)

    half = hidden // 2
    g_qkv = both(lambda a, b: thirds(*b))
    g_one = both(lambda a, b: join(*a, 0, half))
    g_two = both(lambda a, b: join(*a, half, hidden).reshape(ratio * own, width))
    g_proj = both(lambda a, b: join(*a, hidden, hidden + width // 2))
    return (encoded, cut_rows(grad), g[N1_GAIN], g[N1_SHIFT], g_qkv, g[Q_BIAS], g[V_BIAS], g_proj,
            g[B_PROJ], g[G_ATTN], g[N2_GAIN], g[N2_SHIFT], g_one, g_b1, g_two, g[B_TWO], g[G_MLP],
            g_table)


def solution(mesh):
    shards = math.prod(mesh.shape[a] for a in AXES)
    fast = mesh.shape["dp"] == CHIP_Y * CORES and mesh.shape["fsdp"] == CHIP_Z * CHIP_X
    row = P(AXES, None)
    vec = P(None, AXES)
    mat = P(None, AXES, None)
    tab = P(None, None, AXES)
    return jax.shard_map(
        functools.partial(per_device, shards, fast),
        mesh=mesh,
        in_specs=(row, row, row, vec, vec, mat, vec, vec, mat, vec, vec, vec, vec, mat, vec, mat,
                  vec, vec, tab),
        out_specs=(row, row, vec, vec, mat, vec, vec, mat, vec, vec, vec, vec, mat, vec, mat,
                   vec, vec, tab),
        check_vma=False,
    )
```

```python
import functools
import math

import jax
import jax.numpy as jnp
import numpy as np
from jax import lax
from jax.experimental import pallas as pl
from jax.experimental.pallas import tpu as pltpu
from jax.sharding import PartitionSpec as P

GRID = 14
SPAN = 2 * GRID - 1
LAYERS = 2
IMG_ROWS = GRID * GRID + 1
PAD_ROWS = 208
LANES = 256
HEAD = 64
PAIR = 2 * HEAD
NEG = -1e30
TILE = 768
WIDE = 384
GROUP = 4
BLOCK = 16
SMALL_ROWS = 32
F32 = jnp.float32
B16 = jnp.bfloat16
AXES = ("dp", "fsdp")


def cost(us):
    return pl.CostEstimate(flops=us * 4_400_000_000, bytes_accessed=us * 14_000_000, transcendentals=0)


ANY = pl.BlockSpec(memory_space=pl.ANY)
SMEM = pl.BlockSpec(memory_space=pltpu.SMEM)

N1_GAIN, N1_SHIFT, Q_BIAS, V_BIAS, B_PROJ, G_ATTN, N2_GAIN, N2_SHIFT, B_TWO, G_MLP = range(10)
B_ONE = 10
TABLE = 14


def params(limit=56):
    return pltpu.CompilerParams(vmem_limit_bytes=limit * 1024 * 1024)


def dot(a, b, dims):
    return lax.dot_general(a, b, (dims, ((), ())), preferred_element_type=F32)


NN = ((1,), (0,))
NT = ((1,), (1,))
TN = ((0,), (0,))


def lane_onehot():
    out = np.zeros((WIDE, LANES), np.float32)
    for a in range(GRID):
        for b in range(GRID):
            out[SPAN * a + b, 1 + GRID * a + b] = 1.0
    return out


def row_onehot(turned):
    out = np.zeros((PAD_ROWS, BLOCK * GRID), np.float32)
    for c in range(GRID):
        for d in range(GRID):
            out[1 + GRID * c + d, BLOCK * c + (GRID - 1 - d if turned else d)] = 1.0
    return out


def bias_kernel(heads, small_ref, rows_ref, lanes_ref, *refs):
    out_ref, wide_ref = refs[-2:]
    first = lax.rem(pl.program_id(0) * GROUP, heads)
    for i in range(GROUP):
        table = small_ref[0, pl.ds(TABLE + first + i, 1), :]
        one_bias(table, rows_ref, lanes_ref, out_ref.at[i], wide_ref.at[i])


def one_bias(table, rows_ref, lanes_ref, out_ref, wide_ref):
    shifted = pltpu.roll(jnp.broadcast_to(table, (BLOCK, TILE)), TILE - (GRID - 1), 1)
    shifted = pltpu.roll(shifted, 0, 1, stride=1, stride_axis=0)
    for c in range(GRID):
        start = SPAN * (GRID - 1 - c)
        wide_ref[BLOCK * c : BLOCK * (c + 1), :] = shifted[:, start : start + WIDE].astype(B16)
    narrow = dot(wide_ref[...], lanes_ref[...], NN).astype(B16)
    val = dot(rows_ref[...], narrow, NN)
    row = lax.broadcasted_iota(jnp.int32, (PAD_ROWS, LANES), 0)
    lane = lax.broadcasted_iota(jnp.int32, (PAD_ROWS, LANES), 1)
    cls = SPAN * SPAN
    val = jnp.where(lane == 0, table[:, cls : cls + 1], val)
    first = jnp.where(lane == 0, table[:, cls + 2 : cls + 3], table[:, cls + 1 : cls + 2])
    val = jnp.where(row == 0, first, val)
    out_ref[...] = jnp.where(row >= IMG_ROWS, NEG, val)


def build_bias(small, heads, after=()):
    layers = small.shape[0]
    return pl.pallas_call(
        functools.partial(bias_kernel, heads),
        grid=(layers * heads // GROUP,),
        out_shape=jax.ShapeDtypeStruct((layers * heads, PAD_ROWS, LANES), F32),
        in_specs=[
            pl.BlockSpec((1, SMALL_ROWS, TILE), lambda h: (h * GROUP // heads, 0, 0)),
            pl.BlockSpec((PAD_ROWS, BLOCK * GRID), lambda h: (0, 0)),
            pl.BlockSpec((WIDE, LANES), lambda h: (0, 0)),
        ]
        + [ANY] * len(after),
        out_specs=pl.BlockSpec((GROUP, PAD_ROWS, LANES), lambda h: (h, 0, 0)),
        scratch_shapes=[pltpu.VMEM((GROUP, BLOCK * GRID, WIDE), B16)],
        compiler_params=params(),
        cost_estimate=cost(10),
        name="bias_expand",
    )(small, jnp.asarray(row_onehot(False), B16), jnp.asarray(lane_onehot(), B16), *after)


def bias_grad_kernel(g_ref, rows_ref, lanes_ref, *refs):
    out_ref, acc_ref = refs[-2:]
    for i in range(GROUP):
        one_bias_grad(g_ref.at[i], rows_ref, lanes_ref, out_ref.at[i], acc_ref.at[i])


def one_bias_grad(g_ref, rows_ref, lanes_ref, out_ref, acc_ref):
    row = lax.broadcasted_iota(jnp.int32, (PAD_ROWS, LANES), 0)
    lane = lax.broadcasted_iota(jnp.int32, (PAD_ROWS, LANES), 1)
    g = jnp.where((lane < IMG_ROWS) & (row < IMG_ROWS), g_ref[...], 0.0)
    high = g.astype(B16)
    wide = None
    for part in (high, (g - high.astype(F32)).astype(B16)):
        moved = dot(rows_ref[...], part, NN).astype(B16)
        moved = dot(moved, lanes_ref[...], NN)
        wide = moved if wide is None else wide + moved
    acc_ref[...] = jnp.zeros_like(acc_ref)
    for c in range(GRID):
        start = SPAN * (GRID - 1 - c)
        acc_ref[:, start : start + WIDE] += wide[BLOCK * c : BLOCK * (c + 1), :]
    turned = pltpu.roll(acc_ref[...], 0, 1, stride=1, stride_axis=0)
    total = jnp.sum(turned, axis=0, keepdims=True)
    column = jnp.sum(jnp.where(lane[:, :1] == 0, g[:, :1], 0.0), axis=0, keepdims=True)
    to_self = g[0:1, 0:1]
    to_patch = column - to_self
    from_patch = jnp.sum(g[0:1, :], axis=1, keepdims=True) - to_self
    spot = lax.broadcasted_iota(jnp.int32, (1, TILE), 1)
    cls = SPAN * SPAN
    total = jnp.where(spot == cls, to_patch, total)
    total = jnp.where(spot == cls + 1, from_patch, total)
    out_ref[...] = jnp.where(spot == cls + 2, to_self, total)


def reduce_bias(grad, after=()):
    heads = grad.shape[0]
    out = pl.pallas_call(
        bias_grad_kernel,
        grid=(heads // GROUP,),
        out_shape=jax.ShapeDtypeStruct((heads, 1, TILE), F32),
        in_specs=[
            pl.BlockSpec((GROUP, PAD_ROWS, LANES), lambda h: (h, 0, 0)),
            pl.BlockSpec((BLOCK * GRID, PAD_ROWS), lambda h: (0, 0)),
            pl.BlockSpec((LANES, WIDE), lambda h: (0, 0)),
        ]
        + [ANY] * len(after),
        out_specs=pl.BlockSpec((GROUP, 1, TILE), lambda h: (h, 0, 0)),
        scratch_shapes=[pltpu.VMEM((GROUP, BLOCK, TILE), F32)],
        compiler_params=params(),
        cost_estimate=cost(6),
        name="bias_reduce",
    )(grad, jnp.asarray(row_onehot(True).T, B16), jnp.asarray(lane_onehot().T, B16), *after)
    return out


def head_mask(which):
    lane = lax.broadcasted_iota(jnp.int32, (PAD_ROWS, PAIR), 1)
    return (lane < HEAD) if which == 0 else (lane >= HEAD)


def attention_kernel(width, qkv_ref, bias_ref, out_ref, lse_ref):
    heads = width // HEAD
    for pair in range(heads // 2):
        at = pair * PAIR
        q = qkv_ref[0, :, at : at + PAIR]
        k = qkv_ref[0, :, width + at : width + at + PAIR]
        v = qkv_ref[0, :, 2 * width + at : 2 * width + at + PAIR]
        q = q * jnp.asarray(HEAD ** (-0.5), B16)
        v_t = v.T
        parts = []
        for t in range(2):
            head = 2 * pair + t
            q_t = jnp.where(head_mask(t), q, jnp.zeros_like(q))
            scores = dot(k, q_t, NT) + bias_ref[head, :, 0:PAD_ROWS]
            top = jnp.max(scores, axis=0, keepdims=True)
            weights = jnp.exp(scores - top)
            total = jnp.sum(weights, axis=0, keepdims=True)
            probs = (weights * (1.0 / total)).astype(B16)
            lse_ref[0, head : head + 1, 0:PAD_ROWS] = top + jnp.log(total)
            parts.append(dot(v_t[t * HEAD : (t + 1) * HEAD], probs, NN))
        out_ref[0, :, at : at + PAIR] = jnp.concatenate(parts, axis=0).T.astype(B16)


def attention_forward(qkv, bias, layer):
    images = qkv.shape[0]
    width = qkv.shape[2] // 3
    heads = width // HEAD
    return pl.pallas_call(
        functools.partial(attention_kernel, width),
        grid=(images,),
        out_shape=(
            jax.ShapeDtypeStruct((images, PAD_ROWS, width), B16),
            jax.ShapeDtypeStruct((images, 16, LANES), F32),
        ),
        in_specs=[
            pl.BlockSpec((1, PAD_ROWS, 3 * width), lambda i: (i, 0, 0)),
            pl.BlockSpec((heads, PAD_ROWS, LANES), lambda i: (layer, 0, 0)),
        ],
        out_specs=(
            pl.BlockSpec((1, PAD_ROWS, width), lambda i: (i, 0, 0)),
            pl.BlockSpec((1, 16, LANES), lambda i: (i, 0, 0)),
        ),
        compiler_params=params(),
        cost_estimate=cost(8),
        name="attention",
    )(qkv, bias)


def attention_grad_kernel(width, qkv_ref, bias_ref, lse_ref, g_ref, *refs):
    out_ref, dbias_ref = refs[-2:]
    heads = width // HEAD
    scale = HEAD ** (-0.5)

    @pl.when(pl.program_id(0) == 0)
    def _():
        dbias_ref[...] = jnp.zeros_like(dbias_ref)

    for pair in range(heads // 2):
        at = pair * PAIR
        q = qkv_ref[0, :, at : at + PAIR]
        k = qkv_ref[0, :, width + at : width + at + PAIR]
        v = qkv_ref[0, :, 2 * width + at : 2 * width + at + PAIR]
        g = g_ref[0, :, at : at + PAIR]
        q = q * jnp.asarray(scale, B16)
        k_t = k.T
        dq_parts = []
        dk = None
        dv = None
        for t in range(2):
            head = 2 * pair + t
            q_t = jnp.where(head_mask(t), q, jnp.zeros_like(q))
            g_t = jnp.where(head_mask(t), g, jnp.zeros_like(g))
            scores = dot(k, q_t, NT) + bias_ref[head, :, 0:PAD_ROWS]
            probs = jnp.exp(scores - lse_ref[0, head : head + 1, 0:PAD_ROWS])
            dprobs = dot(v, g_t, NT)
            dv_t = dot(probs.astype(B16), g_t, NN)
            mean = jnp.sum(probs * dprobs, axis=0, keepdims=True)
            dscores = (probs * (dprobs - mean)).astype(B16)
            dbias_ref[head, :, 0:PAD_ROWS] += dscores.astype(F32)
            dk_t = dot(dscores, q_t, NN)
            dq_parts.append(dot(k_t[t * HEAD : (t + 1) * HEAD], dscores, NN))
            dk = dk_t if dk is None else dk + dk_t
            dv = dv_t if dv is None else dv + dv_t
        dq = jnp.concatenate(dq_parts, axis=0).T * scale
        out_ref[0, :, at : at + PAIR] = dq.astype(B16)
        out_ref[0, :, width + at : width + at + PAIR] = dk.astype(B16)
        out_ref[0, :, 2 * width + at : 2 * width + at + PAIR] = dv.astype(B16)


def attention_backward(qkv, bias, lse, grad, layer, after=()):
    images = qkv.shape[0]
    width = qkv.shape[2] // 3
    heads = width // HEAD
    return pl.pallas_call(
        functools.partial(attention_grad_kernel, width),
        grid=(images,),
        out_shape=(
            jax.ShapeDtypeStruct((images, PAD_ROWS, 3 * width), B16),
            jax.ShapeDtypeStruct((heads, PAD_ROWS, LANES), F32),
        ),
        in_specs=[
            pl.BlockSpec((1, PAD_ROWS, 3 * width), lambda i: (i, 0, 0)),
            pl.BlockSpec((heads, PAD_ROWS, LANES), lambda i: (layer, 0, 0)),
            pl.BlockSpec((1, 16, LANES), lambda i: (i, 0, 0)),
            pl.BlockSpec((1, PAD_ROWS, width), lambda i: (i, 0, 0)),
        ]
        + [ANY] * len(after),
        out_specs=(
            pl.BlockSpec((1, PAD_ROWS, 3 * width), lambda i: (i, 0, 0)),
            pl.BlockSpec((heads, PAD_ROWS, LANES), lambda i: (0, 0, 0)),
        ),
        compiler_params=params(),
        cost_estimate=cost(12),
        name="attention_grad",
    )(qkv, bias, lse, grad, *after)


def normalize(x):
    centered = x - jnp.mean(x, -1, keepdims=True)
    scale = lax.rsqrt(jnp.mean(centered * centered, -1, keepdims=True) + 1e-06)
    return centered * scale, scale


def normalize_grad(x_hat, scale, dy):
    return scale * (
        dy - jnp.mean(dy, -1, keepdims=True) - x_hat * jnp.mean(dy * x_hat, -1, keepdims=True)
    )


def gelu_and_slope(x):
    t = 1.0 / (1.0 + (0.3275911 / math.sqrt(2.0)) * jnp.abs(x))
    bell = jnp.exp(-0.5 * x * x)
    poly = 0.5 * 1.061405429
    for coef in (-1.453152027, 1.421413741, -0.284496736, 0.254829592):
        poly = poly * t + 0.5 * coef
    tail = poly * t * bell
    phi = jnp.where(x >= 0, 1.0 - tail, tail)
    return x * phi, phi + x * bell * (1.0 / math.sqrt(2.0 * math.pi))


def total_rows(v):
    return jnp.sum(v, axis=0, keepdims=True)


def small_spec(layer):
    return pl.BlockSpec((1, SMALL_ROWS, TILE), lambda i: (layer, 0, 0))


def whole_spec(shape):
    return pl.BlockSpec(shape, lambda i: (0,) * len(shape))


def col_spec(weight):
    array, first = weight
    return pl.BlockSpec((array.shape[0], TILE), lambda i: (0, first + i))


def qkv_kernel(x_ref, small_ref, w_ref, qkv_ref, h_ref):
    step = pl.program_id(0)

    @pl.when(step == 0)
    def _():
        x_hat, _ = normalize(x_ref[...])
        gain = small_ref[0, N1_GAIN : N1_GAIN + 1]
        h_ref[...] = (x_hat * gain + small_ref[0, N1_SHIFT : N1_SHIFT + 1]).astype(B16)

    zero = jnp.zeros((1, TILE), F32)
    bias = jnp.where(step == 0, small_ref[0, Q_BIAS : Q_BIAS + 1], zero)
    bias = jnp.where(step == 2, small_ref[0, V_BIAS : V_BIAS + 1], bias)
    qkv_ref[...] = (dot(h_ref[...], w_ref[...], NN) + bias).astype(B16)


def qkv_forward(x, small, layer, w_qkv):
    rows, width = x.shape
    return pl.pallas_call(
        qkv_kernel,
        grid=(3,),
        out_shape=(
            jax.ShapeDtypeStruct((rows, 3 * width), B16),
            jax.ShapeDtypeStruct((rows, width), B16),
        ),
        in_specs=[whole_spec((rows, width)), small_spec(layer), col_spec(w_qkv)],
        out_specs=(
            pl.BlockSpec((rows, TILE), lambda i: (0, i)),
            whole_spec((rows, width)),
        ),
        compiler_params=params(),
        cost_estimate=cost(6),
        name="qkv",
    )(x, small, w_qkv[0])


def qkv_grad_kernel(core_ref, g_ref, h_ref, x_ref, dmid_ref, small_ref, w_ref, *refs):
    theirs_ref, mine_ref, dx_ref, sums_ref, ht_ref, dh_ref = refs[-6:]
    step = pl.program_id(0)

    @pl.when(step == 0)
    def _():
        ht_ref[...] = h_ref[...].T
        sums_ref[...] = jnp.zeros_like(sums_ref)

    g = g_ref[...]
    dw = dot(ht_ref[...], g, NN).astype(B16)
    low, high = dw[:, : TILE // 2], dw[:, TILE // 2 :]

    @pl.when(core_ref[0] == 0)
    def _():
        mine_ref[...] = low
        theirs_ref[...] = high

    @pl.when(core_ref[0] != 0)
    def _():
        mine_ref[...] = high
        theirs_ref[...] = low

    part = dot(g, w_ref[...], NT)
    total = total_rows(g.astype(F32))

    @pl.when(step == 0)
    def _():
        dh_ref[...] = part
        sums_ref[Q_BIAS : Q_BIAS + 1] = total

    @pl.when(step > 0)
    def _():
        dh_ref[...] += part

    @pl.when(step == 2)
    def _():
        sums_ref[V_BIAS : V_BIAS + 1] = total
        dh = dh_ref[...]
        x_hat, scale = normalize(x_ref[...])
        sums_ref[N1_GAIN : N1_GAIN + 1] = total_rows(dh * x_hat)
        sums_ref[N1_SHIFT : N1_SHIFT + 1] = total_rows(dh)
        gain = small_ref[0, N1_GAIN : N1_GAIN + 1]
        dx_ref[...] = dmid_ref[...] + normalize_grad(x_hat, scale, dh * gain)


def qkv_backward(core, grad, h, x, d_mid, small, layer, w_qkv, after=()):
    rows, width = x.shape
    whole = whole_spec((rows, width))
    tiles = pl.BlockSpec((rows, TILE), lambda i: (0, i))
    return pl.pallas_call(
        qkv_grad_kernel,
        grid=(3,),
        out_shape=(
            jax.ShapeDtypeStruct((width, 3 * width // 2), B16),
            jax.ShapeDtypeStruct((width, 3 * width // 2), B16),
            jax.ShapeDtypeStruct((rows, width), F32),
            jax.ShapeDtypeStruct((8, width), F32),
        ),
        in_specs=[SMEM, tiles, whole, whole, whole, small_spec(layer), col_spec(w_qkv)]
        + [ANY] * len(after),
        out_specs=(
            pl.BlockSpec((width, TILE // 2), lambda i: (0, i)),
            pl.BlockSpec((width, TILE // 2), lambda i: (0, i)),
            whole,
            whole_spec((8, width)),
        ),
        scratch_shapes=[pltpu.VMEM((width, rows), B16), pltpu.VMEM((rows, width), F32)],
        compiler_params=params(),
        cost_estimate=cost(11),
        name="qkv_grad",
    )(core, grad, h, x, d_mid, small, w_qkv[0], *after)


def mlp_kernel(
    x_ref, att_ref, small_ref, wp_ref, w1_ref, w2_ref,
    out_ref, branch_ref, mid_ref, mlp_ref, h2_ref, act_ref, slope_ref,
):
    step = pl.program_id(0)

    def vec(i):
        return small_ref[0, i : i + 1]

    @pl.when(step == 0)
    def _():
        branch = dot(att_ref[...], wp_ref[...], NN) + vec(B_PROJ)
        branch_ref[...] = branch
        mid = x_ref[...] + vec(G_ATTN) * branch
        mid_ref[...] = mid
        x_hat, _ = normalize(mid)
        h2_ref[...] = (x_hat * vec(N2_GAIN) + vec(N2_SHIFT)).astype(B16)

    pre = dot(h2_ref[...], w1_ref[...], NN) + small_ref[0, pl.ds(B_ONE + step, 1)]
    act, slope = gelu_and_slope(pre)
    act = act.astype(B16)
    act_ref[...] = act
    slope_ref[...] = slope.astype(B16)
    part = dot(act, w2_ref[...], NN)

    @pl.when(step == 0)
    def _():
        mlp_ref[...] = part + vec(B_TWO)

    @pl.when(step > 0)
    def _():
        mlp_ref[...] += part

    @pl.when(step == pl.num_programs(0) - 1)
    def _():
        out_ref[...] = mid_ref[...] + vec(G_MLP) * mlp_ref[...]


def mlp_forward(x, att, small, layer, w_proj, w_one, w_two):
    rows, width = x.shape
    hidden = w_two.shape[0]
    whole = whole_spec((rows, width))
    cols = pl.BlockSpec((rows, TILE), lambda i: (0, i))
    full = jax.ShapeDtypeStruct((rows, width), F32)
    proj_at = w_proj[1]
    return pl.pallas_call(
        mlp_kernel,
        grid=(hidden // TILE,),
        out_shape=(
            full, full, full, full,
            jax.ShapeDtypeStruct((rows, width), B16),
            jax.ShapeDtypeStruct((rows, hidden), B16),
            jax.ShapeDtypeStruct((rows, hidden), B16),
        ),
        in_specs=[
            whole,
            whole,
            small_spec(layer),
            pl.BlockSpec((width, TILE), lambda i: (0, proj_at)),
            col_spec(w_one),
            pl.BlockSpec((TILE, width), lambda i: (i, 0)),
        ],
        out_specs=(whole, whole, whole, whole, whole, cols, cols),
        compiler_params=params(),
        cost_estimate=cost(15),
        name="mlp",
    )(x, att, small, w_proj[0], w_one[0], w_two)


SUM_ROWS = 16
STRIP = 128


def mlp_grad_kernel(
    core_ref, g_ref, mid_ref, mlp_ref, branch_ref, att_ref, small_ref, h2_ref, act_ref, slope_ref, wp_ref,
    w1_ref, w2_ref, *refs,
):
    (theirs_ref, mine_ref, dmid_ref, datt_ref, sums_ref,
     dmlp_ref, h2t_ref, dh2_ref, one_ref, wide_ref, two_ref, proj_ref, sems) = refs[-13:]
    step = pl.program_id(0)
    steps = pl.num_programs(0)
    slot = lax.rem(step, 2)
    width = mid_ref.shape[1]
    hidden = 4 * width
    part_rows = TILE // 4

    def vec(i):
        return small_ref[0, i : i + 1]

    def put(row, value):
        at = row - B_PROJ
        sums_ref[at : at + 1] = value

    def copy_one(out_ref, j, s):
        return pltpu.make_async_copy(
            one_ref.at[s],
            out_ref.at[:, pl.ds(pl.multiple_of(lax.rem(j, 2) * TILE, TILE), TILE)],
            sems.at[0, s],
        )

    def copy_two(out_ref, j, s, which):
        return pltpu.make_async_copy(
            two_ref.at[s, which],
            out_ref.at[pl.ds(pl.multiple_of(j * part_rows, part_rows), part_rows),
                       pl.ds(2 * width, 2 * width)],
            sems.at[1 + which, s],
        )

    def proj_copy(out_ref, which):
        return pltpu.make_async_copy(
            proj_ref.at[which], out_ref.at[:, pl.ds(4 * width, width // 2)], sems.at[3, which]
        )

    def on_halves(run):
        for core in range(2):

            @pl.when(core_ref[0] == core)
            def _(core=core):
                run(mine_ref, core)
                run(theirs_ref, 1 - core)

    def send_one(j, s):
        def run(out_ref, which):
            @pl.when(j // 2 == which)
            def _():
                copy_one(out_ref, j, s).start()

        on_halves(run)

    def send_two(j, s):
        on_halves(lambda out_ref, which: copy_two(out_ref, j, s, which).start())

    def wait_step(j, s):
        copy_one(mine_ref, j, s).wait()
        for which in range(2):
            copy_two(mine_ref, j, s, which).wait()

    @pl.when(step == 0)
    def _():
        g = g_ref[...]
        dmlp = (g * vec(G_MLP)).astype(B16)
        dmlp_ref[...] = dmlp
        h2t_ref[...] = h2_ref[...].T
        sums_ref[...] = jnp.zeros_like(sums_ref)
        put(G_MLP, total_rows(g * mlp_ref[...]))
        put(B_TWO, total_rows(dmlp.astype(F32)))

    @pl.when(step >= 2)
    def _():
        wait_step(step - 2, slot)

    dmlp = dmlp_ref[...]
    dact = dot(dmlp, w2_ref[...], NT)
    dpre = (dact * slope_ref[...].astype(F32)).astype(B16)
    wide = dot(act_ref[...].T, dmlp, NN)
    for t in range(wide_ref.shape[0]):
        wide_ref[t] = wide[:, t * STRIP : (t + 1) * STRIP]
        for k in range(4):
            at = (k % 2) * width + t * STRIP
            two_ref[slot, k // 2, :, at : at + STRIP] = wide_ref[
                t, pl.ds(k, part_rows, stride=4), :
            ].astype(B16)
    send_two(step, slot)
    one_ref[slot] = dot(h2t_ref[...], dpre, NN).astype(B16)
    send_one(step, slot)
    sums_ref[pl.ds(B_ONE - B_PROJ + step, 1)] = total_rows(dpre.astype(F32))
    part = dot(dpre, w1_ref[...], NT)

    @pl.when(step == 0)
    def _():
        dh2_ref[...] = part

    @pl.when(step > 0)
    def _():
        dh2_ref[...] += part

    @pl.when(step == steps - 1)
    def _():
        x_hat, scale = normalize(mid_ref[...])
        dh2 = dh2_ref[...]
        put(N2_GAIN, total_rows(dh2 * x_hat))
        put(N2_SHIFT, total_rows(dh2))
        dmid = g_ref[...] + normalize_grad(x_hat, scale, dh2 * vec(N2_GAIN))
        dmid_ref[...] = dmid
        dbranch = (dmid * vec(G_ATTN)).astype(B16)
        put(G_ATTN, total_rows(dmid * branch_ref[...]))
        put(B_PROJ, total_rows(dbranch.astype(F32)))
        dproj = dot(att_ref[...].T, dbranch, NN).astype(B16)
        proj_ref[0] = dproj[:, : width // 2]
        proj_ref[1] = dproj[:, width // 2 :]
        on_halves(lambda out_ref, which: proj_copy(out_ref, which).start())
        datt_ref[...] = dot(dbranch, wp_ref[...], NT).astype(B16)
        wait_step(step - 1, 1 - slot)
        wait_step(step, slot)
        for which in range(2):
            proj_copy(mine_ref, which).wait()


def mlp_backward(core, grad, mid, mlp_out, branch, att, small, layer, h2, act, slope, w_proj, w_one,
                 w_two, after=()):
    rows, width = mid.shape
    hidden = w_two.shape[0]
    whole = whole_spec((rows, width))
    cols = pl.BlockSpec((rows, TILE), lambda i: (0, i))
    proj_at = w_proj[1]
    return pl.pallas_call(
        mlp_grad_kernel,
        grid=(hidden // TILE,),
        out_shape=(
            jax.ShapeDtypeStruct((width, hidden + width // 2), B16),
            jax.ShapeDtypeStruct((width, hidden + width // 2), B16),
            jax.ShapeDtypeStruct((rows, width), F32),
            jax.ShapeDtypeStruct((rows, width), B16),
            jax.ShapeDtypeStruct((SUM_ROWS, width), F32),
        ),
        in_specs=[
            SMEM, whole, whole, whole, whole, whole, small_spec(layer), whole, cols, cols,
            pl.BlockSpec((width, TILE), lambda i: (0, proj_at)),
            col_spec(w_one),
            pl.BlockSpec((TILE, width), lambda i: (i, 0)),
        ]
        + [ANY] * len(after),
        out_specs=(ANY, ANY, whole, whole, whole_spec((SUM_ROWS, width))),
        scratch_shapes=[
            pltpu.VMEM((rows, width), B16),
            pltpu.VMEM((width, rows), B16),
            pltpu.VMEM((rows, width), F32),
            pltpu.VMEM((2, width, TILE), B16),
            pltpu.VMEM((width // STRIP, TILE, STRIP), F32),
            pltpu.VMEM((2, 2, TILE // 4, 2 * width), B16),
            pltpu.VMEM((2, width, width // 2), B16),
            pltpu.SemaphoreType.DMA((4, 2)),
        ],
        compiler_params=params(),
        cost_estimate=cost(20),
        name="mlp_grad",
    )(core, grad, mid, mlp_out, branch, att, small, h2, act, slope, w_proj[0], w_one[0], w_two, *after)


CHIP_Y, CORES, CHIP_Z, CHIP_X = 2, 2, 4, 2
FAST_SHARDS = CHIP_Y * CORES * CHIP_Z * CHIP_X

def place(y, c, z, x):
    return (y * CORES + c) * (CHIP_Z * CHIP_X) + z * CHIP_X + x

def moves(fn):
    pairs = []
    for y in range(CHIP_Y):
        for c in range(CORES):
            for z in range(CHIP_Z):
                for x in range(CHIP_X):
                    pairs.append((place(y, c, z, x), place(*fn(y, c, z, x))))
    return pairs

CORE_SWAP = moves(lambda y, c, z, x: (y, 1 - c, z, x))
PLANE = (
    moves(lambda y, c, z, x: (y, c, z, 1 - x) if c == 0 else (1 - y, c, z, x)),
    moves(lambda y, c, z, x: (1 - y, c, z, x) if c == 0 else (y, c, z, 1 - x)),
)
X_SWAP = moves(lambda y, c, z, x: (y, c, z, 1 - x))
Y_SWAP = moves(lambda y, c, z, x: (1 - y, c, z, x))
Z_SHIFT = [moves(lambda y, c, z, x, k=k: (y, c, (z + k) % CHIP_Z, x)) for k in range(CHIP_Z)]

def send(v, pairs):
    return lax.ppermute(v, AXES, pairs)

def my_place():
    dp = lax.axis_index("dp"); fs = lax.axis_index("fsdp")
    return dp // CORES, dp % CORES, fs // CHIP_X, fs % CHIP_X

def half_of(v, which):
    h = v.shape[-1] // 2
    return lax.dynamic_slice_in_dim(v, which * h, h, axis=v.ndim - 1)

def no_sooner(arrays):
    zero = jnp.zeros((), B16)
    for v in arrays:
        zero = zero + jnp.minimum(jnp.abs(v[(0,) * v.ndim]), 0).astype(B16)
    return zero


class Gathering:
    def __init__(self, mats):
        self.mats = mats
        _, c, _, _ = my_place()

        def pick(which):
            return jnp.concatenate(
                [half_of(m, which)[i] for m in mats for i in range(m.shape[0])], axis=-1
            )

        self.piece = jnp.stack([pick(c), send(pick(1 - c), CORE_SWAP)])

    def along(self, behind=()):
        piece = self.piece + no_sooner(behind) if behind else self.piece
        self.moved = [send(piece, Z_SHIFT[k]) for k in range(1, CHIP_Z)]
        return self.moved

    def plane(self, behind=()):
        base = jnp.stack([self.piece] + self.moved)
        if behind:
            base = base + no_sooner(behind)
        self.own = [base, send(base, PLANE[0]), send(base, PLANE[1])]
        return self.own

    def far(self, behind=()):
        first = self.own[1] + no_sooner(behind) if behind else self.own[1]
        self.own.append(send(first, PLANE[1]))
        self.other = [send(v, CORE_SWAP) for v in self.own]

    def finish(self, after=()):
        return assemble(self.own, self.other, self.mats, after)


def assemble_kernel(counts, widths, pos_ref, *refs):
    src = refs[:8]; outs = refs[-1 - len(counts):-1]; sem = refs[-1]
    y, c, z, x = (pos_ref[i] for i in range(4))
    copies = []
    for side in range(2):
        core = c if side == 0 else 1 - c
        for a in range(4):
            for e in range(4):
                f1, f2 = a & 1, a >> 1
                fx = jnp.where(core == 0, f1, f2)
                fy = jnp.where(core == 0, f2, f1)
                yy = (y + fy) % 2
                xx = (x + fx) % 2
                zz = (z + CHIP_Z - e) % CHIP_Z
                for dc in range(2):
                    cc = core if dc == 0 else 1 - core
                    d = place(yy, cc, zz, xx)
                    col = 0
                    for out, count, w in zip(outs, counts, widths):
                        for k in range(count):
                            cp = pltpu.make_async_copy(
                                src[side * 4 + a].at[e, dc, :, pl.ds(col, w)],
                                out.at[d, k, :, pl.ds(pl.multiple_of(core * w, 128), w)],
                                sem,
                            )
                            cp.start(); copies.append(cp)
                            col += w
    for cp in copies:
        cp.wait()

def assemble(own, other, mats, after=()):
    rows = mats[0].shape[1]
    counts = [m.shape[0] for m in mats]; widths = [m.shape[2] // 2 for m in mats]
    pos = jnp.stack([p.astype(jnp.int32) for p in my_place()])
    return pl.pallas_call(
        functools.partial(assemble_kernel, counts, widths),
        out_shape=[jax.ShapeDtypeStruct((FAST_SHARDS, n, rows, 2 * w), B16) for n, w in zip(counts, widths)],
        in_specs=[pl.BlockSpec(memory_space=pltpu.SMEM)] + [ANY] * (8 + len(after)),
        out_specs=[pl.BlockSpec(memory_space=pltpu.VMEM)] * len(counts),
        scratch_shapes=[pltpu.SemaphoreType.DMA],
        compiler_params=params(),
        cost_estimate=cost(7),
        name="assemble",
    )(pos, *own, *other, *after)


def sum_plane(v, behind=()):
    v = v + send(v, CORE_SWAP)
    v = v + send(v, X_SWAP)
    if behind:
        v = v + no_sooner(behind).astype(v.dtype)
    return v + send(v, Y_SWAP)


class Reduction:
    def __init__(self, theirs, mine):
        self.theirs = theirs
        self.own = mine
        self.y, self.c, self.z, self.x = my_place()
        self.split = (CHIP_Y, CORES, CHIP_Z, CHIP_X, mine.shape[0] // FAST_SHARDS)

    def swap(self):
        self.got = send(self.theirs, CORE_SWAP)
        return [self.got]

    def part(self, f1, f2):
        c = self.c
        fx = jnp.where(c == 0, f1, f2)
        fy = jnp.where(c == 0, f2, f1)

        def cut(v):
            v = v.reshape(self.split + (v.shape[-1],))
            at = ((self.y + fy) % CHIP_Y, 0, 0, (self.x + fx) % CHIP_X, 0, 0)
            size = (1, CORES, CHIP_Z, 1) + v.shape[4:]
            return lax.dynamic_slice(v, at, size)[0, :, :, 0].transpose(1, 0, 2, 3).astype(F32)

        own, got = lax.optimization_barrier((self.own, self.got))
        return cut(own) + cut(got)

    def far(self):
        self.r3 = send(self.part(1, 1).astype(B16), PLANE[1])
        return [self.r3]

    def side(self):
        self.r2 = send(self.part(0, 1).astype(B16), PLANE[1])
        return [self.r2]

    def near(self):
        self.r1 = send((self.part(1, 0) + self.r3.astype(F32)).astype(B16), PLANE[0])
        return [self.r1]

    def along(self):
        base = self.part(0, 0) + self.r2.astype(F32) + self.r1.astype(F32)

        def at_z(k):
            return lax.dynamic_slice_in_dim(base, (self.z + k) % CHIP_Z, 1, axis=0)[0]

        self.mine = at_z(0)
        self.rz = [send(at_z(k).astype(B16), Z_SHIFT[k]) for k in range(1, CHIP_Z)]
        return self.rz

    def finish(self, behind=()):
        total = self.mine + no_sooner(behind).astype(F32) if behind else self.mine
        for r in self.rz:
            total = total + r.astype(F32)
        c = self.c
        keep = lax.dynamic_slice_in_dim(total, c, 1, axis=0)[0]
        give = lax.dynamic_slice_in_dim(total, 1 - c, 1, axis=0)[0]
        other = send(give, CORE_SWAP)
        first = jnp.where(c == 0, keep, other)
        second = jnp.where(c == 0, other, keep)
        return first, second


def unpack_kernel(first, src_ref, *refs):
    out_ref, sem = refs[-2:]
    shards, ratio, _, width = out_ref.shape
    copies = []
    for d in range(shards):
        for k in range(ratio):
            copy = pltpu.make_async_copy(
                src_ref.at[d, :, pl.ds(first + k * width, width)], out_ref.at[d, k], sem
            )
            copy.start()
            copies.append(copy)
    for copy in copies:
        copy.wait()


def unpack_two(packed, first, ratio, width, after=()):
    shards, rows, _ = packed.shape
    return pl.pallas_call(
        functools.partial(unpack_kernel, first),
        out_shape=jax.ShapeDtypeStruct((shards, ratio, rows, width), B16),
        in_specs=[ANY] * (1 + len(after)),
        out_specs=pl.BlockSpec(memory_space=pltpu.VMEM),
        scratch_shapes=[pltpu.SemaphoreType.DMA],
        compiler_params=params(),
        cost_estimate=cost(5),
        name="unpack",
    )(packed, *after)


def small_offsets(own, entries, device):
    per_row = TILE // (4 * own)
    return own * device, 4 * own * lax.rem(device, per_row), entries * device, device // per_row


def by_row(vectors, hidden, tables):
    row = lax.broadcasted_iota(jnp.int32, vectors.shape, 0)
    return jnp.where(row < B_ONE, vectors, jnp.where(row < TABLE, hidden, tables))


def own_kernel(*refs):
    out_ref, tmp_ref = refs[-2:]
    hidden_ref, table_ref = refs[-4:-2]
    tmp_ref[...] = jnp.zeros_like(tmp_ref)
    for layer in range(LAYERS):
        for i, ref in enumerate(refs[:B_ONE]):
            tmp_ref[layer, i : i + 1, : ref.shape[1]] = ref[layer : layer + 1, :].astype(F32)
        for i in range(B_ONE, TABLE):
            tmp_ref[layer, i : i + 1, : hidden_ref.shape[1]] = hidden_ref[
                layer : layer + 1, :
            ].astype(F32)
        heads, entries = table_ref.shape[1:]
        tmp_ref[layer, TABLE : TABLE + heads, :entries] = table_ref[layer].astype(F32)
    out_ref[...] = tmp_ref[...].astype(B16)


def own_small(vectors, hidden, table):
    whole = pl.BlockSpec(memory_space=pltpu.VMEM)
    return pl.pallas_call(
        own_kernel,
        out_shape=jax.ShapeDtypeStruct((LAYERS, SMALL_ROWS, STRIP), B16),
        in_specs=[whole] * (len(vectors) + 2),
        out_specs=whole,
        scratch_shapes=[pltpu.VMEM((LAYERS, SMALL_ROWS, STRIP), F32)],
        compiler_params=params(),
        cost_estimate=cost(1),
        name="small_own",
    )(*vectors, hidden, table)


def place_kernel(own, entries, device_ref, *refs):
    out_ref = refs[-1]
    row = lax.broadcasted_iota(jnp.int32, (SMALL_ROWS, TILE), 0)
    for layer in range(out_ref.shape[0]):
        total = jnp.zeros((SMALL_ROWS, TILE), F32)
        for k, piece_ref in enumerate(refs[:-1]):
            vec_at, b1_at, tab_at, line = small_offsets(own, entries, device_ref[k])
            piece = piece_ref[layer].astype(F32)
            rest = jnp.zeros((SMALL_ROWS, TILE - piece.shape[1]), F32)
            wide = jnp.concatenate([piece, rest], axis=1)
            hidden = jnp.where(row - B_ONE == line, pltpu.roll(wide, b1_at, 1), 0.0)
            total += by_row(pltpu.roll(wide, vec_at, 1), hidden, pltpu.roll(wide, tab_at, 1))
        out_ref[layer] = total.astype(B16)


def put_small(pieces, devices, own, entries):
    whole = pl.BlockSpec(memory_space=pltpu.VMEM)
    return pl.pallas_call(
        functools.partial(place_kernel, own, entries),
        out_shape=jax.ShapeDtypeStruct(pieces[0].shape[:2] + (TILE,), B16),
        in_specs=[SMEM] + [whole] * len(pieces),
        out_specs=whole,
        compiler_params=params(),
        cost_estimate=cost(1),
        name="small_place",
    )(devices, *pieces)


def collect_kernel(own, entries, device_ref, total_ref, *refs):
    outs = refs[-device_ref.shape[0] :]
    for k, out_ref in enumerate(outs):
        vec_at, b1_at, tab_at, line = small_offsets(own, entries, device_ref[k])

        def turn(v, at):
            return pltpu.roll(v, lax.rem(TILE - at, TILE), 1)

        for layer in range(total_ref.shape[0]):
            total = total_ref[layer]
            hidden = jnp.broadcast_to(total_ref[layer, pl.ds(B_ONE + line, 1), :], total.shape)
            wide = by_row(turn(total, vec_at), turn(hidden, b1_at), turn(total, tab_at))
            out_ref[layer] = wide[:, : out_ref.shape[2]]


def collect(total, devices, own, entries, after=()):
    whole = pl.BlockSpec(memory_space=pltpu.VMEM)
    count = devices.shape[0]
    piece = jax.ShapeDtypeStruct(total.shape[:2] + (STRIP,), F32)
    return pl.pallas_call(
        functools.partial(collect_kernel, own, entries),
        out_shape=[piece] * count,
        in_specs=[SMEM, whole] + [ANY] * len(after),
        out_specs=[whole] * count,
        compiler_params=params(),
        cost_estimate=cost(2),
        name="small_collect",
    )(devices, total, *after)


def pack_kernel(*refs):
    out_ref = refs[-1]
    out_ref[...] = jnp.zeros_like(out_ref)
    for layer in range(LAYERS):
        first, second, table = refs[3 * layer : 3 * layer + 3]
        out_ref[layer, 0:B_PROJ] = first[0:B_PROJ]
        out_ref[layer, B_PROJ:TABLE] = second[0 : TABLE - B_PROJ]
        for head in range(table.shape[0]):
            out_ref[layer, TABLE + head : TABLE + head + 1] = table[head]


def pack_small(parts, after=()):
    whole = pl.BlockSpec(memory_space=pltpu.VMEM)
    return pl.pallas_call(
        pack_kernel,
        out_shape=jax.ShapeDtypeStruct((LAYERS, SMALL_ROWS, TILE), F32),
        in_specs=[whole] * len(parts) + [ANY] * len(after),
        out_specs=whole,
        compiler_params=params(),
        cost_estimate=cost(2),
        name="small_pack",
    )(*parts, *after)


def per_device(
    shards, fast,
    tokens, masked_rows, cotangent, norm1_gain, norm1_bias, qkv_weight, q_bias, v_bias,
    proj_weight, proj_bias, gamma_attn, norm2_gain, norm2_bias, fc1_weight, fc1_bias,
    fc2_weight, fc2_bias, gamma_mlp, rel_table,
):
    vectors = (norm1_gain, norm1_bias, q_bias, v_bias, proj_bias, gamma_attn, norm2_gain,
               norm2_bias, fc2_bias, gamma_mlp)
    width = tokens.shape[1]
    images = masked_rows.shape[0]
    heads, entries = rel_table.shape[1:]
    own = qkv_weight.shape[1]
    ratio = fc2_weight.shape[1] // own
    hidden = fc1_weight.shape[2]
    me = lax.axis_index("dp") * lax.axis_size("fsdp") + lax.axis_index("fsdp")

    def pad_rows(v):
        v = v.astype(F32).reshape(images, IMG_ROWS, width)
        v = jnp.pad(v, ((0, 0), (0, PAD_ROWS - IMG_ROWS), (0, 0)))
        return v.reshape(images * PAD_ROWS, width)

    def cut_rows(v):
        return v.reshape(images, PAD_ROWS, width)[:, :IMG_ROWS].reshape(images * IMG_ROWS, width)

    used = TABLE + heads
    piece = own_small(vectors, fc1_bias, rel_table)
    hops = range(CHIP_Z) if fast else range(1)
    ring = CHIP_Z * CHIP_X

    def along_z(k):
        return (me // ring) * ring + (me + k * CHIP_X) % ring if fast else me

    backs = jnp.stack([along_z(-k) for k in hops]).astype(jnp.int32)
    ahead = jnp.stack([along_z(k) for k in hops]).astype(jnp.int32)
    pieces = [piece] + [send(piece, Z_SHIFT[k]) for k in hops[1:]]
    small = put_small(pieces, backs, own, entries)
    small = (sum_plane(small) if fast else lax.psum(small, AXES)).astype(F32)

    def two_blocks(layer):
        return fc2_weight[layer].reshape(ratio, own, width)

    def fetch_packed(layer, behind=()):
        two = two_blocks(layer)
        block = jnp.concatenate(
            [qkv_weight[layer], proj_weight[layer], fc1_weight[layer]]
            + [two[i] for i in range(ratio)],
            axis=1,
        )
        if behind:
            block = block + no_sooner(behind)
        return lax.all_gather(block, AXES, axis=0, tiled=True)

    if not fast:
        packed_weights = [fetch_packed(layer) for layer in range(LAYERS)]
        bias = build_bias(small, heads)
    else:
        first = Gathering([qkv_weight[0][None], proj_weight[0][None]])
        second = Gathering([fc1_weight[0][None], two_blocks(0)])
        moved = first.along()
        first.plane()
        first.far()
        moved = second.along(moved)
        bias = build_bias(small, heads, [moved[0], moved[2]])
        packed_weights = [None, fetch_packed(1)]
    weights = []
    x = pad_rows(tokens)
    saved = []
    for layer in range(LAYERS):
        full = packed_weights[layer]
        if full is None:
            w_qkv, w_proj = first.finish([bias])
            w_qkv = (w_qkv.reshape(width, 3 * width), 0)
            w_proj = (w_proj.reshape(width, width), 0)
        else:
            w_qkv, w_proj, w_one = (full, 0), (full, 3), (full, 4)
        qkv, h = qkv_forward(x, small, layer, w_qkv)
        qkv = qkv.reshape(images, PAD_ROWS, 3 * width)
        att, lse = attention_forward(qkv, bias, layer)
        att = att.reshape(images * PAD_ROWS, width)
        if full is None:
            second.plane([w_qkv[0]])
            second.far([att])
            w_one, w_two = second.finish()
            w_one = (w_one.reshape(width, hidden), 0)
        elif fast:
            w_two = unpack_two(full.reshape(shards, own, -1), 4 * width + hidden, ratio, width)
        else:
            w_two = full[:, 4 * width + hidden :].reshape(shards, own, ratio, width)
            w_two = w_two.transpose(0, 2, 1, 3)
        w_two = w_two.reshape(hidden, width)
        weights.append((w_qkv, w_proj, w_one, w_two))
        out, branch, mid, mlp_out, h2, act, slope = mlp_forward(
            x, att, small, layer, w_proj, w_one, w_two
        )
        saved.append((x, h, qkv, lse, att, branch, mid, mlp_out, h2, act, slope))
        x = out
    encoded = cut_rows(x.astype(B16))

    positions = jnp.arange(IMG_ROWS, dtype=jnp.int32)
    mask = jnp.any(masked_rows[:, :, None] == positions[None, None, :], axis=1)
    mask = jnp.pad(mask, ((0, 0), (0, PAD_ROWS - IMG_ROWS))).reshape(-1, 1)
    grad = jnp.where(mask, pad_rows(cotangent), 0.0)

    def scatter(theirs, mine):
        both = jnp.stack([mine, theirs])
        own_part = lax.psum_scatter(both, AXES, scatter_dimension=1, tiled=True).astype(F32)
        return own_part[0], own_part[1]

    core = (lax.axis_index("dp") % CORES if fast else jnp.int32(0)).astype(jnp.int32).reshape(1)
    reduced = [None] * LAYERS
    small_grads = [None] * LAYERS
    tables = [None] * LAYERS

    def backward(layer, grad, hooks):
        x, h, qkv, lse, att, branch, mid, mlp_out, h2, act, slope = saved[layer]
        w_qkv, w_proj, w_one, w_two = weights[layer]
        theirs, mine, d_mid, d_att, mlp_sums = mlp_backward(
            core, grad, mid, mlp_out, branch, att, small, layer, h2, act, slope, w_proj, w_one,
            w_two, hooks[0](),
        )
        main = (theirs, mine)
        d_qkv, d_bias = attention_backward(
            qkv, bias, lse, d_att.reshape(images, PAD_ROWS, width), layer, hooks[1](main)
        )
        tables[layer] = d_bias
        theirs, mine, grad, qkv_sums = qkv_backward(
            core, d_qkv.reshape(images * PAD_ROWS, 3 * width), h, x, d_mid, small, layer, w_qkv,
            hooks[2](),
        )
        small_grads[layer] = (qkv_sums, mlp_sums)
        return grad, main, (theirs, mine)

    if not fast:
        for layer in reversed(range(LAYERS)):
            none = (lambda: (), lambda main: (), lambda: ())
            grad, main, rest = backward(layer, grad, none)
            reduced[layer] = (scatter(*main), scatter(*rest))
        tables = [reduce_bias(t) for t in tables]
    else:
        a1, b1, a0, b0 = (None,) * 4

        def one_attention(main):
            nonlocal a1
            a1 = Reduction(*main)
            return ()

        def one_qkv():
            return a1.swap()

        grad, _, rest = backward(1, grad, (lambda: (), one_attention, one_qkv))
        b1 = Reduction(*rest)

        def zero_mlp():
            return a1.far()

        def zero_attention(main):
            nonlocal a0
            a0 = Reduction(*main)
            a0.swap()
            return a1.side() + b1.swap()

        def zero_qkv():
            return a1.near() + b1.far() + a0.far()

        grad, _, rest = backward(0, grad, (zero_mlp, zero_attention, zero_qkv))
        b0 = Reduction(*rest)
        moved = a1.along()
        a0.side()
        a0.near()
        b1.side()
        b0.swap()
        b0.far()
        b0.side()
        tables[1] = reduce_bias(tables[1], [small_grads[0][0]] + moved)
        tables[0] = reduce_bias(tables[0], [tables[1], a0.r1] + b1.near())
        a0.along()
        b1.along()

    parts = []
    for (qkv_sums, mlp_sums), table in zip(small_grads, tables):
        parts += [qkv_sums, mlp_sums, table]
    totals = pack_small(parts, [b0.r3, b0.r2, a0.rz[0]] if fast else ())
    totals = sum_plane(totals, a0.rz) if fast else lax.psum(totals, AXES)
    late = ()
    if fast:
        late = b0.near() + b1.rz
    pieces = collect(totals, ahead, own, entries, late)
    if fast:
        b0.along()
        reduced[1] = (a1.finish([pieces[0]]), b1.finish([pieces[0]]))
        reduced[0] = (a0.finish([pieces[0]]), b0.finish())
    g_small = pieces[0]
    for k in hops[1:]:
        g_small = g_small + send(pieces[k], Z_SHIFT[k])
    g = [g_small[:, i, :own] for i in range(B_ONE)]
    g_b1 = g_small[:, B_ONE, : ratio * own]
    g_table = g_small[:, TABLE:used, :entries]

    def both(pick):
        return jnp.stack([pick(*r) for r in reduced])

    def thirds(low, high):
        half = width // 2
        cols = [v[:, i * half : (i + 1) * half] for i in range(3) for v in (low, high)]
        return jnp.concatenate(cols, axis=1)

    def join(low, high, first, last):
        return jnp.concatenate([low[:, first:last], high[:, first:last]], axis=1)

    half = hidden // 2
    g_qkv = both(lambda a, b: thirds(*b))
    g_one = both(lambda a, b: join(*a, 0, half))
    g_two = both(lambda a, b: join(*a, half, hidden).reshape(ratio * own, width))
    g_proj = both(lambda a, b: join(*a, hidden, hidden + width // 2))
    return (encoded, cut_rows(grad), g[N1_GAIN], g[N1_SHIFT], g_qkv, g[Q_BIAS], g[V_BIAS], g_proj,
            g[B_PROJ], g[G_ATTN], g[N2_GAIN], g[N2_SHIFT], g_one, g_b1, g_two, g[B_TWO], g[G_MLP],
            g_table)


def solution(mesh):
    shards = math.prod(mesh.shape[a] for a in AXES)
    fast = mesh.shape["dp"] == CHIP_Y * CORES and mesh.shape["fsdp"] == CHIP_Z * CHIP_X
    row = P(AXES, None)
    vec = P(None, AXES)
    mat = P(None, AXES, None)
    tab = P(None, None, AXES)
    return jax.shard_map(
        functools.partial(per_device, shards, fast),
        mesh=mesh,
        in_specs=(row, row, row, vec, vec, mat, vec, vec, mat, vec, vec, vec, vec, mat, vec, mat,
                  vec, vec, tab),
        out_specs=(row, row, vec, vec, mat, vec, vec, mat, vec, vec, vec, vec, mat, vec, mat,
                   vec, vec, tab),
        check_vma=False,
    )
```

```python
import functools
import math

import jax
import jax.numpy as jnp
import numpy as np
from jax import lax
from jax.experimental import pallas as pl
from jax.experimental.pallas import tpu as pltpu
from jax.sharding import PartitionSpec as P

GRID = 14
SPAN = 2 * GRID - 1
LAYERS = 2
IMG_ROWS = GRID * GRID + 1
PAD_ROWS = 208
LANES = 256
HEAD = 64
PAIR = 2 * HEAD
NEG = -1e30
TILE = 768
WIDE = 384
GROUP = 4
BLOCK = 16
SMALL_ROWS = 32
F32 = jnp.float32
B16 = jnp.bfloat16
AXES = ("dp", "fsdp")


def cost(us):
    return pl.CostEstimate(flops=us * 4_400_000_000, bytes_accessed=us * 14_000_000, transcendentals=0)


ANY = pl.BlockSpec(memory_space=pl.ANY)
SMEM = pl.BlockSpec(memory_space=pltpu.SMEM)

N1_GAIN, N1_SHIFT, Q_BIAS, V_BIAS, B_PROJ, G_ATTN, N2_GAIN, N2_SHIFT, B_TWO, G_MLP = range(10)
B_ONE = 10
TABLE = 14


def params(limit=56):
    return pltpu.CompilerParams(vmem_limit_bytes=limit * 1024 * 1024)


def dot(a, b, dims):
    return lax.dot_general(a, b, (dims, ((), ())), preferred_element_type=F32)


NN = ((1,), (0,))
NT = ((1,), (1,))
TN = ((0,), (0,))


def lane_onehot():
    out = np.zeros((WIDE, LANES), np.float32)
    for a in range(GRID):
        for b in range(GRID):
            out[SPAN * a + b, 1 + GRID * a + b] = 1.0
    return out


def row_onehot(turned):
    out = np.zeros((PAD_ROWS, BLOCK * GRID), np.float32)
    for c in range(GRID):
        for d in range(GRID):
            out[1 + GRID * c + d, BLOCK * c + (GRID - 1 - d if turned else d)] = 1.0
    return out


def bias_kernel(small_ref, rows_ref, lanes_ref, *refs):
    out_ref, wide_ref = refs[-2:]
    first = pl.program_id(0) * GROUP
    for i in range(GROUP):
        table = small_ref[0, pl.ds(TABLE + first + i, 1), :]
        one_bias(table, rows_ref, lanes_ref, out_ref.at[i], wide_ref.at[i])


def one_bias(table, rows_ref, lanes_ref, out_ref, wide_ref):
    shifted = pltpu.roll(jnp.broadcast_to(table, (BLOCK, TILE)), TILE - (GRID - 1), 1)
    shifted = pltpu.roll(shifted, 0, 1, stride=1, stride_axis=0)
    for c in range(GRID):
        start = SPAN * (GRID - 1 - c)
        wide_ref[BLOCK * c : BLOCK * (c + 1), :] = shifted[:, start : start + WIDE].astype(B16)
    narrow = dot(wide_ref[...], lanes_ref[...], NN).astype(B16)
    val = dot(rows_ref[...], narrow, NN)
    row = lax.broadcasted_iota(jnp.int32, (PAD_ROWS, LANES), 0)
    lane = lax.broadcasted_iota(jnp.int32, (PAD_ROWS, LANES), 1)
    cls = SPAN * SPAN
    val = jnp.where(lane == 0, table[:, cls : cls + 1], val)
    first = jnp.where(lane == 0, table[:, cls + 2 : cls + 3], table[:, cls + 1 : cls + 2])
    val = jnp.where(row == 0, first, val)
    out_ref[...] = jnp.where(row >= IMG_ROWS, NEG, val)


def build_bias(small, layer, heads, after=()):
    return pl.pallas_call(
        bias_kernel,
        grid=(heads // GROUP,),
        out_shape=jax.ShapeDtypeStruct((heads, PAD_ROWS, LANES), F32),
        in_specs=[
            pl.BlockSpec((1, SMALL_ROWS, TILE), lambda h: (layer, 0, 0)),
            pl.BlockSpec((PAD_ROWS, BLOCK * GRID), lambda h: (0, 0)),
            pl.BlockSpec((WIDE, LANES), lambda h: (0, 0)),
        ]
        + [ANY] * len(after),
        out_specs=pl.BlockSpec((GROUP, PAD_ROWS, LANES), lambda h: (h, 0, 0)),
        scratch_shapes=[pltpu.VMEM((GROUP, BLOCK * GRID, WIDE), B16)],
        compiler_params=params(),
        cost_estimate=cost(5),
        name="bias_expand",
    )(small, jnp.asarray(row_onehot(False), B16), jnp.asarray(lane_onehot(), B16), *after)


def bias_grad_kernel(g_ref, rows_ref, lanes_ref, *refs):
    out_ref, acc_ref = refs[-2:]
    for i in range(GROUP):
        one_bias_grad(g_ref.at[i], rows_ref, lanes_ref, out_ref.at[i], acc_ref.at[i])


def one_bias_grad(g_ref, rows_ref, lanes_ref, out_ref, acc_ref):
    row = lax.broadcasted_iota(jnp.int32, (PAD_ROWS, LANES), 0)
    lane = lax.broadcasted_iota(jnp.int32, (PAD_ROWS, LANES), 1)
    g = jnp.where((lane < IMG_ROWS) & (row < IMG_ROWS), g_ref[...], 0.0)
    high = g.astype(B16)
    wide = None
    for part in (high, (g - high.astype(F32)).astype(B16)):
        moved = dot(rows_ref[...], part, NN).astype(B16)
        moved = dot(moved, lanes_ref[...], NN)
        wide = moved if wide is None else wide + moved
    acc_ref[...] = jnp.zeros_like(acc_ref)
    for c in range(GRID):
        start = SPAN * (GRID - 1 - c)
        acc_ref[:, start : start + WIDE] += wide[BLOCK * c : BLOCK * (c + 1), :]
    turned = pltpu.roll(acc_ref[...], 0, 1, stride=1, stride_axis=0)
    total = jnp.sum(turned, axis=0, keepdims=True)
    column = jnp.sum(jnp.where(lane[:, :1] == 0, g[:, :1], 0.0), axis=0, keepdims=True)
    to_self = g[0:1, 0:1]
    to_patch = column - to_self
    from_patch = jnp.sum(g[0:1, :], axis=1, keepdims=True) - to_self
    spot = lax.broadcasted_iota(jnp.int32, (1, TILE), 1)
    cls = SPAN * SPAN
    total = jnp.where(spot == cls, to_patch, total)
    total = jnp.where(spot == cls + 1, from_patch, total)
    out_ref[...] = jnp.where(spot == cls + 2, to_self, total)


def reduce_bias(grad, after=()):
    heads = grad.shape[0]
    out = pl.pallas_call(
        bias_grad_kernel,
        grid=(heads // GROUP,),
        out_shape=jax.ShapeDtypeStruct((heads, 1, TILE), F32),
        in_specs=[
            pl.BlockSpec((GROUP, PAD_ROWS, LANES), lambda h: (h, 0, 0)),
            pl.BlockSpec((BLOCK * GRID, PAD_ROWS), lambda h: (0, 0)),
            pl.BlockSpec((LANES, WIDE), lambda h: (0, 0)),
        ]
        + [ANY] * len(after),
        out_specs=pl.BlockSpec((GROUP, 1, TILE), lambda h: (h, 0, 0)),
        scratch_shapes=[pltpu.VMEM((GROUP, BLOCK, TILE), F32)],
        compiler_params=params(),
        cost_estimate=cost(6),
        name="bias_reduce",
    )(grad, jnp.asarray(row_onehot(True).T, B16), jnp.asarray(lane_onehot().T, B16), *after)
    return out


def head_mask(which):
    lane = lax.broadcasted_iota(jnp.int32, (PAD_ROWS, PAIR), 1)
    return (lane < HEAD) if which == 0 else (lane >= HEAD)


def attention_kernel(width, qkv_ref, bias_ref, out_ref, lse_ref):
    heads = width // HEAD
    for pair in range(heads // 2):
        at = pair * PAIR
        q = qkv_ref[0, :, at : at + PAIR]
        k = qkv_ref[0, :, width + at : width + at + PAIR]
        v = qkv_ref[0, :, 2 * width + at : 2 * width + at + PAIR]
        q = q * jnp.asarray(HEAD ** (-0.5), B16)
        v_t = v.T
        parts = []
        for t in range(2):
            head = 2 * pair + t
            q_t = jnp.where(head_mask(t), q, jnp.zeros_like(q))
            scores = dot(k, q_t, NT) + bias_ref[head, :, 0:PAD_ROWS]
            top = jnp.max(scores, axis=0, keepdims=True)
            weights = jnp.exp(scores - top)
            total = jnp.sum(weights, axis=0, keepdims=True)
            probs = (weights * (1.0 / total)).astype(B16)
            lse_ref[0, head : head + 1, 0:PAD_ROWS] = top + jnp.log(total)
            parts.append(dot(v_t[t * HEAD : (t + 1) * HEAD], probs, NN))
        out_ref[0, :, at : at + PAIR] = jnp.concatenate(parts, axis=0).T.astype(B16)


def attention_forward(qkv, bias):
    images = qkv.shape[0]
    width = qkv.shape[2] // 3
    heads = width // HEAD
    return pl.pallas_call(
        functools.partial(attention_kernel, width),
        grid=(images,),
        out_shape=(
            jax.ShapeDtypeStruct((images, PAD_ROWS, width), B16),
            jax.ShapeDtypeStruct((images, 16, LANES), F32),
        ),
        in_specs=[
            pl.BlockSpec((1, PAD_ROWS, 3 * width), lambda i: (i, 0, 0)),
            pl.BlockSpec((heads, PAD_ROWS, LANES), lambda i: (0, 0, 0)),
        ],
        out_specs=(
            pl.BlockSpec((1, PAD_ROWS, width), lambda i: (i, 0, 0)),
            pl.BlockSpec((1, 16, LANES), lambda i: (i, 0, 0)),
        ),
        compiler_params=params(),
        cost_estimate=cost(8),
        name="attention",
    )(qkv, bias)


def attention_grad_kernel(width, qkv_ref, bias_ref, lse_ref, g_ref, *refs):
    out_ref, dbias_ref = refs[-2:]
    heads = width // HEAD
    scale = HEAD ** (-0.5)

    @pl.when(pl.program_id(0) == 0)
    def _():
        dbias_ref[...] = jnp.zeros_like(dbias_ref)

    for pair in range(heads // 2):
        at = pair * PAIR
        q = qkv_ref[0, :, at : at + PAIR]
        k = qkv_ref[0, :, width + at : width + at + PAIR]
        v = qkv_ref[0, :, 2 * width + at : 2 * width + at + PAIR]
        g = g_ref[0, :, at : at + PAIR]
        q = q * jnp.asarray(scale, B16)
        k_t = k.T
        dq_parts = []
        dk = None
        dv = None
        for t in range(2):
            head = 2 * pair + t
            q_t = jnp.where(head_mask(t), q, jnp.zeros_like(q))
            g_t = jnp.where(head_mask(t), g, jnp.zeros_like(g))
            scores = dot(k, q_t, NT) + bias_ref[head, :, 0:PAD_ROWS]
            probs = jnp.exp(scores - lse_ref[0, head : head + 1, 0:PAD_ROWS])
            dprobs = dot(v, g_t, NT)
            dv_t = dot(probs.astype(B16), g_t, NN)
            mean = jnp.sum(probs * dprobs, axis=0, keepdims=True)
            dscores = (probs * (dprobs - mean)).astype(B16)
            dbias_ref[head, :, 0:PAD_ROWS] += dscores.astype(F32)
            dk_t = dot(dscores, q_t, NN)
            dq_parts.append(dot(k_t[t * HEAD : (t + 1) * HEAD], dscores, NN))
            dk = dk_t if dk is None else dk + dk_t
            dv = dv_t if dv is None else dv + dv_t
        dq = jnp.concatenate(dq_parts, axis=0).T * scale
        out_ref[0, :, at : at + PAIR] = dq.astype(B16)
        out_ref[0, :, width + at : width + at + PAIR] = dk.astype(B16)
        out_ref[0, :, 2 * width + at : 2 * width + at + PAIR] = dv.astype(B16)


def attention_backward(qkv, bias, lse, grad, after=()):
    images = qkv.shape[0]
    width = qkv.shape[2] // 3
    heads = width // HEAD
    return pl.pallas_call(
        functools.partial(attention_grad_kernel, width),
        grid=(images,),
        out_shape=(
            jax.ShapeDtypeStruct((images, PAD_ROWS, 3 * width), B16),
            jax.ShapeDtypeStruct((heads, PAD_ROWS, LANES), F32),
        ),
        in_specs=[
            pl.BlockSpec((1, PAD_ROWS, 3 * width), lambda i: (i, 0, 0)),
            pl.BlockSpec((heads, PAD_ROWS, LANES), lambda i: (0, 0, 0)),
            pl.BlockSpec((1, 16, LANES), lambda i: (i, 0, 0)),
            pl.BlockSpec((1, PAD_ROWS, width), lambda i: (i, 0, 0)),
        ]
        + [ANY] * len(after),
        out_specs=(
            pl.BlockSpec((1, PAD_ROWS, 3 * width), lambda i: (i, 0, 0)),
            pl.BlockSpec((heads, PAD_ROWS, LANES), lambda i: (0, 0, 0)),
        ),
        compiler_params=params(),
        cost_estimate=cost(12),
        name="attention_grad",
    )(qkv, bias, lse, grad, *after)


def normalize(x):
    centered = x - jnp.mean(x, -1, keepdims=True)
    scale = lax.rsqrt(jnp.mean(centered * centered, -1, keepdims=True) + 1e-06)
    return centered * scale, scale


def normalize_grad(x_hat, scale, dy):
    return scale * (
        dy - jnp.mean(dy, -1, keepdims=True) - x_hat * jnp.mean(dy * x_hat, -1, keepdims=True)
    )


def gelu_and_slope(x):
    t = 1.0 / (1.0 + (0.3275911 / math.sqrt(2.0)) * jnp.abs(x))
    bell = jnp.exp(-0.5 * x * x)
    poly = 0.5 * 1.061405429
    for coef in (-1.453152027, 1.421413741, -0.284496736, 0.254829592):
        poly = poly * t + 0.5 * coef
    tail = poly * t * bell
    phi = jnp.where(x >= 0, 1.0 - tail, tail)
    return x * phi, phi + x * bell * (1.0 / math.sqrt(2.0 * math.pi))


def total_rows(v):
    return jnp.sum(v, axis=0, keepdims=True)


def small_spec(layer):
    return pl.BlockSpec((1, SMALL_ROWS, TILE), lambda i: (layer, 0, 0))


def whole_spec(shape):
    return pl.BlockSpec(shape, lambda i: (0,) * len(shape))


def col_spec(weight):
    array, first = weight
    return pl.BlockSpec((array.shape[0], TILE), lambda i: (0, first + i))


def qkv_kernel(x_ref, small_ref, w_ref, qkv_ref, h_ref):
    step = pl.program_id(0)

    @pl.when(step == 0)
    def _():
        x_hat, _ = normalize(x_ref[...])
        gain = small_ref[0, N1_GAIN : N1_GAIN + 1]
        h_ref[...] = (x_hat * gain + small_ref[0, N1_SHIFT : N1_SHIFT + 1]).astype(B16)

    zero = jnp.zeros((1, TILE), F32)
    bias = jnp.where(step == 0, small_ref[0, Q_BIAS : Q_BIAS + 1], zero)
    bias = jnp.where(step == 2, small_ref[0, V_BIAS : V_BIAS + 1], bias)
    qkv_ref[...] = (dot(h_ref[...], w_ref[...], NN) + bias).astype(B16)


def qkv_forward(x, small, layer, w_qkv):
    rows, width = x.shape
    return pl.pallas_call(
        qkv_kernel,
        grid=(3,),
        out_shape=(
            jax.ShapeDtypeStruct((rows, 3 * width), B16),
            jax.ShapeDtypeStruct((rows, width), B16),
        ),
        in_specs=[whole_spec((rows, width)), small_spec(layer), col_spec(w_qkv)],
        out_specs=(
            pl.BlockSpec((rows, TILE), lambda i: (0, i)),
            whole_spec((rows, width)),
        ),
        compiler_params=params(),
        cost_estimate=cost(6),
        name="qkv",
    )(x, small, w_qkv[0])


def qkv_grad_kernel(core_ref, g_ref, h_ref, x_ref, dmid_ref, small_ref, w_ref, *refs):
    theirs_ref, mine_ref, dx_ref, sums_ref, ht_ref, dh_ref = refs[-6:]
    step = pl.program_id(0)

    @pl.when(step == 0)
    def _():
        ht_ref[...] = h_ref[...].T
        sums_ref[...] = jnp.zeros_like(sums_ref)

    g = g_ref[...]
    dw = dot(ht_ref[...], g, NN).astype(B16)
    low, high = dw[:, : TILE // 2], dw[:, TILE // 2 :]

    @pl.when(core_ref[0] == 0)
    def _():
        mine_ref[...] = low
        theirs_ref[...] = high

    @pl.when(core_ref[0] != 0)
    def _():
        mine_ref[...] = high
        theirs_ref[...] = low

    part = dot(g, w_ref[...], NT)
    total = total_rows(g.astype(F32))

    @pl.when(step == 0)
    def _():
        dh_ref[...] = part
        sums_ref[Q_BIAS : Q_BIAS + 1] = total

    @pl.when(step > 0)
    def _():
        dh_ref[...] += part

    @pl.when(step == 2)
    def _():
        sums_ref[V_BIAS : V_BIAS + 1] = total
        dh = dh_ref[...]
        x_hat, scale = normalize(x_ref[...])
        sums_ref[N1_GAIN : N1_GAIN + 1] = total_rows(dh * x_hat)
        sums_ref[N1_SHIFT : N1_SHIFT + 1] = total_rows(dh)
        gain = small_ref[0, N1_GAIN : N1_GAIN + 1]
        dx_ref[...] = dmid_ref[...] + normalize_grad(x_hat, scale, dh * gain)


def qkv_backward(core, grad, h, x, d_mid, small, layer, w_qkv, after=()):
    rows, width = x.shape
    whole = whole_spec((rows, width))
    tiles = pl.BlockSpec((rows, TILE), lambda i: (0, i))
    return pl.pallas_call(
        qkv_grad_kernel,
        grid=(3,),
        out_shape=(
            jax.ShapeDtypeStruct((width, 3 * width // 2), B16),
            jax.ShapeDtypeStruct((width, 3 * width // 2), B16),
            jax.ShapeDtypeStruct((rows, width), F32),
            jax.ShapeDtypeStruct((8, width), F32),
        ),
        in_specs=[SMEM, tiles, whole, whole, whole, small_spec(layer), col_spec(w_qkv)]
        + [ANY] * len(after),
        out_specs=(
            pl.BlockSpec((width, TILE // 2), lambda i: (0, i)),
            pl.BlockSpec((width, TILE // 2), lambda i: (0, i)),
            whole,
            whole_spec((8, width)),
        ),
        scratch_shapes=[pltpu.VMEM((width, rows), B16), pltpu.VMEM((rows, width), F32)],
        compiler_params=params(),
        cost_estimate=cost(11),
        name="qkv_grad",
    )(core, grad, h, x, d_mid, small, w_qkv[0], *after)


def mlp_kernel(
    x_ref, att_ref, small_ref, wp_ref, w1_ref, w2_ref,
    out_ref, branch_ref, mid_ref, mlp_ref, h2_ref, act_ref, slope_ref,
):
    step = pl.program_id(0)

    def vec(i):
        return small_ref[0, i : i + 1]

    @pl.when(step == 0)
    def _():
        branch = dot(att_ref[...], wp_ref[...], NN) + vec(B_PROJ)
        branch_ref[...] = branch
        mid = x_ref[...] + vec(G_ATTN) * branch
        mid_ref[...] = mid
        x_hat, _ = normalize(mid)
        h2_ref[...] = (x_hat * vec(N2_GAIN) + vec(N2_SHIFT)).astype(B16)

    pre = dot(h2_ref[...], w1_ref[...], NN) + small_ref[0, pl.ds(B_ONE + step, 1)]
    act, slope = gelu_and_slope(pre)
    act = act.astype(B16)
    act_ref[...] = act
    slope_ref[...] = slope.astype(B16)
    part = dot(act, w2_ref[...], NN)

    @pl.when(step == 0)
    def _():
        mlp_ref[...] = part + vec(B_TWO)

    @pl.when(step > 0)
    def _():
        mlp_ref[...] += part

    @pl.when(step == pl.num_programs(0) - 1)
    def _():
        out_ref[...] = mid_ref[...] + vec(G_MLP) * mlp_ref[...]


def mlp_forward(x, att, small, layer, w_proj, w_one, w_two):
    rows, width = x.shape
    hidden = w_two.shape[0]
    whole = whole_spec((rows, width))
    cols = pl.BlockSpec((rows, TILE), lambda i: (0, i))
    full = jax.ShapeDtypeStruct((rows, width), F32)
    proj_at = w_proj[1]
    return pl.pallas_call(
        mlp_kernel,
        grid=(hidden // TILE,),
        out_shape=(
            full, full, full, full,
            jax.ShapeDtypeStruct((rows, width), B16),
            jax.ShapeDtypeStruct((rows, hidden), B16),
            jax.ShapeDtypeStruct((rows, hidden), B16),
        ),
        in_specs=[
            whole,
            whole,
            small_spec(layer),
            pl.BlockSpec((width, TILE), lambda i: (0, proj_at)),
            col_spec(w_one),
            pl.BlockSpec((TILE, width), lambda i: (i, 0)),
        ],
        out_specs=(whole, whole, whole, whole, whole, cols, cols),
        compiler_params=params(),
        cost_estimate=cost(15),
        name="mlp",
    )(x, att, small, w_proj[0], w_one[0], w_two)


SUM_ROWS = 16
STRIP = 128


def mlp_grad_kernel(
    core_ref, g_ref, mid_ref, mlp_ref, branch_ref, att_ref, small_ref, h2_ref, act_ref, slope_ref, wp_ref,
    w1_ref, w2_ref, *refs,
):
    (theirs_ref, mine_ref, dmid_ref, datt_ref, sums_ref,
     dmlp_ref, h2t_ref, dh2_ref, one_ref, wide_ref, two_ref, proj_ref, sems) = refs[-13:]
    step = pl.program_id(0)
    steps = pl.num_programs(0)
    slot = lax.rem(step, 2)
    width = mid_ref.shape[1]
    hidden = 4 * width
    part_rows = TILE // 4

    def vec(i):
        return small_ref[0, i : i + 1]

    def put(row, value):
        at = row - B_PROJ
        sums_ref[at : at + 1] = value

    def copy_one(out_ref, j, s):
        return pltpu.make_async_copy(
            one_ref.at[s],
            out_ref.at[:, pl.ds(pl.multiple_of(lax.rem(j, 2) * TILE, TILE), TILE)],
            sems.at[0, s],
        )

    def copy_two(out_ref, j, s, which):
        return pltpu.make_async_copy(
            two_ref.at[s, which],
            out_ref.at[pl.ds(pl.multiple_of(j * part_rows, part_rows), part_rows),
                       pl.ds(2 * width, 2 * width)],
            sems.at[1 + which, s],
        )

    def proj_copy(out_ref, which):
        return pltpu.make_async_copy(
            proj_ref.at[which], out_ref.at[:, pl.ds(4 * width, width // 2)], sems.at[3, which]
        )

    def on_halves(run):
        for core in range(2):

            @pl.when(core_ref[0] == core)
            def _(core=core):
                run(mine_ref, core)
                run(theirs_ref, 1 - core)

    def send_one(j, s):
        def run(out_ref, which):
            @pl.when(j // 2 == which)
            def _():
                copy_one(out_ref, j, s).start()

        on_halves(run)

    def send_two(j, s):
        on_halves(lambda out_ref, which: copy_two(out_ref, j, s, which).start())

    def wait_step(j, s):
        copy_one(mine_ref, j, s).wait()
        for which in range(2):
            copy_two(mine_ref, j, s, which).wait()

    @pl.when(step == 0)
    def _():
        g = g_ref[...]
        dmlp = (g * vec(G_MLP)).astype(B16)
        dmlp_ref[...] = dmlp
        h2t_ref[...] = h2_ref[...].T
        sums_ref[...] = jnp.zeros_like(sums_ref)
        put(G_MLP, total_rows(g * mlp_ref[...]))
        put(B_TWO, total_rows(dmlp.astype(F32)))

    @pl.when(step >= 2)
    def _():
        wait_step(step - 2, slot)

    dmlp = dmlp_ref[...]
    dact = dot(dmlp, w2_ref[...], NT)
    dpre = (dact * slope_ref[...].astype(F32)).astype(B16)
    wide = dot(act_ref[...].T, dmlp, NN)
    for t in range(wide_ref.shape[0]):
        wide_ref[t] = wide[:, t * STRIP : (t + 1) * STRIP]
        for k in range(4):
            at = (k % 2) * width + t * STRIP
            two_ref[slot, k // 2, :, at : at + STRIP] = wide_ref[
                t, pl.ds(k, part_rows, stride=4), :
            ].astype(B16)
    send_two(step, slot)
    one_ref[slot] = dot(h2t_ref[...], dpre, NN).astype(B16)
    send_one(step, slot)
    sums_ref[pl.ds(B_ONE - B_PROJ + step, 1)] = total_rows(dpre.astype(F32))
    part = dot(dpre, w1_ref[...], NT)

    @pl.when(step == 0)
    def _():
        dh2_ref[...] = part

    @pl.when(step > 0)
    def _():
        dh2_ref[...] += part

    @pl.when(step == steps - 1)
    def _():
        x_hat, scale = normalize(mid_ref[...])
        dh2 = dh2_ref[...]
        put(N2_GAIN, total_rows(dh2 * x_hat))
        put(N2_SHIFT, total_rows(dh2))
        dmid = g_ref[...] + normalize_grad(x_hat, scale, dh2 * vec(N2_GAIN))
        dmid_ref[...] = dmid
        dbranch = (dmid * vec(G_ATTN)).astype(B16)
        put(G_ATTN, total_rows(dmid * branch_ref[...]))
        put(B_PROJ, total_rows(dbranch.astype(F32)))
        dproj = dot(att_ref[...].T, dbranch, NN).astype(B16)
        proj_ref[0] = dproj[:, : width // 2]
        proj_ref[1] = dproj[:, width // 2 :]
        on_halves(lambda out_ref, which: proj_copy(out_ref, which).start())
        datt_ref[...] = dot(dbranch, wp_ref[...], NT).astype(B16)
        wait_step(step - 1, 1 - slot)
        wait_step(step, slot)
        for which in range(2):
            proj_copy(mine_ref, which).wait()


def mlp_backward(core, grad, mid, mlp_out, branch, att, small, layer, h2, act, slope, w_proj, w_one,
                 w_two, after=()):
    rows, width = mid.shape
    hidden = w_two.shape[0]
    whole = whole_spec((rows, width))
    cols = pl.BlockSpec((rows, TILE), lambda i: (0, i))
    proj_at = w_proj[1]
    return pl.pallas_call(
        mlp_grad_kernel,
        grid=(hidden // TILE,),
        out_shape=(
            jax.ShapeDtypeStruct((width, hidden + width // 2), B16),
            jax.ShapeDtypeStruct((width, hidden + width // 2), B16),
            jax.ShapeDtypeStruct((rows, width), F32),
            jax.ShapeDtypeStruct((rows, width), B16),
            jax.ShapeDtypeStruct((SUM_ROWS, width), F32),
        ),
        in_specs=[
            SMEM, whole, whole, whole, whole, whole, small_spec(layer), whole, cols, cols,
            pl.BlockSpec((width, TILE), lambda i: (0, proj_at)),
            col_spec(w_one),
            pl.BlockSpec((TILE, width), lambda i: (i, 0)),
        ]
        + [ANY] * len(after),
        out_specs=(ANY, ANY, whole, whole, whole_spec((SUM_ROWS, width))),
        scratch_shapes=[
            pltpu.VMEM((rows, width), B16),
            pltpu.VMEM((width, rows), B16),
            pltpu.VMEM((rows, width), F32),
            pltpu.VMEM((2, width, TILE), B16),
            pltpu.VMEM((width // STRIP, TILE, STRIP), F32),
            pltpu.VMEM((2, 2, TILE // 4, 2 * width), B16),
            pltpu.VMEM((2, width, width // 2), B16),
            pltpu.SemaphoreType.DMA((4, 2)),
        ],
        compiler_params=params(),
        cost_estimate=cost(20),
        name="mlp_grad",
    )(core, grad, mid, mlp_out, branch, att, small, h2, act, slope, w_proj[0], w_one[0], w_two, *after)


CHIP_Y, CORES, CHIP_Z, CHIP_X = 2, 2, 4, 2
FAST_SHARDS = CHIP_Y * CORES * CHIP_Z * CHIP_X

def place(y, c, z, x):
    return (y * CORES + c) * (CHIP_Z * CHIP_X) + z * CHIP_X + x

def moves(fn):
    pairs = []
    for y in range(CHIP_Y):
        for c in range(CORES):
            for z in range(CHIP_Z):
                for x in range(CHIP_X):
                    pairs.append((place(y, c, z, x), place(*fn(y, c, z, x))))
    return pairs

CORE_SWAP = moves(lambda y, c, z, x: (y, 1 - c, z, x))
PLANE = (
    moves(lambda y, c, z, x: (y, c, z, 1 - x) if c == 0 else (1 - y, c, z, x)),
    moves(lambda y, c, z, x: (1 - y, c, z, x) if c == 0 else (y, c, z, 1 - x)),
)
X_SWAP = moves(lambda y, c, z, x: (y, c, z, 1 - x))
Y_SWAP = moves(lambda y, c, z, x: (1 - y, c, z, x))
Z_SHIFT = [moves(lambda y, c, z, x, k=k: (y, c, (z + k) % CHIP_Z, x)) for k in range(CHIP_Z)]

def send(v, pairs):
    return lax.ppermute(v, AXES, pairs)

def my_place():
    dp = lax.axis_index("dp"); fs = lax.axis_index("fsdp")
    return dp // CORES, dp % CORES, fs // CHIP_X, fs % CHIP_X

def half_of(v, which):
    h = v.shape[-1] // 2
    return lax.dynamic_slice_in_dim(v, which * h, h, axis=v.ndim - 1)

def no_sooner(arrays):
    zero = jnp.zeros((), B16)
    for v in arrays:
        zero = zero + jnp.minimum(jnp.abs(v[(0,) * v.ndim]), 0).astype(B16)
    return zero


class Gathering:
    def __init__(self, mats):
        self.mats = mats
        _, c, _, _ = my_place()

        def pick(which):
            return jnp.concatenate(
                [half_of(m, which)[i] for m in mats for i in range(m.shape[0])], axis=-1
            )

        self.piece = jnp.stack([pick(c), send(pick(1 - c), CORE_SWAP)])

    def along(self, behind=()):
        piece = self.piece + no_sooner(behind) if behind else self.piece
        self.moved = [send(piece, Z_SHIFT[k]) for k in range(1, CHIP_Z)]
        return self.moved

    def plane(self, behind=()):
        base = jnp.stack([self.piece] + self.moved)
        if behind:
            base = base + no_sooner(behind)
        self.own = [base, send(base, PLANE[0]), send(base, PLANE[1])]
        return self.own

    def far(self, behind=()):
        first = self.own[1] + no_sooner(behind) if behind else self.own[1]
        self.own.append(send(first, PLANE[1]))
        self.other = [send(v, CORE_SWAP) for v in self.own]

    def finish(self, after=()):
        return assemble(self.own, self.other, self.mats, after)


def assemble_kernel(counts, widths, pos_ref, *refs):
    src = refs[:8]; outs = refs[-1 - len(counts):-1]; sem = refs[-1]
    y, c, z, x = (pos_ref[i] for i in range(4))
    copies = []
    for side in range(2):
        core = c if side == 0 else 1 - c
        for a in range(4):
            for e in range(4):
                f1, f2 = a & 1, a >> 1
                fx = jnp.where(core == 0, f1, f2)
                fy = jnp.where(core == 0, f2, f1)
                yy = (y + fy) % 2
                xx = (x + fx) % 2
                zz = (z + CHIP_Z - e) % CHIP_Z
                for dc in range(2):
                    cc = core if dc == 0 else 1 - core
                    d = place(yy, cc, zz, xx)
                    col = 0
                    for out, count, w in zip(outs, counts, widths):
                        for k in range(count):
                            cp = pltpu.make_async_copy(
                                src[side * 4 + a].at[e, dc, :, pl.ds(col, w)],
                                out.at[d, k, :, pl.ds(pl.multiple_of(core * w, 128), w)],
                                sem,
                            )
                            cp.start(); copies.append(cp)
                            col += w
    for cp in copies:
        cp.wait()

def assemble(own, other, mats, after=()):
    rows = mats[0].shape[1]
    counts = [m.shape[0] for m in mats]; widths = [m.shape[2] // 2 for m in mats]
    pos = jnp.stack([p.astype(jnp.int32) for p in my_place()])
    return pl.pallas_call(
        functools.partial(assemble_kernel, counts, widths),
        out_shape=[jax.ShapeDtypeStruct((FAST_SHARDS, n, rows, 2 * w), B16) for n, w in zip(counts, widths)],
        in_specs=[pl.BlockSpec(memory_space=pltpu.SMEM)] + [ANY] * (8 + len(after)),
        out_specs=[pl.BlockSpec(memory_space=pltpu.VMEM)] * len(counts),
        scratch_shapes=[pltpu.SemaphoreType.DMA],
        compiler_params=params(),
        cost_estimate=cost(7),
        name="assemble",
    )(pos, *own, *other, *after)


def sum_plane(v, behind=()):
    v = v + send(v, CORE_SWAP)
    v = v + send(v, X_SWAP)
    if behind:
        v = v + no_sooner(behind).astype(v.dtype)
    return v + send(v, Y_SWAP)


class Reduction:
    def __init__(self, theirs, mine):
        self.theirs = theirs
        self.own = mine
        self.y, self.c, self.z, self.x = my_place()
        self.split = (CHIP_Y, CORES, CHIP_Z, CHIP_X, mine.shape[0] // FAST_SHARDS)

    def swap(self):
        self.got = send(self.theirs, CORE_SWAP)
        return [self.got]

    def part(self, f1, f2):
        c = self.c
        fx = jnp.where(c == 0, f1, f2)
        fy = jnp.where(c == 0, f2, f1)

        def cut(v):
            v = v.reshape(self.split + (v.shape[-1],))
            at = ((self.y + fy) % CHIP_Y, 0, 0, (self.x + fx) % CHIP_X, 0, 0)
            size = (1, CORES, CHIP_Z, 1) + v.shape[4:]
            return lax.dynamic_slice(v, at, size)[0, :, :, 0].transpose(1, 0, 2, 3).astype(F32)

        own, got = lax.optimization_barrier((self.own, self.got))
        return cut(own) + cut(got)

    def far(self):
        self.r3 = send(self.part(1, 1).astype(B16), PLANE[1])
        return [self.r3]

    def side(self):
        self.r2 = send(self.part(0, 1).astype(B16), PLANE[1])
        return [self.r2]

    def near(self):
        self.r1 = send((self.part(1, 0) + self.r3.astype(F32)).astype(B16), PLANE[0])
        return [self.r1]

    def along(self):
        base = self.part(0, 0) + self.r2.astype(F32) + self.r1.astype(F32)

        def at_z(k):
            return lax.dynamic_slice_in_dim(base, (self.z + k) % CHIP_Z, 1, axis=0)[0]

        self.mine = at_z(0)
        self.rz = [send(at_z(k).astype(B16), Z_SHIFT[k]) for k in range(1, CHIP_Z)]
        return self.rz

    def finish(self, behind=()):
        total = self.mine + no_sooner(behind).astype(F32) if behind else self.mine
        for r in self.rz:
            total = total + r.astype(F32)
        c = self.c
        keep = lax.dynamic_slice_in_dim(total, c, 1, axis=0)[0]
        give = lax.dynamic_slice_in_dim(total, 1 - c, 1, axis=0)[0]
        other = send(give, CORE_SWAP)
        first = jnp.where(c == 0, keep, other)
        second = jnp.where(c == 0, other, keep)
        return first, second


def unpack_kernel(first, src_ref, *refs):
    out_ref, ready_ref, sem = refs[-3:]
    shards, ratio, _, width = out_ref.shape
    copies = []
    for d in range(shards):
        for k in range(ratio):
            copy = pltpu.make_async_copy(
                src_ref.at[d, :, pl.ds(first + k * width, width)], out_ref.at[d, k], sem
            )
            copy.start()
            copies.append(copy)
    ready_ref[...] = jnp.zeros_like(ready_ref)
    for copy in copies:
        copy.wait()


def unpack_two(packed, first, ratio, width, after=()):
    shards, rows, _ = packed.shape
    return pl.pallas_call(
        functools.partial(unpack_kernel, first),
        out_shape=(
            jax.ShapeDtypeStruct((shards, ratio, rows, width), B16),
            jax.ShapeDtypeStruct((8, 128), F32),
        ),
        in_specs=[ANY] * (1 + len(after)),
        out_specs=(pl.BlockSpec(memory_space=pltpu.VMEM), pl.BlockSpec(memory_space=pltpu.VMEM)),
        scratch_shapes=[pltpu.SemaphoreType.DMA],
        compiler_params=params(),
        cost_estimate=cost(5),
        name="unpack",
    )(packed, *after)


def small_offsets(own, entries, device):
    per_row = TILE // (4 * own)
    return own * device, 4 * own * lax.rem(device, per_row), entries * device, device // per_row


def by_row(vectors, hidden, tables):
    row = lax.broadcasted_iota(jnp.int32, vectors.shape, 0)
    return jnp.where(row < B_ONE, vectors, jnp.where(row < TABLE, hidden, tables))


def own_kernel(*refs):
    out_ref, tmp_ref = refs[-2:]
    hidden_ref, table_ref = refs[-4:-2]
    tmp_ref[...] = jnp.zeros_like(tmp_ref)
    for layer in range(LAYERS):
        for i, ref in enumerate(refs[:B_ONE]):
            tmp_ref[layer, i : i + 1, : ref.shape[1]] = ref[layer : layer + 1, :].astype(F32)
        for i in range(B_ONE, TABLE):
            tmp_ref[layer, i : i + 1, : hidden_ref.shape[1]] = hidden_ref[
                layer : layer + 1, :
            ].astype(F32)
        heads, entries = table_ref.shape[1:]
        tmp_ref[layer, TABLE : TABLE + heads, :entries] = table_ref[layer].astype(F32)
    out_ref[...] = tmp_ref[...].astype(B16)


def own_small(vectors, hidden, table):
    whole = pl.BlockSpec(memory_space=pltpu.VMEM)
    return pl.pallas_call(
        own_kernel,
        out_shape=jax.ShapeDtypeStruct((LAYERS, SMALL_ROWS, STRIP), B16),
        in_specs=[whole] * (len(vectors) + 2),
        out_specs=whole,
        scratch_shapes=[pltpu.VMEM((LAYERS, SMALL_ROWS, STRIP), F32)],
        compiler_params=params(),
        cost_estimate=cost(1),
        name="small_own",
    )(*vectors, hidden, table)


def place_kernel(own, entries, device_ref, *refs):
    out_ref = refs[-1]
    row = lax.broadcasted_iota(jnp.int32, (SMALL_ROWS, TILE), 0)
    for layer in range(out_ref.shape[0]):
        total = jnp.zeros((SMALL_ROWS, TILE), F32)
        for k, piece_ref in enumerate(refs[:-1]):
            vec_at, b1_at, tab_at, line = small_offsets(own, entries, device_ref[k])
            piece = piece_ref[layer].astype(F32)
            rest = jnp.zeros((SMALL_ROWS, TILE - piece.shape[1]), F32)
            wide = jnp.concatenate([piece, rest], axis=1)
            hidden = jnp.where(row - B_ONE == line, pltpu.roll(wide, b1_at, 1), 0.0)
            total += by_row(pltpu.roll(wide, vec_at, 1), hidden, pltpu.roll(wide, tab_at, 1))
        out_ref[layer] = total.astype(B16)


def put_small(pieces, devices, own, entries):
    whole = pl.BlockSpec(memory_space=pltpu.VMEM)
    return pl.pallas_call(
        functools.partial(place_kernel, own, entries),
        out_shape=jax.ShapeDtypeStruct(pieces[0].shape[:2] + (TILE,), B16),
        in_specs=[SMEM] + [whole] * len(pieces),
        out_specs=whole,
        compiler_params=params(),
        cost_estimate=cost(1),
        name="small_place",
    )(devices, *pieces)


def collect_kernel(own, entries, device_ref, total_ref, *refs):
    outs = refs[-device_ref.shape[0] :]
    for k, out_ref in enumerate(outs):
        vec_at, b1_at, tab_at, line = small_offsets(own, entries, device_ref[k])

        def turn(v, at):
            return pltpu.roll(v, lax.rem(TILE - at, TILE), 1)

        for layer in range(total_ref.shape[0]):
            total = total_ref[layer]
            hidden = jnp.broadcast_to(total_ref[layer, pl.ds(B_ONE + line, 1), :], total.shape)
            wide = by_row(turn(total, vec_at), turn(hidden, b1_at), turn(total, tab_at))
            out_ref[layer] = wide[:, : out_ref.shape[2]]


def collect(total, devices, own, entries, after=()):
    whole = pl.BlockSpec(memory_space=pltpu.VMEM)
    count = devices.shape[0]
    piece = jax.ShapeDtypeStruct(total.shape[:2] + (STRIP,), F32)
    return pl.pallas_call(
        functools.partial(collect_kernel, own, entries),
        out_shape=[piece] * count,
        in_specs=[SMEM, whole] + [ANY] * len(after),
        out_specs=[whole] * count,
        compiler_params=params(),
        cost_estimate=cost(2),
        name="small_collect",
    )(devices, total, *after)


def pack_kernel(*refs):
    out_ref = refs[-1]
    out_ref[...] = jnp.zeros_like(out_ref)
    for layer in range(LAYERS):
        first, second, table = refs[3 * layer : 3 * layer + 3]
        out_ref[layer, 0:B_PROJ] = first[0:B_PROJ]
        out_ref[layer, B_PROJ:TABLE] = second[0 : TABLE - B_PROJ]
        for head in range(table.shape[0]):
            out_ref[layer, TABLE + head : TABLE + head + 1] = table[head]


def pack_small(parts, after=()):
    whole = pl.BlockSpec(memory_space=pltpu.VMEM)
    return pl.pallas_call(
        pack_kernel,
        out_shape=jax.ShapeDtypeStruct((LAYERS, SMALL_ROWS, TILE), F32),
        in_specs=[whole] * len(parts) + [ANY] * len(after),
        out_specs=whole,
        compiler_params=params(),
        cost_estimate=cost(2),
        name="small_pack",
    )(*parts, *after)


def per_device(
    shards, fast,
    tokens, masked_rows, cotangent, norm1_gain, norm1_bias, qkv_weight, q_bias, v_bias,
    proj_weight, proj_bias, gamma_attn, norm2_gain, norm2_bias, fc1_weight, fc1_bias,
    fc2_weight, fc2_bias, gamma_mlp, rel_table,
):
    vectors = (norm1_gain, norm1_bias, q_bias, v_bias, proj_bias, gamma_attn, norm2_gain,
               norm2_bias, fc2_bias, gamma_mlp)
    width = tokens.shape[1]
    images = masked_rows.shape[0]
    heads, entries = rel_table.shape[1:]
    own = qkv_weight.shape[1]
    ratio = fc2_weight.shape[1] // own
    hidden = fc1_weight.shape[2]
    me = lax.axis_index("dp") * lax.axis_size("fsdp") + lax.axis_index("fsdp")

    def pad_rows(v):
        v = v.astype(F32).reshape(images, IMG_ROWS, width)
        v = jnp.pad(v, ((0, 0), (0, PAD_ROWS - IMG_ROWS), (0, 0)))
        return v.reshape(images * PAD_ROWS, width)

    def cut_rows(v):
        return v.reshape(images, PAD_ROWS, width)[:, :IMG_ROWS].reshape(images * IMG_ROWS, width)

    used = TABLE + heads
    piece = own_small(vectors, fc1_bias, rel_table)
    hops = range(CHIP_Z) if fast else range(1)
    ring = CHIP_Z * CHIP_X

    def along_z(k):
        return (me // ring) * ring + (me + k * CHIP_X) % ring if fast else me

    backs = jnp.stack([along_z(-k) for k in hops]).astype(jnp.int32)
    ahead = jnp.stack([along_z(k) for k in hops]).astype(jnp.int32)
    pieces = [piece] + [send(piece, Z_SHIFT[k]) for k in hops[1:]]
    small = put_small(pieces, backs, own, entries)
    small = (sum_plane(small) if fast else lax.psum(small, AXES)).astype(F32)

    def two_blocks(layer):
        return fc2_weight[layer].reshape(ratio, own, width)

    def fetch_packed(layer, behind=()):
        two = two_blocks(layer)
        block = jnp.concatenate(
            [qkv_weight[layer], proj_weight[layer], fc1_weight[layer]]
            + [two[i] for i in range(ratio)],
            axis=1,
        )
        if behind:
            block = block + no_sooner(behind)
        return lax.all_gather(block, AXES, axis=0, tiled=True)

    if not fast:
        packed_weights = [fetch_packed(layer) for layer in range(LAYERS)]
        bias = [build_bias(small, layer, heads) for layer in range(LAYERS)]
    else:
        first = Gathering([qkv_weight[0][None], proj_weight[0][None]])
        second = Gathering([fc1_weight[0][None], two_blocks(0)])
        moved = first.along()
        first.plane()
        first.far()
        moved = second.along(moved)
        bias = [build_bias(small, 0, heads, [moved[0], moved[2]])]
        packed_weights = [None, fetch_packed(1)]
    weights = []
    x = pad_rows(tokens)
    saved = []
    for layer in range(LAYERS):
        full = packed_weights[layer]
        if full is None:
            w_qkv, w_proj = first.finish([bias[0]])
            w_qkv = (w_qkv.reshape(width, 3 * width), 0)
            w_proj = (w_proj.reshape(width, width), 0)
        else:
            w_qkv, w_proj, w_one = (full, 0), (full, 3), (full, 4)
        qkv, h = qkv_forward(x, small, layer, w_qkv)
        qkv = qkv.reshape(images, PAD_ROWS, 3 * width)
        att, lse = attention_forward(qkv, bias[layer])
        att = att.reshape(images * PAD_ROWS, width)
        if full is None:
            second.plane([w_qkv[0]])
            second.far([att])
            bias.append(build_bias(small, 1, heads, [lse]))
            later = packed_weights[1].reshape(shards, own, -1)
            later, ready = unpack_two(later, 4 * width + hidden, ratio, width, [lse])
            w_one, w_two = second.finish([ready])
            w_one = (w_one.reshape(width, hidden), 0)
        elif fast:
            w_two = later
        else:
            w_two = full[:, 4 * width + hidden :].reshape(shards, own, ratio, width)
            w_two = w_two.transpose(0, 2, 1, 3)
        w_two = w_two.reshape(hidden, width)
        weights.append((w_qkv, w_proj, w_one, w_two))
        out, branch, mid, mlp_out, h2, act, slope = mlp_forward(
            x, att, small, layer, w_proj, w_one, w_two
        )
        saved.append((x, h, qkv, lse, att, branch, mid, mlp_out, h2, act, slope))
        x = out
    encoded = cut_rows(x.astype(B16))

    positions = jnp.arange(IMG_ROWS, dtype=jnp.int32)
    mask = jnp.any(masked_rows[:, :, None] == positions[None, None, :], axis=1)
    mask = jnp.pad(mask, ((0, 0), (0, PAD_ROWS - IMG_ROWS))).reshape(-1, 1)
    grad = jnp.where(mask, pad_rows(cotangent), 0.0)

    def scatter(theirs, mine):
        both = jnp.stack([mine, theirs])
        own_part = lax.psum_scatter(both, AXES, scatter_dimension=1, tiled=True).astype(F32)
        return own_part[0], own_part[1]

    core = (lax.axis_index("dp") % CORES if fast else jnp.int32(0)).astype(jnp.int32).reshape(1)
    reduced = [None] * LAYERS
    small_grads = [None] * LAYERS
    tables = [None] * LAYERS

    def backward(layer, grad, hooks):
        x, h, qkv, lse, att, branch, mid, mlp_out, h2, act, slope = saved[layer]
        w_qkv, w_proj, w_one, w_two = weights[layer]
        theirs, mine, d_mid, d_att, mlp_sums = mlp_backward(
            core, grad, mid, mlp_out, branch, att, small, layer, h2, act, slope, w_proj, w_one,
            w_two, hooks[0](),
        )
        main = (theirs, mine)
        d_qkv, d_bias = attention_backward(
            qkv, bias[layer], lse, d_att.reshape(images, PAD_ROWS, width), hooks[1](main)
        )
        tables[layer] = d_bias
        theirs, mine, grad, qkv_sums = qkv_backward(
            core, d_qkv.reshape(images * PAD_ROWS, 3 * width), h, x, d_mid, small, layer, w_qkv,
            hooks[2](),
        )
        small_grads[layer] = (qkv_sums, mlp_sums)
        return grad, main, (theirs, mine)

    if not fast:
        for layer in reversed(range(LAYERS)):
            none = (lambda: (), lambda main: (), lambda: ())
            grad, main, rest = backward(layer, grad, none)
            reduced[layer] = (scatter(*main), scatter(*rest))
        tables = [reduce_bias(t) for t in tables]
    else:
        a1, b1, a0, b0 = (None,) * 4

        def one_attention(main):
            nonlocal a1
            a1 = Reduction(*main)
            return ()

        def one_qkv():
            return a1.swap()

        grad, _, rest = backward(1, grad, (lambda: (), one_attention, one_qkv))
        b1 = Reduction(*rest)

        def zero_mlp():
            return a1.far()

        def zero_attention(main):
            nonlocal a0
            a0 = Reduction(*main)
            a0.swap()
            return a1.side() + b1.swap()

        def zero_qkv():
            return a1.near() + b1.far() + a0.far()

        grad, _, rest = backward(0, grad, (zero_mlp, zero_attention, zero_qkv))
        b0 = Reduction(*rest)
        moved = a1.along()
        a0.side()
        a0.near()
        b1.side()
        b0.swap()
        b0.far()
        b0.side()
        tables[1] = reduce_bias(tables[1], [small_grads[0][0]] + moved)
        tables[0] = reduce_bias(tables[0], [tables[1], a0.r1] + b1.near())
        a0.along()
        b1.along()

    parts = []
    for (qkv_sums, mlp_sums), table in zip(small_grads, tables):
        parts += [qkv_sums, mlp_sums, table]
    totals = pack_small(parts, [b0.r3, b0.r2, a0.rz[0]] if fast else ())
    totals = sum_plane(totals, a0.rz[1:2]) if fast else lax.psum(totals, AXES)
    late = ()
    if fast:
        late = b0.near() + b1.rz
    pieces = collect(totals, ahead, own, entries, late)
    if fast:
        b0.along()
        reduced[1] = (a1.finish([pieces[0]]), b1.finish([pieces[0]]))
        reduced[0] = (a0.finish([pieces[0]]), b0.finish())
    g_small = pieces[0]
    for k in hops[1:]:
        g_small = g_small + send(pieces[k], Z_SHIFT[k])
    g = [g_small[:, i, :own] for i in range(B_ONE)]
    g_b1 = g_small[:, B_ONE, : ratio * own]
    g_table = g_small[:, TABLE:used, :entries]

    def both(pick):
        return jnp.stack([pick(*r) for r in reduced])

    def thirds(low, high):
        half = width // 2
        cols = [v[:, i * half : (i + 1) * half] for i in range(3) for v in (low, high)]
        return jnp.concatenate(cols, axis=1)

    def join(low, high, first, last):
        return jnp.concatenate([low[:, first:last], high[:, first:last]], axis=1)

    half = hidden // 2
    g_qkv = both(lambda a, b: thirds(*b))
    g_one = both(lambda a, b: join(*a, 0, half))
    g_two = both(lambda a, b: join(*a, half, hidden).reshape(ratio * own, width))
    g_proj = both(lambda a, b: join(*a, hidden, hidden + width // 2))
    return (encoded, cut_rows(grad), g[N1_GAIN], g[N1_SHIFT], g_qkv, g[Q_BIAS], g[V_BIAS], g_proj,
            g[B_PROJ], g[G_ATTN], g[N2_GAIN], g[N2_SHIFT], g_one, g_b1, g_two, g[B_TWO], g[G_MLP],
            g_table)


def solution(mesh):
    shards = math.prod(mesh.shape[a] for a in AXES)
    fast = mesh.shape["dp"] == CHIP_Y * CORES and mesh.shape["fsdp"] == CHIP_Z * CHIP_X
    row = P(AXES, None)
    vec = P(None, AXES)
    mat = P(None, AXES, None)
    tab = P(None, None, AXES)
    return jax.shard_map(
        functools.partial(per_device, shards, fast),
        mesh=mesh,
        in_specs=(row, row, row, vec, vec, mat, vec, vec, mat, vec, vec, vec, vec, mat, vec, mat,
                  vec, vec, tab),
        out_specs=(row, row, vec, vec, mat, vec, vec, mat, vec, vec, vec, vec, mat, vec, mat,
                   vec, vec, tab),
        check_vma=False,
    )
```
